32 devices in a mesh: blk: 16 (over z, x, core), fsdp: 2 (over y).
Axes of the slice: x: 2, y: 2, z: 4, core: 2. Of those that a mesh axis runs over, the one named last changes fastest.
Arguments:
- features: bfloat16 [2, 2, 4096, 256], P(None, 'fsdp', 'blk'), may hold values from -6 to 6
- neighbours: int32 [2, 2, 4096, 32], P(None, 'fsdp', 'blk'), may hold values from 0 to 4095, as said below
- slot_mask: int32 [2, 2, 4096, 32], P(None, 'fsdp', 'blk'), may hold values from 0 to 1, as said below
- projections: bfloat16 [2, 196608], P(None, ('blk', 'fsdp')), may hold values from -0.5 to 0.5
- vectors: bfloat16 [2, 1024], P(None, ('blk', 'fsdp')), may hold values from -2 to 2
- out_cotangent: bfloat16 [2, 2, 4096, 256], P(None, 'fsdp', 'blk'), may hold values from -6 to 6
Outputs:
- layer_output: bfloat16 [2, 2, 4096, 256], P(None, 'fsdp', 'blk')
- input_gradient: float32 [2, 2, 4096, 256], P(None, 'fsdp', 'blk')
- projection_gradient: float32 [2, 196608], P(None, ('blk', 'fsdp'))
- vector_gradient: float32 [2, 1024], P(None, ('blk', 'fsdp'))
The draws below stay inside these ranges and needn't reach their ends.
Inputs may be any that keep to these rules, and one draw needn't show every extreme that they name: `neighbours`: slot 0 of every node names the node itself. Every slot names a node of the node's own graph. Within a micro-batch and group, the rows below 64 of every device's block of 256 rows form one graph over the whole group; every other graph holds at most 96 nodes that are consecutive among the remaining rows of the group taken in order, so it lies on one device or on two neighbouring ones. `slot_mask`: slot 0 is always 1.
All inputs are finite; a program needn't handle non-finite values.
Results may differ from the reference program's by a relative error of at most 0.018.
Values may be sent and summed in bfloat16 or wider, within the bound.
A program may use at most 256 MiB of HBM per device.

```python
import jax
import jax.numpy as jnp
from jax import lax

D = 256
HEADS = 4
HEAD_DIM = 64
SLOTS = 32
LAYERS = 2
MICRO = 2
NT = 256
NODES_G = 4096
N_FSDP = 2


def one_group(key):
    key_sizes, key_pick, key_degree = jax.random.split(key, 3)
    quarter = NT // 4
    small_rows = NT - quarter
    size_low = min(8, small_rows // 2 + 1)
    size_high = min(96, small_rows)
    device_count = NODES_G // NT
    small_total = device_count * small_rows
    big_total = device_count * quarter
    node = jnp.arange(NODES_G, dtype=jnp.int32)
    device = node // NT
    offset = node % NT
    is_big = offset < quarter
    small_index = device * small_rows + jnp.maximum(offset - quarter, 0)
    graph_sizes = jax.random.randint(key_sizes, (small_total,), size_low, size_high + 1)
    starts = jnp.cumsum(graph_sizes) - graph_sizes
    graph_index = jnp.searchsorted(starts, small_index, side='right') - 1
    graph_start = starts[graph_index]
    graph_size = jnp.minimum(graph_start + graph_sizes[graph_index], small_total) - graph_start
    pick_limit = jnp.where(is_big, big_total, graph_size)
    base_index = jnp.where(is_big, 0, graph_start)
    member = base_index[:, None] + jax.random.randint(key_pick, (NODES_G, SLOTS), 0, pick_limit[:, None])
    big_node = member // quarter * NT + member % quarter
    small_node = member // small_rows * NT + quarter + member % small_rows
    chosen = jnp.where(is_big[:, None], big_node, small_node)
    chosen = chosen.at[:, 0].set(node)
    degree = jnp.where(is_big, SLOTS, jax.random.randint(key_degree, (NODES_G,), 4, SLOTS + 1))
    usable = (jnp.arange(SLOTS)[None, :] < degree[:, None]).astype(jnp.int32)
    return (chosen.astype(jnp.int32), usable)


def graph_draw(key):
    group_keys = jax.random.split(key, MICRO * N_FSDP)
    chosen, usable = jax.vmap(one_group)(group_keys)
    return (chosen.reshape(MICRO, N_FSDP, NODES_G, SLOTS), usable.reshape(MICRO, N_FSDP, NODES_G, SLOTS))


def draw_neighbours(key, part):
    chosen, usable = graph_draw(key)
    return chosen


def draw_slot_mask(key, part):
    chosen, usable = graph_draw(key)
    return usable


def draw_projections(key, part):
    key = jax.random.fold_in(key, 3)
    raw_values = jnp.clip(jax.random.normal(key, (LAYERS, 3, D * D), jnp.float32), -4.0, 4.0)
    scales = jnp.array([2.0, 1.0, 0.6], jnp.float32) * D ** (-0.5)
    return (raw_values * scales[None, :, None]).reshape(LAYERS, 3 * D * D).astype(jnp.bfloat16)


def draw_vectors(key, part):
    key = jax.random.fold_in(key, 5)
    key_attn, key_bias, key_gain, key_shift = jax.random.split(key, 4)
    attn_part = 0.12 * jnp.clip(jax.random.normal(key_attn, (LAYERS, D), jnp.float32), -4.0, 4.0)
    bias_part = 0.5 * jnp.clip(jax.random.normal(key_bias, (LAYERS, D), jnp.float32), -4.0, 4.0)
    gain_part = jax.random.uniform(key_gain, (LAYERS, D), jnp.float32, 0.5, 1.5)
    shift_part = 0.5 * jnp.clip(jax.random.normal(key_shift, (LAYERS, D), jnp.float32), -4.0, 4.0)
    return jnp.stack([attn_part, bias_part, gain_part, shift_part], axis=1).reshape(LAYERS, 4 * D).astype(jnp.bfloat16)


def block_levels(key, shape, cuts, least, high):
    factor_of = 1.0
    for dim, blocks in cuts:
        steps = jax.random.uniform(jax.random.fold_in(jax.random.fold_in(key, 6), dim), (blocks,), jnp.float32, least / len(cuts), high / len(cuts))
        factor_of = factor_of * jnp.repeat(jnp.exp(steps), shape[dim] // blocks).reshape((-1,) + (1,) * (len(shape) - 1 - dim))
    return factor_of


def bell_draw(stream_key, shape, width, reach, cuts=(), held_as=jnp.bfloat16):
    drawn = jax.random.normal(stream_key, shape, jnp.float32) * width
    if len(cuts) > 0:
        drawn = block_levels(stream_key, shape, cuts, -0.22, 0.18) * drawn
    return jnp.clip(drawn, min=-reach, max=reach).astype(held_as)


def setup_inputs(seed: int = 0) -> dict:
    keys = jax.random.split(jax.random.key(seed), 7)
    features = bell_draw(keys[0], (MICRO, N_FSDP, NODES_G, D), 1.0, 6.0, ((1, 2), (2, 16)))
    neighbours = draw_neighbours(jax.random.fold_in(keys[6], 71), 0)
    slot_mask = draw_slot_mask(jax.random.fold_in(keys[6], 71), 0)
    projections = draw_projections(jax.random.fold_in(keys[6], 71), 0)
    vectors = draw_vectors(jax.random.fold_in(keys[6], 71), 0)
    out_cotangent = bell_draw(keys[5], (MICRO, N_FSDP, NODES_G, D), 1.0, 6.0, ((1, 2), (2, 16)))
    return {"features": features, "neighbours": neighbours, "slot_mask": slot_mask, "projections": projections, "vectors": vectors, "out_cotangent": out_cotangent}


@jax.custom_vjp
def low(v):
    return lax.optimization_barrier(v.astype(jnp.bfloat16)).astype(jnp.float32)

@jax.custom_vjp
def low_back(v):
    return v

def low_keep(v):
    return (low(v), None)

def low_pass(kept, grad):
    return (grad,)

def back_keep(v):
    return (v, None)

def back_low(kept, grad):
    return (low(grad),)
low.defvjp(low_keep, low_pass)
low_back.defvjp(back_keep, back_low)
highest = lax.Precision.HIGHEST
epsilon = 1e-05

def smooth_leaky(values):
    return 0.2 * values + 0.8 * jax.nn.silu(values)

def attention(sources, targets, neighbour_rows, mask_rows, attn_vector):

    def one_block(operands):
        target_block, neighbour_block, mask_block = operands
        gathered = jnp.take(sources, neighbour_block, axis=0)
        summed = gathered + target_block[:, None, :]
        lifted = smooth_leaky(summed)
        logits = lax.optimization_barrier(jnp.sum((lifted * attn_vector).reshape(NT, SLOTS, HEADS, HEAD_DIM), axis=-1))
        usable = mask_block[:, :, None] > 0
        logits = jnp.where(usable, logits, -1e+30)
        largest = lax.optimization_barrier(jnp.max(logits, axis=1, keepdims=True))
        raised = jnp.exp(logits - largest) * usable.astype(jnp.float32)
        shares = low(raised / lax.optimization_barrier(jnp.sum(raised, axis=1, keepdims=True)))
        message = jnp.einsum('nsh,nshe->nhe', shares, gathered.reshape(NT, SLOTS, HEADS, HEAD_DIM), precision=highest)
        return low_back(message.reshape(NT, D))
    pieces = lax.map(jax.checkpoint(one_block), (targets.reshape(-1, NT, D), neighbour_rows.reshape(-1, NT, SLOTS), mask_rows.reshape(-1, NT, SLOTS)))
    return pieces.reshape(NODES_G, D)

def layer(hidden, weight_set, vector_set, neighbour_rows, mask_rows):
    projected = jnp.einsum('nd,kde->kne', hidden, weight_set, precision=highest)
    sources = low(low_back(projected[0]))
    targets = low_back(projected[1])
    residue = low_back(projected[2])
    message = attention(sources, targets, neighbour_rows, mask_rows, vector_set[0])
    summed = message + vector_set[1] + residue
    centred = summed - lax.optimization_barrier(jnp.mean(summed, axis=-1, keepdims=True))
    spread = lax.optimization_barrier(jnp.mean(jnp.square(centred), axis=-1, keepdims=True))
    normed = centred * lax.rsqrt(spread + epsilon)
    return jax.nn.elu(normed * vector_set[2] + vector_set[3])

def reference(features, neighbours, slot_mask, projections, vectors, out_cotangent):

    def forward(feature_values, projection_values, vector_values):
        weight_sets = projection_values.reshape(LAYERS, 3, D, D)
        vector_sets = vector_values.reshape(LAYERS, 4, D)
        micro_rows = []
        for micro_index in range(MICRO):
            group_rows = []
            for group_index in range(N_FSDP):
                hidden = feature_values[micro_index, group_index]
                for layer_index in range(LAYERS):
                    activated = layer(hidden, weight_sets[layer_index], vector_sets[layer_index], neighbours[micro_index, group_index], slot_mask[micro_index, group_index])
                    hidden = low(activated) if layer_index + 1 < LAYERS else activated
                group_rows.append(hidden)
            micro_rows.append(jnp.stack(group_rows))
        return jnp.stack(micro_rows)
    result, pullback = jax.vjp(forward, features.astype(jnp.float32), projections.astype(jnp.float32), vectors.astype(jnp.float32))
    grad_features, grad_projections, grad_vectors = pullback(out_cotangent.astype(jnp.float32))
    return (result.astype(jnp.bfloat16), grad_features, grad_projections, grad_vectors)
```

```python
import functools
import types

import jax
import jax.numpy as jnp
from jax import lax
from jax.experimental import pallas as pl
from jax.experimental.pallas import tpu as pltpu
from jax.sharding import PartitionSpec as P

HEADS = 4
MICRO = 2
LAYERS = 2
SLOTS = 32
WIDTH = 256
HEAD_WIDTH = WIDTH // HEADS
NODES = 256
BIG = 64
SMALL = NODES - BIG
RIM = 96
EXT = SMALL + 2 * RIM
BLOCKS = NODES // BIG
PAIRS = BIG * SLOTS
STEPS = 8
LANES = PAIRS // STEPS
UNIT = BIG
EPSILON = 1e-05
F32 = jnp.float32
BF16 = jnp.bfloat16
MESH = pl.DeviceIdType.MESH


def nn(left, right):
    return lax.dot_general(
        left, right, (((1,), (0,)), ((), ())), preferred_element_type=F32
    )


def nt(left, right, precision=None):
    return lax.dot_general(
        left, right, (((1,), (1,)), ((), ())), preferred_element_type=F32, precision=precision
    )


def tn(left, right):
    return lax.dot_general(
        left, right, (((0,), (0,)), ((), ())), preferred_element_type=F32
    )


def upper_lanes():
    return lax.broadcasted_iota(jnp.int32, (WIDTH, 128), 1) >= 64


def both_halves(tile):
    return tile + pltpu.roll(tile, 64, 1)


def scratch_plan(depth, shared_weights):
    big_total = 4 * depth * UNIT
    tables = 4 + (LAYERS if shared_weights else 0)
    copies = MICRO if depth <= 4 else 1
    vm = pltpu.VMEM
    plan = dict(
        hot_big=vm((copies, big_total, PAIRS), BF16),
        hot_small=vm((copies, 3, 256, PAIRS), BF16),
        place=vm((MICRO, BLOCKS, STEPS, LANES), jnp.int32),
        used=vm((MICRO, BLOCKS, STEPS, LANES), F32),
        rows_of=vm((4, BLOCKS, WIDTH, PAIRS), BF16),
        shares=vm((4, BLOCKS, STEPS, 8, LANES), F32),
        table=vm((tables, big_total, WIDTH), BF16),
        ext=vm((4, EXT, WIDTH), BF16),
        turned_big=vm((WIDTH, big_total), BF16),
        turned_small=vm((WIDTH, 256), BF16),
        hidden=vm((4, NODES, WIDTH), BF16),
        hidden_t=vm((4, WIDTH, NODES), BF16),
        weights_t=vm((LAYERS, 2 * WIDTH, WIDTH), BF16),
        vecs=vm((LAYERS, 4, WIDTH, 128), F32),
        targets=vm((4, WIDTH, NODES), F32),
        residue=vm((MICRO, WIDTH, NODES), F32),
        doubled=vm((WIDTH, 128), F32),
        scores=vm((STEPS, 8, LANES), F32),
        low_shares=vm((HEADS, STEPS, LANES), F32),
        logit_grads=vm((HEADS, STEPS, LANES), F32),
        message=vm((BLOCKS, WIDTH, 128), F32),
        normed=vm((4, WIDTH, NODES), F32),
        inverse=vm((4, 8, NODES), F32),
        act=vm((WIDTH, NODES), BF16),
        grad_act=vm((MICRO, WIDTH, NODES), F32),
        grad_out=vm((BLOCKS, WIDTH, 128), F32),
        grad_out_t=vm((4, WIDTH, NODES), BF16),
        grad_targets_t=vm((4, WIDTH, NODES), BF16),
        grad_sources_t=vm((4, WIDTH, NODES), BF16),
        grad_targets=vm((BLOCKS, WIDTH, 128), F32),
        terms=vm((WIDTH, PAIRS), BF16),
        grad_ext=vm((EXT, WIDTH), F32),
        grad_small=vm((MICRO, SMALL, WIDTH), F32),
        grad_vecs=vm((LAYERS, 4, WIDTH, 128), F32),
        part=vm((tables, big_total, WIDTH), BF16),
        land_core=vm((tables, big_total // 2, WIDTH), BF16),
        land_x=vm((tables, big_total // 4, WIDTH), BF16),
        land_z=vm((tables, depth - 1, UNIT, WIDTH), BF16),
        land_rim=vm((4, 2, RIM, WIDTH), BF16),
        send_rim=vm((4, 2, RIM, WIDTH), BF16),
        gather_send=pltpu.SemaphoreType.DMA((tables, depth + 4)),
        gather_recv=pltpu.SemaphoreType.DMA((tables, depth + 4)),
        reduce_send=pltpu.SemaphoreType.DMA((tables, depth + 4)),
        reduce_recv=pltpu.SemaphoreType.DMA((tables, depth + 4)),
    )
    if shared_weights:
        plan.update(
            weights=vm((LAYERS, 3 * WIDTH, WIDTH), BF16),
            grad_weights=vm((3 * WIDTH, WIDTH), F32),
            last_unit=vm((LAYERS, UNIT, WIDTH), F32),
            last_send=vm((LAYERS, UNIT, WIDTH), BF16),
            land_y=vm((LAYERS, UNIT // 2, WIDTH), BF16),
        )
    return plan


def step_kernel(depth, shared_weights, names, *refs):
    s = types.SimpleNamespace(**dict(zip(names, refs, strict=True)))
    big_total = 4 * depth * UNIT
    kept = s.hot_big.shape[0]
    me = lax.axis_index("blk")
    core = lax.rem(me, 2)
    along_x = lax.rem(lax.div(me, 2), 2)
    along_z = lax.div(me, 4)
    own_f = lax.axis_index("fsdp")
    block_count = 4 * depth
    before = lax.rem(me + block_count - 1, block_count)
    after = lax.rem(me + 1, block_count)
    z_peers = [
        lax.rem(along_z + k, depth) * 4 + along_x * 2 + core for k in range(1, depth)
    ]
    x_peer = along_z * 4 + (1 - along_x) * 2 + core
    sibling = along_z * 4 + along_x * 2 + (1 - core)

    def unit_row(z, x, c):
        return pl.multiple_of(((c * 2 + x) * depth + z) * UNIT, UNIT)

    own_row = unit_row(along_z, along_x, core)
    z_rows = [
        unit_row(lax.rem(along_z + k, depth), along_x, core) for k in range(1, depth)
    ]

    def remote(src, dst, sems, slot, **where):
        send, recv = sems
        return pltpu.make_async_remote_copy(
            src_ref=src,
            dst_ref=dst,
            send_sem=send.at[slot],
            recv_sem=recv.at[slot],
            device_id=where,
            device_id_type=MESH,
        )

    gather_sems = (s.gather_send, s.gather_recv)
    reduce_sems = (s.reduce_send, s.reduce_recv)
    x_slot, core_slot, low_slot, high_slot, y_slot = (depth - 1 + i for i in range(5))

    def gather_y(q):
        piece = s.table.at[q, pl.ds(pl.multiple_of(own_row + own_f * 32, 32), 32)]
        return remote(piece, piece, gather_sems, (q, y_slot), fsdp=1 - own_f)

    def gather_z(q):
        piece = s.table.at[q, pl.ds(own_row, UNIT)]
        return [
            remote(piece, piece, gather_sems, (q, k), blk=peer)
            for k, peer in enumerate(z_peers)
        ]

    def gather_x(q):
        piece = s.table.at[q, pl.ds(unit_row(0, along_x, core), depth * UNIT)]
        return remote(piece, piece, gather_sems, (q, x_slot), blk=x_peer)

    def gather_core(q):
        piece = s.table.at[q, pl.ds(unit_row(0, 0, core), 2 * depth * UNIT)]
        return remote(piece, piece, gather_sems, (q, core_slot), blk=sibling)

    def gather_rims(p):
        low = remote(
            s.ext.at[p, pl.ds(RIM, RIM)],
            s.ext.at[p, pl.ds(RIM + SMALL, RIM)],
            gather_sems,
            (p, low_slot),
            blk=before,
        )
        high = remote(
            s.ext.at[p, pl.ds(SMALL, RIM)],
            s.ext.at[p, pl.ds(0, RIM)],
            gather_sems,
            (p, high_slot),
            blk=after,
        )
        return [low, high]

    def start(copies):
        for copy in copies if isinstance(copies, list) else [copies]:
            copy.start()

    def finish(copies):
        for copy in copies if isinstance(copies, list) else [copies]:
            copy.wait()

    def reduce_core(q):
        return remote(
            s.part.at[q, pl.ds(unit_row(0, 0, 1 - core), 2 * depth * UNIT)],
            s.land_core.at[q],
            reduce_sems,
            (q, core_slot),
            blk=sibling,
        )

    def reduce_x(q):
        return remote(
            s.part.at[q, pl.ds(unit_row(0, 1 - along_x, core), depth * UNIT)],
            s.land_x.at[q],
            reduce_sems,
            (q, x_slot),
            blk=x_peer,
        )

    def reduce_z(q):
        return [
            remote(
                s.part.at[q, pl.ds(row, UNIT)],
                s.land_z.at[q, k],
                reduce_sems,
                (q, k),
                blk=peer,
            )
            for k, (peer, row) in enumerate(zip(z_peers, z_rows))
        ]

    def reduce_rims(p):
        low = remote(
            s.send_rim.at[p, 0], s.land_rim.at[p, 1], reduce_sems, (p, low_slot), blk=before
        )
        high = remote(
            s.send_rim.at[p, 1], s.land_rim.at[p, 0], reduce_sems, (p, high_slot), blk=after
        )
        return [low, high]

    def reduce_y(layer):
        return remote(
            s.last_send.at[layer, pl.ds(pl.multiple_of((1 - own_f) * 32, 32), 32)],
            s.land_y.at[layer],
            reduce_sems,
            (4 + layer, y_slot),
            fsdp=1 - own_f,
        )

    def add_into(q, row, landed, count):
        def body(i, carry):
            here = pl.ds(pl.multiple_of(row + i * UNIT, UNIT), UNIT)
            there = pl.ds(pl.multiple_of(i * UNIT, UNIT), UNIT)
            s.part[q, here] = (
                s.part[q, here].astype(F32) + landed[q, there].astype(F32)
            ).astype(BF16)
            return carry

        lax.fori_loop(0, count, body, 0)

    def reduce_to_x(q):
        finish(reduce_core(q))
        add_into(q, unit_row(0, 0, core), s.land_core, 2 * depth)
        start(reduce_x(q))

    def reduce_to_z(q):
        finish(reduce_x(q))
        add_into(q, unit_row(0, along_x, core), s.land_x, depth)
        start(reduce_z(q))

    def reduced_unit(q):
        finish(reduce_z(q))
        total = s.part[q, pl.ds(own_row, UNIT)].astype(F32)
        for k in range(depth - 1):
            total = total + s.land_z[q, k].astype(F32)
        return total

    def prepare(m):
        def compact(rows, block):
            part = rows[:, block * BIG : (block + 1) * BIG]
            tile = jnp.concatenate([part[:16], part[16:]], axis=1)
            return jnp.concatenate([tile[:8], tile[8:]], axis=1)

        picked = jnp.transpose(s.neighbours[m])
        usable = jnp.transpose(s.slot_mask[m])
        device = lax.shift_right_logical(picked, 8)
        offset = jnp.bitwise_and(picked, 255)
        z = lax.shift_right_logical(device, 2)
        x = jnp.bitwise_and(lax.shift_right_logical(device, 1), 1)
        c = jnp.bitwise_and(device, 1)
        big_place = ((c * 2 + x) * depth + z) * UNIT + offset
        small_place = (device - me) * SMALL + (offset - BIG)
        for block in range(BLOCKS):
            if block == 0:
                s.place[m, 0] = compact(big_place, 0)
            else:
                s.place[m, block] = compact(small_place + (RIM - (block - 1) * BIG), block)
            s.used[m, block] = compact(usable, block).astype(F32)
        s.hidden[m] = s.features[m]
        s.hidden_t[m] = jnp.transpose(s.features[m])
        s.grad_act[m] = jnp.transpose(s.out_cotangent[m].astype(F32))

    def mark(row, least):
        tile = lax.broadcasted_iota(jnp.int32, (256, LANES), 0)
        return jnp.where(tile == row - least, 1.0, 0.0).astype(BF16)

    def lanes_of(step):
        return pl.ds(pl.multiple_of(step * LANES, LANES), LANES)

    def mark_big(m):
        slot = m if kept > 1 else 0

        def tile(w, carry):
            here = pl.ds(pl.multiple_of(w * 256, 256), 256)
            for step in range(STEPS):
                lanes = pl.ds(step * LANES, LANES)
                row = s.place[m, 0, pl.ds(step, 1), :]
                s.hot_big[slot, here, lanes] = mark(row, w * 256)
            return carry

        lax.fori_loop(0, big_total // 256, tile, 0)

    def mark_small(m):
        def block_body(b, carry):
            for step in range(STEPS):
                lanes = pl.ds(step * LANES, LANES)
                row = s.place[m, b + 1, pl.ds(step, 1), :]
                s.hot_small[m if kept > 1 else 0, b, :, lanes] = mark(row, 0)
            return carry

        lax.fori_loop(0, 3, block_body, 0)

    def load_layer(layer):
        if shared_weights:
            units = {}
            for c in range(2):
                for x in range(2):
                    for z in range(depth):
                        for y in range(2):
                            chunk = ((z * 2 + x) * 2 + c) * 2 + y
                            at = (((c * 2 + x) * depth + z) * 2 + y) * 32
                            units[chunk] = s.table[4 + layer, pl.ds(at, 32)].astype(F32)
            flat = jnp.concatenate(
                [units[i][:24] for i in range(len(units))], axis=0
            ).astype(BF16)
            rows = units[0][24:]
            for i in range(1, len(units)):
                rows = rows + units[i][24:]
            s.weights[layer] = flat
        else:
            rows = s.all_vectors[layer].astype(F32)
        for k in range(2):
            s.weights_t[layer, pl.ds(k * WIDTH, WIDTH)] = jnp.transpose(
                s.weights[layer, pl.ds((k + 1) * WIDTH, WIDTH)]
            )
        which = lax.broadcasted_iota(jnp.int32, (8, 512), 0)
        lane = lax.shift_right_logical(lax.broadcasted_iota(jnp.int32, (8, 512), 1), 7)
        chosen = jnp.where(which == lane, 1.0, 0.0).astype(BF16)
        wide = tn(rows.astype(BF16), chosen)
        for k in range(4):
            s.vecs[layer, k] = wide[:, k * 128 : (k + 1) * 128]

    def project(p, layer, m):
        hidden = s.hidden[p]
        sources = (0.5 * nn(hidden, s.weights[layer, pl.ds(0, WIDTH)])).astype(BF16)
        s.table[p, pl.ds(own_row, UNIT)] = sources[:BIG]
        s.ext[p, pl.ds(RIM, SMALL)] = sources[BIG:]
        start(gather_z(p))
        start(gather_rims(p))
        s.targets[p] = 0.5 * nt(s.weights_t[layer, pl.ds(0, WIDTH)], hidden)
        bias = s.vecs[layer, 1]
        s.residue[m] = nt(s.weights_t[layer, pl.ds(WIDTH, WIDTH)], hidden) + jnp.concatenate(
            [bias, bias], axis=1
        )

    def double(wide, block):
        odd = jnp.bitwise_and(block, 1) == 1
        return jnp.where(upper_lanes() == odd, wide, pltpu.roll(wide, 64, 1))

    def tile_of(block):
        return pl.ds(pl.multiple_of(lax.div(block, 2) * 128, 128), 128)

    def head_rows(h):
        if isinstance(h, int):
            return pl.ds(h * HEAD_WIDTH, HEAD_WIDTH)
        return pl.ds(pl.multiple_of(h * HEAD_WIDTH, HEAD_WIDTH), HEAD_WIDTH)

    def by_head(ref, step, rows):
        for h in range(HEADS):
            ref[h, pl.ds(step, 1), :] = rows[h : h + 1]

    def attend(p, layer, m, block, turned, hot):
        s.doubled[...] = double(s.targets[p, :, tile_of(block)], block)

        def score(step, carry):
            got = nn(turned[...], hot[:, lanes_of(step)])
            s.rows_of[p, block, :, lanes_of(step)] = got.astype(BF16)
            for h in range(HEADS):
                rows = slice(h * HEAD_WIDTH, (h + 1) * HEAD_WIDTH)
                wanted = s.doubled[rows, :]
                attn = s.vecs[layer, 0, rows, :]
                for half in range(2):
                    z = got[rows, half * 128 : (half + 1) * 128] + wanted
                    lifted = z * (jnp.tanh(z) + 1.5)
                    s.scores[step, h : h + 1, half * 128 : (half + 1) * 128] = jnp.sum(
                        lifted * attn, axis=0, keepdims=True
                    )
            return carry

        lax.fori_loop(0, STEPS, score, 0)

        def halves_max(wide):
            tile = jnp.maximum(wide[:, :128], wide[:, 128:])
            return jnp.maximum(tile, pltpu.roll(tile, 64, 1))

        def halves_sum(wide):
            return both_halves(wide[:, :128] + wide[:, 128:])

        def twice(tile):
            return jnp.concatenate([tile, tile], axis=1)

        used = [s.used[m, block, pl.ds(i, 1), :] for i in range(STEPS)]
        logits = [
            jnp.where(used[i] > 0, 0.8 * s.scores[i], -1e30) for i in range(STEPS)
        ]
        largest = twice(halves_max(functools.reduce(jnp.maximum, logits)))
        raised = [jnp.exp(logits[i] - largest) * used[i] for i in range(STEPS)]
        scale = twice(1.0 / halves_sum(functools.reduce(jnp.add, raised)))
        for i in range(STEPS):
            share = raised[i] * scale
            s.shares[p, block, i] = share
            by_head(s.low_shares, i, share.astype(BF16).astype(F32))

        def gather_head(h, carry):
            total = jnp.zeros((HEAD_WIDTH, 128), F32)
            for i in range(STEPS):
                for half in range(2):
                    lanes = pl.ds(i * LANES + half * 128, 128)
                    share = s.low_shares[h, pl.ds(i, 1), pl.ds(half * 128, 128)]
                    total = total + share * s.rows_of[p, block, head_rows(h), lanes].astype(F32)
            s.message[block, head_rows(h), :] = both_halves(total)
            return carry

        lax.fori_loop(0, HEADS, gather_head, 0)

    def normalise(p, layer, m):
        gain, shift = s.vecs[layer, 2], s.vecs[layer, 3]
        for t in range(2):
            lanes = slice(t * 128, (t + 1) * 128)
            total = jnp.where(upper_lanes(), s.message[2 * t + 1], s.message[2 * t])
            y = 2.0 * total + s.residue[m, :, lanes]
            centred = y - jnp.sum(y, axis=0, keepdims=True) * (1.0 / WIDTH)
            spread = jnp.sum(centred * centred, axis=0, keepdims=True) * (1.0 / WIDTH)
            inverse = lax.rsqrt(spread + EPSILON)
            normed = centred * inverse
            shifted = normed * gain + shift
            s.normed[p, :, lanes] = normed
            s.inverse[p, 0:1, lanes] = inverse
            act = jnp.where(shifted > 0, shifted, jnp.exp(jnp.minimum(shifted, 0.0)) - 1.0)
            s.act[:, lanes] = act.astype(BF16)

        @pl.when(p < 2)
        def _():
            s.hidden_t[p + 2] = s.act[...]
            s.hidden[p + 2] = jnp.transpose(s.act[...])
            project(p + 2, 1, m)

        @pl.when(p >= 2)
        def _():
            s.layer_output[m] = jnp.transpose(s.act[...])

    def forward(p, carry):
        m, layer = lax.rem(p, 2), lax.div(p, 2)
        if kept == 1:
            mark_big(m)
            mark_small(m)
        finish(gather_rims(p))

        def small(b, inner):
            here = pl.ds(pl.multiple_of(b * BIG, BIG), 256)
            s.turned_small[...] = jnp.transpose(s.ext[p, here])
            attend(p, layer, m, b + 1, s.turned_small, s.hot_small.at[m if kept > 1 else 0, b])

            @pl.when(b == 0)
            def _():
                finish(gather_z(p))
                start(gather_x(p))

            @pl.when(b == 1)
            def _():
                finish(gather_x(p))
                start(gather_core(p))

            return inner

        lax.fori_loop(0, 3, small, 0)
        finish(gather_core(p))

        def turn(w, inner):
            here = pl.ds(pl.multiple_of(w * 256, 256), 256)
            s.turned_big[:, here] = jnp.transpose(s.table[p, here])
            return inner

        lax.fori_loop(0, big_total // 256, turn, 0)
        attend(p, layer, m, 0, s.turned_big, s.hot_big.at[m if kept > 1 else 0])
        normalise(p, layer, m)
        return carry

    def through_norm(p, layer, m):
        gain, shift = s.vecs[layer, 2], s.vecs[layer, 3]
        for t in range(2):
            lanes = slice(t * 128, (t + 1) * 128)
            normed = s.normed[p, :, lanes]
            shifted = normed * gain + shift
            grad = s.grad_act[m, :, lanes] * jnp.where(
                shifted > 0, 1.0, jnp.exp(jnp.minimum(shifted, 0.0))
            )
            s.grad_vecs[layer, 2] = s.grad_vecs[layer, 2] + grad * normed
            s.grad_vecs[layer, 3] = s.grad_vecs[layer, 3] + grad
            grad = grad * gain
            first = jnp.sum(grad, axis=0, keepdims=True) * (1.0 / WIDTH)
            second = jnp.sum(grad * normed, axis=0, keepdims=True) * (1.0 / WIDTH)
            grad = s.inverse[p, 0:1, lanes] * (grad - first - normed * second)
            s.grad_vecs[layer, 1] = s.grad_vecs[layer, 1] + grad
            low = grad.astype(BF16)
            s.grad_out_t[p, :, lanes] = low
            wide = low.astype(F32)
            other = pltpu.roll(wide, 64, 1)
            s.grad_out[2 * t] = jnp.where(upper_lanes(), other, wide)
            s.grad_out[2 * t + 1] = jnp.where(upper_lanes(), wide, other)

    def attend_back(p, layer, block):
        s.doubled[...] = double(s.targets[p, :, tile_of(block)], block)

        def share_grads(step, carry):
            for h in range(HEADS):
                rows = slice(h * HEAD_WIDTH, (h + 1) * HEAD_WIDTH)
                grad = s.grad_out[block, rows, :]
                for half in range(2):
                    lanes = pl.ds(pl.multiple_of(step * LANES + half * 128, 128), 128)
                    got = s.rows_of[p, block, rows, lanes].astype(F32)
                    s.scores[step, h : h + 1, half * 128 : (half + 1) * 128] = jnp.sum(
                        got * grad, axis=0, keepdims=True
                    )
            return carry

        lax.fori_loop(0, STEPS, share_grads, 0)
        shares = [s.shares[p, block, i] for i in range(STEPS)]
        total = functools.reduce(jnp.add, [shares[i] * s.scores[i] for i in range(STEPS)])
        total = both_halves(total[:, :128] + total[:, 128:])
        total = jnp.concatenate([total, total], axis=1)
        for i in range(STEPS):
            by_head(s.low_shares, i, shares[i].astype(BF16).astype(F32))
            by_head(s.logit_grads, i, 0.8 * shares[i] * (s.scores[i] - total))

        def head(h, carry):
            rows = head_rows(h)
            wanted = s.doubled[rows, :]
            attn = s.vecs[layer, 0, rows, :]
            grad = s.grad_out[block, rows, :]

            target_sum = attn_sum = jnp.zeros((HEAD_WIDTH, 128), F32)
            for step in range(STEPS):
                for half in range(2):
                    lanes = pl.ds(step * LANES + half * 128, 128)
                    part = pl.ds(half * 128, 128)
                    z = s.rows_of[p, block, rows, lanes].astype(F32) + wanted
                    t = jnp.tanh(z)
                    w = t + 1.5
                    logit_grad = s.logit_grads[h, pl.ds(step, 1), part]
                    attn_sum = attn_sum + logit_grad * (z * w)
                    slope = logit_grad * (w + z * (1.0 - t * t))
                    target_sum = target_sum + slope
                    share = s.low_shares[h, pl.ds(step, 1), part]
                    s.terms[rows, lanes] = (share * grad + attn * slope).astype(BF16)
            s.grad_targets[block, rows, :] = both_halves(target_sum) * attn
            s.grad_vecs[layer, 0, rows, :] = s.grad_vecs[layer, 0, rows, :] + 2.0 * attn_sum
            return carry

        lax.fori_loop(0, HEADS, head, 0)

    def finalise(p, layer, m):
        big = reduced_unit(p)
        finish(reduce_rims(p))
        low = s.grad_small[m, pl.ds(0, RIM)] + s.land_rim[p, 0].astype(F32)
        high = s.grad_small[m, pl.ds(RIM, RIM)] + s.land_rim[p, 1].astype(F32)
        rows = jnp.concatenate([big, low, high], axis=0)
        s.grad_sources_t[p] = jnp.transpose(rows.astype(BF16))
        s.grad_act[m] = (
            nn(s.weights[layer, pl.ds(0, WIDTH)], s.grad_sources_t[p])
            + nn(s.weights[layer, pl.ds(WIDTH, WIDTH)], s.grad_targets_t[p])
            + nn(s.weights[layer, pl.ds(2 * WIDTH, WIDTH)], s.grad_out_t[p])
        )

    def weight_grads(layer):
        for k, grads in enumerate((s.grad_sources_t, s.grad_targets_t, s.grad_out_t)):
            total = nt(
                s.hidden_t[2 * layer], grads[2 * layer]
            ) + nt(s.hidden_t[2 * layer + 1], grads[2 * layer + 1])
            if shared_weights:
                s.grad_weights[pl.ds(k * WIDTH, WIDTH)] = total
            else:
                s.weight_sums[layer, pl.ds(k * WIDTH, WIDTH)] = total
        vector_rows = jnp.zeros((8, WIDTH), F32)
        for k in range(4):
            chosen = jnp.where(
                lax.broadcasted_iota(jnp.int32, (8, 128), 0) == k, 1.0, 0.0
            ).astype(F32)
            vector_rows = vector_rows + nt(
                chosen, s.grad_vecs[layer, k], precision=lax.Precision.HIGHEST
            )
        if not shared_weights:
            s.vector_sums[layer] = vector_rows
            return
        for c in range(2):
            for x in range(2):
                for z in range(depth):
                    for y in range(2):
                        chunk = ((z * 2 + x) * 2 + c) * 2 + y
                        at = (((c * 2 + x) * depth + z) * 2 + y) * 32
                        s.part[4 + layer, pl.ds(at, 32)] = jnp.concatenate(
                            [s.grad_weights[pl.ds(chunk * 24, 24)], vector_rows], axis=0
                        ).astype(BF16)
        start(reduce_core(4 + layer))

    def weight_last(layer):
        unit = reduced_unit(4 + layer)
        s.last_unit[layer] = unit
        s.last_send[layer] = unit.astype(BF16)
        start(reduce_y(layer))

    def weight_done(layer):
        finish(reduce_y(layer))
        mine = s.last_unit[layer, pl.ds(pl.multiple_of(own_f * 32, 32), 32)]
        total = mine + s.land_y[layer].astype(F32)
        s.weight_sums[layer] = total[:24]
        s.vector_sums[layer] = total[24:]

    def backward(i, carry):
        p = lax.rem(i + 2, 4)
        m, layer = lax.rem(p, 2), lax.div(p, 2)
        if kept == 1:
            mark_big(m)
            mark_small(m)

        @pl.when(i >= 2)
        def _():
            finalise(p + 2, 1, m)

        @pl.when(i == 3)
        def _():
            weight_grads(1)

        through_norm(p, layer, m)
        attend_back(p, layer, 0)

        def scatter_big(w, inner):
            here = pl.ds(pl.multiple_of(w * 256, 256), 256)
            slot = m if kept > 1 else 0
            s.part[p, here] = nt(s.hot_big[slot, here], s.terms[...]).astype(BF16)
            return inner

        lax.fori_loop(0, big_total // 256, scatter_big, 0)
        start(reduce_core(p))
        s.grad_ext[...] = jnp.zeros_like(s.grad_ext)

        def small(b, inner):
            attend_back(p, layer, b + 1)
            here = pl.ds(pl.multiple_of(b * BIG, BIG), 256)
            s.grad_ext[here] = s.grad_ext[here] + nt(s.hot_small[m if kept > 1 else 0, b], s.terms[...])

            @pl.when(b == 0)
            def _():
                reduce_to_x(p)
                if shared_weights:

                    @pl.when(i == 3)
                    def _():
                        reduce_to_x(5)

            @pl.when(b == 1)
            def _():
                reduce_to_z(p)
                if shared_weights:

                    @pl.when(i == 3)
                    def _():
                        reduce_to_z(5)

            return inner

        lax.fori_loop(0, 3, small, 0)
        s.send_rim[p, 0] = s.grad_ext[pl.ds(0, RIM)].astype(BF16)
        s.send_rim[p, 1] = s.grad_ext[pl.ds(RIM + SMALL, RIM)].astype(BF16)
        start(reduce_rims(p))
        s.grad_small[m] = s.grad_ext[pl.ds(RIM, SMALL)]
        for t in range(2):
            lanes = slice(t * 128, (t + 1) * 128)
            s.grad_targets_t[p, :, lanes] = jnp.where(
                upper_lanes(), s.grad_targets[2 * t + 1], s.grad_targets[2 * t]
            ).astype(BF16)
        return carry

    barrier = pltpu.get_barrier_semaphore()
    partners = [dict(blk=d) for d in [*z_peers, x_peer, sibling, before, after]]
    if shared_weights:
        partners.append(dict(fsdp=1 - own_f))
    for partner in partners:
        pl.semaphore_signal(barrier, inc=1, device_id=partner, device_id_type=MESH)
    pl.semaphore_wait(barrier, len(partners))

    if shared_weights:
        for layer in range(LAYERS):
            s.table[4 + layer, pl.ds(pl.multiple_of(own_row + own_f * 32, 32), 32)] = (
                s.weight_units[layer]
            )
            start(gather_y(4 + layer))
    prepare(0)
    prepare(1)
    s.scores[...] = jnp.zeros_like(s.scores)
    s.grad_vecs[...] = jnp.zeros_like(s.grad_vecs)
    if shared_weights:
        for layer in range(LAYERS):
            finish(gather_y(4 + layer))
            start(gather_z(4 + layer))
    if kept > 1:
        mark_small(0)
    if shared_weights:
        for layer in range(LAYERS):
            finish(gather_z(4 + layer))
            start(gather_x(4 + layer))
    if kept > 1:
        mark_small(1)
    if shared_weights:
        for layer in range(LAYERS):
            finish(gather_x(4 + layer))
            start(gather_core(4 + layer))
    if kept > 1:
        mark_big(0)
        mark_big(1)
    if shared_weights:
        finish(gather_core(4))
    load_layer(0)
    project(0, 0, 0)
    project(1, 0, 1)
    if shared_weights:
        finish(gather_core(5))
    load_layer(1)
    lax.fori_loop(0, 4, forward, 0)
    lax.fori_loop(0, 4, backward, 0)
    if shared_weights:
        weight_last(1)
    finalise(0, 0, 0)
    s.input_gradient[0] = jnp.transpose(s.grad_act[0])
    finalise(1, 0, 1)
    weight_grads(0)
    s.input_gradient[1] = jnp.transpose(s.grad_act[1])
    if shared_weights:
        reduce_to_x(4)
        weight_done(1)
        reduce_to_z(4)
        weight_last(0)
        weight_done(0)


def per_device(depth, fsdp_count, features, neighbours, slot_mask, projections, vectors, out_cotangent):
    layers, weight_chunk = projections.shape
    vector_chunk = vectors.shape[1]
    place = lax.axis_index("blk") * fsdp_count + lax.axis_index("fsdp")
    shared_weights = fsdp_count == 2 and weight_chunk == 24 * WIDTH and depth == 4
    inputs = dict(
        features=features[:, 0],
        neighbours=neighbours[:, 0],
        slot_mask=slot_mask[:, 0],
        out_cotangent=out_cotangent[:, 0],
    )
    if shared_weights:
        own = lax.dynamic_update_slice(
            jnp.zeros((layers, 8 * WIDTH), BF16), vectors, (0, place * vector_chunk)
        )
        inputs["weight_units"] = jnp.concatenate(
            [projections.reshape(layers, 24, WIDTH), own.reshape(layers, 8, WIDTH)], axis=1
        )
        weight_rows = 24
    else:
        axes = ("blk", "fsdp")
        gathered = lax.all_gather(projections, axes, axis=1, tiled=True)
        inputs["weights"] = gathered.reshape(layers, 3 * WIDTH, WIDTH)
        gathered = lax.all_gather(vectors, axes, axis=1, tiled=True)
        inputs["all_vectors"] = jnp.pad(
            gathered.reshape(layers, 4, WIDTH), ((0, 0), (0, 4), (0, 0))
        )
        weight_rows = 3 * WIDTH
    outputs = dict(
        layer_output=jax.ShapeDtypeStruct((MICRO, NODES, WIDTH), BF16),
        input_gradient=jax.ShapeDtypeStruct((MICRO, NODES, WIDTH), F32),
        weight_sums=jax.ShapeDtypeStruct((layers, weight_rows, WIDTH), F32),
        vector_sums=jax.ShapeDtypeStruct((layers, 8, WIDTH), F32),
    )
    scratch = scratch_plan(depth, shared_weights)
    in_vmem = pl.BlockSpec(memory_space=pltpu.VMEM)
    layer_output, input_gradient, weight_sums, vector_sums = pl.pallas_call(
        functools.partial(
            step_kernel, depth, shared_weights, [*inputs, *outputs, *scratch]
        ),
        out_shape=list(outputs.values()),
        in_specs=[in_vmem] * len(inputs),
        out_specs=[in_vmem] * len(outputs),
        scratch_shapes=list(scratch.values()),
        compiler_params=pltpu.CompilerParams(
            collective_id=0, has_side_effects=True, vmem_limit_bytes=63 * 1024 * 1024
        ),
    )(*inputs.values())
    if shared_weights:
        weight_sums = weight_sums.reshape(layers, weight_chunk)
        vector_sums = lax.dynamic_slice(
            vector_sums.reshape(layers, 8 * WIDTH),
            (0, place * vector_chunk),
            (layers, vector_chunk),
        )
    else:
        axes = ("blk", "fsdp")
        weight_sums = lax.psum_scatter(
            weight_sums.reshape(layers, -1), axes, scatter_dimension=1, tiled=True
        )
        vector_sums = lax.psum_scatter(
            vector_sums[:, :4].reshape(layers, -1), axes, scatter_dimension=1, tiled=True
        )
    return layer_output[:, None], input_gradient[:, None], weight_sums, vector_sums


def solution(mesh):
    return jax.shard_map(
        functools.partial(per_device, mesh.shape["blk"] // 4, mesh.shape["fsdp"]),
        mesh=mesh,
        in_specs=(
            P(None, "fsdp", "blk", None),
            P(None, "fsdp", "blk", None),
            P(None, "fsdp", "blk", None),
            P(None, ("blk", "fsdp")),
            P(None, ("blk", "fsdp")),
            P(None, "fsdp", "blk", None),
        ),
        out_specs=(
            P(None, "fsdp", "blk", None),
            P(None, "fsdp", "blk", None),
            P(None, ("blk", "fsdp")),
            P(None, ("blk", "fsdp")),
        ),
        check_vma=False,
    )
```

```python
import functools
import types

import jax
import jax.numpy as jnp
from jax import lax
from jax.experimental import pallas as pl
from jax.experimental.pallas import tpu as pltpu
from jax.sharding import PartitionSpec as P

HEADS = 4
MICRO = 2
LAYERS = 2
SLOTS = 32
WIDTH = 256
HEAD_WIDTH = WIDTH // HEADS
NODES = 256
BIG = 64
SMALL = NODES - BIG
RIM = 96
EXT = SMALL + 2 * RIM
BLOCKS = NODES // BIG
SMALLS = BLOCKS - 1
PAIRS = BIG * SLOTS
STEPS = 8
LANES = PAIRS // STEPS
UNIT = BIG
CHUNK = 24
PIECE = UNIT // 2
EPSILON = 1e-05
F32 = jnp.float32
BF16 = jnp.bfloat16
MESH = pl.DeviceIdType.MESH


def nn(left, right):
    return lax.dot_general(
        left, right, (((1,), (0,)), ((), ())), preferred_element_type=F32
    )


def nt(left, right, precision=None):
    return lax.dot_general(
        left, right, (((1,), (1,)), ((), ())), preferred_element_type=F32, precision=precision
    )


def tn(left, right):
    return lax.dot_general(
        left, right, (((0,), (0,)), ((), ())), preferred_element_type=F32
    )


def upper_lanes():
    return lax.broadcasted_iota(jnp.int32, (WIDTH, 128), 1) >= 64


def join_halves(even, odd):
    upper = upper_lanes()
    return jnp.where(upper, odd, even) + pltpu.roll(jnp.where(upper, even, odd), 64, 1)


def scratch_plan(depth, shared_weights):
    big_total = 4 * depth * UNIT
    tables = 4 + (LAYERS if shared_weights else 0)
    copies = MICRO if depth <= 4 else 1
    peers = 2 * depth - 1
    vm = pltpu.VMEM
    plan = dict(
        hot_big=vm((copies, big_total, PAIRS), BF16),
        hot_small=vm((copies, SMALLS, 256, PAIRS), BF16),
        place=vm((MICRO, BLOCKS, STEPS, LANES), jnp.int32),
        used=vm((MICRO, BLOCKS, STEPS, LANES), F32),
        rows_0=vm((4, WIDTH, PAIRS), BF16),
        rows_1=vm((4, WIDTH, PAIRS), BF16),
        rows_2=vm((4, WIDTH, PAIRS), BF16),
        rows_3=vm((4, WIDTH, PAIRS), BF16),
        shares=vm((4, BLOCKS, STEPS, 8, LANES), F32),
        table=vm((tables, big_total, WIDTH), BF16),
        ext=vm((4, EXT, WIDTH), BF16),
        turned_big=vm((WIDTH, big_total), BF16),
        turned_small=vm((SMALLS, WIDTH, 256), BF16),
        hidden_t=vm((4, WIDTH, NODES), BF16),
        weights_t=vm((LAYERS, 2 * WIDTH, WIDTH), BF16),
        vecs=vm((LAYERS, 4, WIDTH, 128), F32),
        attn_low=vm((LAYERS, WIDTH, 128), BF16),
        targets=vm((4, WIDTH, NODES), F32),
        residue=vm((MICRO, WIDTH, NODES), F32),
        doubled=vm((BLOCKS, WIDTH, 128), F32),
        doubled_low=vm((BLOCKS, WIDTH, 128), BF16),
        scores=vm((BLOCKS, STEPS, 8, LANES), F32),
        message=vm((MICRO, BLOCKS, WIDTH, 128), F32),
        normed=vm((4, WIDTH, NODES), F32),
        inverse=vm((4, 8, NODES), F32),
        act=vm((WIDTH, NODES), BF16),
        grad_act=vm((MICRO, WIDTH, NODES), F32),
        grad_out=vm((MICRO, BLOCKS, WIDTH, 128), BF16),
        grad_out_t=vm((4, WIDTH, NODES), BF16),
        grad_targets_t=vm((4, WIDTH, NODES), BF16),
        grad_sources_t=vm((4, WIDTH, NODES), BF16),
        terms_0=vm((WIDTH, PAIRS), BF16),
        terms_1=vm((WIDTH, PAIRS), BF16),
        grad_ext=vm((EXT, WIDTH), F32),
        grad_small=vm((MICRO, SMALL, WIDTH), F32),
        grad_vecs=vm((LAYERS, 4, WIDTH, 128), F32),
        land_core=vm((tables, big_total // 2, WIDTH), BF16),
        land=vm((4, peers, UNIT, WIDTH), BF16),
        land_rim=vm((4, 2, RIM, WIDTH), BF16),
        send_rim=vm((4, 2, RIM, WIDTH), BF16),
        gather_send=pltpu.SemaphoreType.DMA((tables, 18)),
        gather_recv=pltpu.SemaphoreType.DMA((tables, 18)),
        reduce_send=pltpu.SemaphoreType.DMA((tables, 18)),
        reduce_recv=pltpu.SemaphoreType.DMA((tables, 18)),
    )
    if shared_weights:
        plan.update(
            weights=vm((LAYERS, 3 * WIDTH, WIDTH), BF16),
            grad_weights=vm((3 * WIDTH, WIDTH), F32),
            land_piece=vm((LAYERS, 2 * peers + 1, PIECE, WIDTH), BF16),
        )
    return plan


def step_kernel(depth, shared_weights, names, *refs):
    s = types.SimpleNamespace(**dict(zip(names, refs, strict=True)))
    big_total = 4 * depth * UNIT
    kept = s.hot_big.shape[0]
    me = lax.axis_index("blk")
    core = lax.rem(me, 2)
    along_x = lax.rem(lax.div(me, 2), 2)
    along_z = lax.div(me, 4)
    own_f = lax.axis_index("fsdp")
    block_count = 4 * depth
    before = lax.rem(me + block_count - 1, block_count)
    after = lax.rem(me + 1, block_count)
    sibling = along_z * 4 + along_x * 2 + (1 - core)

    def unit_row(z, x, c):
        return pl.multiple_of(((c * 2 + x) * depth + z) * UNIT, UNIT)

    own_row = unit_row(along_z, along_x, core)
    rows_of = (s.rows_0, s.rows_1, s.rows_2, s.rows_3)
    terms = (s.terms_0, s.terms_1)
    far = []
    for dz in sorted(range(depth), reverse=True):
        for dx in (1, 0):
            if dz or dx:
                z, x = lax.rem(along_z + dz, depth), lax.rem(along_x + dx, 2)
                far.append((z * 4 + x * 2 + core, unit_row(z, x, core)))

    def remote(src, dst, sems, slot, **where):
        send, recv = sems
        return pltpu.make_async_remote_copy(
            src_ref=src,
            dst_ref=dst,
            send_sem=send.at[slot],
            recv_sem=recv.at[slot],
            device_id=where,
            device_id_type=MESH,
        )

    gather_sems = (s.gather_send, s.gather_recv)
    reduce_sems = (s.reduce_send, s.reduce_recv)
    core_slot, low_slot, high_slot = 15, 16, 17

    def half_rows(c):
        return pl.ds(unit_row(0, 0, c), 2 * depth * UNIT)

    def piece_rows(row, f):
        return pl.ds(pl.multiple_of(row + f * PIECE, PIECE), PIECE)

    def gather_far(p):
        unit = s.table.at[p, pl.ds(own_row, UNIT)]
        return [
            remote(unit, unit, gather_sems, (p, k), blk=peer)
            for k, (peer, _) in enumerate(far)
        ]

    def all_far():
        found = []
        for peer, row in far:
            for f in (1 - own_f, own_f):
                found.append((peer, f, piece_rows(row, f)))
        found.append((me, 1 - own_f, piece_rows(own_row, 1 - own_f)))
        return found

    def gather_pieces(layer):
        piece = s.table.at[4 + layer, piece_rows(own_row, own_f)]
        return [
            remote(piece, piece, gather_sems, (4 + layer, k), blk=peer, fsdp=f)
            for k, (peer, f, _) in enumerate(all_far())
        ]

    def gather_core(q):
        half = s.table.at[q, half_rows(core)]
        return [remote(half, half, gather_sems, (q, core_slot), blk=sibling)]

    def gather_rims(p):
        low = remote(
            s.ext.at[p, pl.ds(RIM, RIM)],
            s.ext.at[p, pl.ds(RIM + SMALL, RIM)],
            gather_sems,
            (p, low_slot),
            blk=before,
        )
        high = remote(
            s.ext.at[p, pl.ds(SMALL, RIM)],
            s.ext.at[p, pl.ds(0, RIM)],
            gather_sems,
            (p, high_slot),
            blk=after,
        )
        return [low, high]

    def reduce_core(q):
        return [
            remote(
                s.table.at[q, half_rows(1 - core)],
                s.land_core.at[q],
                reduce_sems,
                (q, core_slot),
                blk=sibling,
            )
        ]

    def reduce_far(p):
        return [
            remote(
                s.table.at[p, pl.ds(row, UNIT)],
                s.land.at[p, k],
                reduce_sems,
                (p, k),
                blk=peer,
            )
            for k, (peer, row) in enumerate(far)
        ]

    def reduce_pieces(layer):
        return [
            remote(
                s.table.at[4 + layer, rows],
                s.land_piece.at[layer, k],
                reduce_sems,
                (4 + layer, k),
                blk=peer,
                fsdp=f,
            )
            for k, (peer, f, rows) in enumerate(all_far())
        ]

    def reduce_rims(p):
        low = remote(
            s.send_rim.at[p, 0], s.land_rim.at[p, 1], reduce_sems, (p, low_slot), blk=before
        )
        high = remote(
            s.send_rim.at[p, 1], s.land_rim.at[p, 0], reduce_sems, (p, high_slot), blk=after
        )
        return [low, high]

    def start(copies):
        for copy in copies:
            copy.start()

    def finish(copies):
        for copy in copies:
            copy.wait()

    def add_core(q):
        finish(reduce_core(q))
        first = unit_row(0, 0, core)

        def body(i, carry):
            here = pl.ds(pl.multiple_of(first + i * UNIT, UNIT), UNIT)
            there = pl.ds(pl.multiple_of(i * UNIT, UNIT), UNIT)
            s.table[q, here] = (
                s.table[q, here].astype(F32) + s.land_core[q, there].astype(F32)
            ).astype(BF16)
            return carry

        lax.fori_loop(0, 2 * depth, body, 0)

    def reduce_on(p):
        add_core(p)
        start(reduce_far(p))

    def reduced_unit(p):
        finish(reduce_far(p))
        total = s.table[p, pl.ds(own_row, UNIT)].astype(F32)
        for k in range(len(far)):
            total = total + s.land[p, k].astype(F32)
        return total

    def prepare(m):
        def compact(rows, block):
            part = rows[:, block * BIG : (block + 1) * BIG]
            tile = jnp.concatenate([part[:16], part[16:]], axis=1)
            return jnp.concatenate([tile[:8], tile[8:]], axis=1)

        picked = s.neighbours[m]
        usable = s.slot_mask[m]
        device = lax.shift_right_logical(picked, 8)
        offset = jnp.bitwise_and(picked, 255)
        z = lax.shift_right_logical(device, 2)
        x = jnp.bitwise_and(lax.shift_right_logical(device, 1), 1)
        c = jnp.bitwise_and(device, 1)
        big_place = ((c * 2 + x) * depth + z) * UNIT + offset
        small_place = (device - me) * SMALL + (offset - BIG)
        for block in range(BLOCKS):
            if block == 0:
                s.place[m, 0] = compact(big_place, 0)
            else:
                s.place[m, block] = compact(small_place + (RIM - (block - 1) * BIG), block)
            s.used[m, block] = compact(usable, block).astype(F32)
        s.hidden_t[m] = jnp.transpose(s.features[m])
        s.grad_act[m] = jnp.transpose(s.out_cotangent[m].astype(F32))

    def mark(row, least):
        tile = lax.broadcasted_iota(jnp.int32, (256, LANES), 0)
        return jnp.where(tile == row - least, 1.0, 0.0).astype(BF16)

    def lanes_of(step):
        return pl.ds(pl.multiple_of(step * LANES, LANES), LANES)

    def mark_big(m):
        slot = m if kept > 1 else 0

        def tile(w, carry):
            here = pl.ds(pl.multiple_of(w * 256, 256), 256)
            for step in range(STEPS):
                lanes = pl.ds(step * LANES, LANES)
                row = s.place[m, 0, pl.ds(step, 1), :]
                s.hot_big[slot, here, lanes] = mark(row, w * 256)
            return carry

        lax.fori_loop(0, big_total // 256, tile, 0)

    def mark_small(m):
        slot = m if kept > 1 else 0

        def block_body(b, carry):
            for step in range(STEPS):
                lanes = pl.ds(step * LANES, LANES)
                row = s.place[m, b + 1, pl.ds(step, 1), :]
                s.hot_small[slot, b, :, lanes] = mark(row, 0)
            return carry

        lax.fori_loop(0, SMALLS, block_body, 0)

    place = me * 2 + own_f
    vector_row, vector_lane = lax.div(place, 8), lax.rem(place, 8) * 32

    def vector_place():
        lane = lax.broadcasted_iota(jnp.int32, (32, WIDTH), 1)
        element = lax.broadcasted_iota(jnp.int32, (32, WIDTH), 0)
        return jnp.where(lane == element + vector_lane, 1.0, 0.0)

    def own_row_of_eight():
        return lax.broadcasted_iota(jnp.int32, (8, WIDTH), 0) == vector_row

    def own_piece(layer):
        flat = s.projections[...].astype(F32)[layer : layer + 1]
        rows = [flat[:, i * WIDTH : (i + 1) * WIDTH] for i in range(CHUNK)]
        own = s.vectors[...][layer : layer + 1].astype(F32)
        own = nn(jnp.broadcast_to(own, (8, 32)).astype(BF16), vector_place().astype(BF16))
        rows.append(jnp.where(own_row_of_eight(), own, 0.0))
        s.table[4 + layer, piece_rows(own_row, own_f)] = jnp.concatenate(
            rows, axis=0
        ).astype(BF16)

    def chunks():
        for c in range(2):
            for x in range(2):
                for z in range(depth):
                    for y in range(2):
                        yield (
                            ((z * 2 + x) * 2 + c) * 2 + y,
                            (((c * 2 + x) * depth + z) * 2 + y) * PIECE,
                        )

    def load_layer(layer):
        if shared_weights:
            pieces = {
                chunk: s.table[4 + layer, pl.ds(at, PIECE)].astype(F32)
                for chunk, at in chunks()
            }
            s.weights[layer] = jnp.concatenate(
                [pieces[i][:CHUNK] for i in range(len(pieces))], axis=0
            ).astype(BF16)
            rows = pieces[0][CHUNK:]
            for i in range(1, len(pieces)):
                rows = rows + pieces[i][CHUNK:]
        else:
            rows = s.all_vectors[layer].astype(F32)
        for k in range(2):
            s.weights_t[layer, pl.ds(k * WIDTH, WIDTH)] = jnp.transpose(
                s.weights[layer, pl.ds((k + 1) * WIDTH, WIDTH)]
            )
        which = lax.broadcasted_iota(jnp.int32, (8, 512), 0)
        lane = lax.shift_right_logical(lax.broadcasted_iota(jnp.int32, (8, 512), 1), 7)
        chosen = jnp.where(which == lane, 1.0, 0.0).astype(BF16)
        wide = tn(rows.astype(BF16), chosen)
        for k in range(4):
            s.vecs[layer, k] = wide[:, k * 128 : (k + 1) * 128]
        s.attn_low[layer] = wide[:, :128].astype(BF16)

    def project(p, layer, m, hidden):
        sources = (0.5 * nn(hidden, s.weights[layer, pl.ds(0, WIDTH)])).astype(BF16)
        s.table[p, pl.ds(own_row, UNIT)] = sources[:BIG]
        s.ext[p, pl.ds(RIM, SMALL)] = sources[BIG:]
        start(gather_rims(p))
        start(gather_far(p))
        s.targets[p] = 0.5 * nt(s.weights_t[layer, pl.ds(0, WIDTH)], hidden)
        bias = s.vecs[layer, 1]
        s.residue[m] = nt(s.weights_t[layer, pl.ds(WIDTH, WIDTH)], hidden) + jnp.concatenate(
            [bias, bias], axis=1
        )

    def spread(p, block, low):
        wide = s.targets[p, :, pl.ds((block // 2) * 128, 128)]
        odd = block % 2 == 1
        tile = jnp.where(upper_lanes() == odd, wide, pltpu.roll(wide, 64, 1))
        if low:
            s.doubled_low[block] = tile.astype(BF16)
        else:
            s.doubled[block] = tile

    def score(p, layer, block, step):
        for h in range(HEADS):
            rows = slice(h * HEAD_WIDTH, (h + 1) * HEAD_WIDTH)
            wanted = s.doubled[block, rows, :]
            attn = s.vecs[layer, 0, rows, :]
            for half in range(2):
                lanes = pl.ds(pl.multiple_of(step * LANES + half * 128, 128), 128)
                z = rows_of[block][p, rows, lanes].astype(F32) + wanted
                lifted = z * (jnp.tanh(z) + 1.5)
                s.scores[block, step, h : h + 1, half * 128 : (half + 1) * 128] = jnp.sum(
                    lifted * attn, axis=0, keepdims=True
                )

    def halves_max(wide):
        tile = jnp.maximum(wide[:, :128], wide[:, 128:])
        tile = jnp.maximum(tile, pltpu.roll(tile, 64, 1))
        return jnp.concatenate([tile, tile], axis=1)

    def halves_sum(wide):
        tile = wide[:, :128] + wide[:, 128:]
        tile = tile + pltpu.roll(tile, 64, 1)
        return jnp.concatenate([tile, tile], axis=1)

    def softmax(p, m, blocks):
        for block in blocks:
            used = [s.used[m, block, pl.ds(i, 1), :] for i in range(STEPS)]
            logits = [
                jnp.where(used[i] > 0, 0.8 * s.scores[block, i], -1e30) for i in range(STEPS)
            ]
            largest = halves_max(functools.reduce(jnp.maximum, logits))
            raised = [jnp.exp(logits[i] - largest) * used[i] for i in range(STEPS)]
            scale = 1.0 / halves_sum(functools.reduce(jnp.add, raised))
            for i in range(STEPS):
                share = raised[i] * scale
                s.shares[p, block, i] = share

    def pass_message(p, m, block, step):
        for h in range(HEADS):
            rows = slice(h * HEAD_WIDTH, (h + 1) * HEAD_WIDTH)
            total = s.message[m, block, rows, :]
            for half in range(2):
                lanes = pl.ds(pl.multiple_of(step * LANES + half * 128, 128), 128)
                share = s.shares[p, block, step, h : h + 1, half * 128 : (half + 1) * 128]
                share = share.astype(BF16).astype(F32)
                total = total + share * rows_of[block][p, rows, lanes].astype(F32)
            s.message[m, block, rows, :] = total

    def small_rows(p, m, b, part):
        lanes = pl.ds(part * 2 * LANES, 2 * LANES)
        hot = s.hot_small[m if kept > 1 else 0, b, :, lanes]
        rows_of[b + 1][p, :, lanes] = nn(s.turned_small[b], hot).astype(BF16)

    def big_rows(p, m, part):
        lanes = pl.ds(part * 2 * LANES, 2 * LANES)
        hot = s.hot_big[m if kept > 1 else 0, :, lanes]
        rows_of[0][p, :, lanes] = nn(s.turned_big[...], hot).astype(BF16)

    def smalls(p, layer, m):
        finish(gather_rims(p))
        for b in range(SMALLS):
            s.turned_small[b] = jnp.transpose(s.ext[p, pl.ds(b * BIG, 256)])
            spread(p, b + 1, False)
        for part in range(STEPS // 2):
            small_rows(p, m, 0, part)
        for b in range(SMALLS):
            for step in range(STEPS):
                score(p, layer, b + 1, step)
                if b + 1 < SMALLS and step % 2:
                    small_rows(p, m, b + 1, step // 2)

    def big(p, layer, m):
        def turn(w, inner):
            here = pl.ds(pl.multiple_of(w * 256, 256), 256)
            s.turned_big[:, here] = jnp.transpose(s.table[p, here])
            return inner

        lax.fori_loop(0, big_total // 256, turn, 0)
        spread(p, 0, False)
        s.message[m] = jnp.zeros((BLOCKS, WIDTH, 128), F32)

        for part in range(STEPS // 2):
            big_rows(p, m, part)
            for block in range(1, BLOCKS):
                for step in (2 * part, 2 * part + 1):
                    pass_message(p, m, block, step)

        def body(step, carry):
            score(p, layer, 0, step)
            return carry

        lax.fori_loop(0, STEPS, body, 0)
        softmax(p, m, [0])

        def message_body(step, carry):
            pass_message(p, m, 0, step)
            return carry

        lax.fori_loop(0, STEPS, message_body, 0)

    def normalise(p, layer, m):
        gain, shift = s.vecs[layer, 2], s.vecs[layer, 3]
        for t in range(2):
            lanes = slice(t * 128, (t + 1) * 128)
            total = join_halves(s.message[m, 2 * t], s.message[m, 2 * t + 1])
            y = 2.0 * total + s.residue[m, :, lanes]
            centred = y - jnp.sum(y, axis=0, keepdims=True) * (1.0 / WIDTH)
            spread_of = jnp.sum(centred * centred, axis=0, keepdims=True) * (1.0 / WIDTH)
            inverse = lax.rsqrt(spread_of + EPSILON)
            normed = centred * inverse
            shifted = normed * gain + shift
            s.normed[p, :, lanes] = normed
            s.inverse[p, 0:1, lanes] = inverse
            act = jnp.where(shifted > 0, shifted, jnp.exp(jnp.minimum(shifted, 0.0)) - 1.0)
            s.act[:, lanes] = act.astype(BF16)

        @pl.when(layer == 0)
        def _():
            s.hidden_t[m + 2] = s.act[...]
            project(m + 2, 1, m, jnp.transpose(s.act[...]))

        @pl.when(layer == 1)
        def _():
            s.layer_output[m] = jnp.transpose(s.act[...])

    def forward(layer, carry):
        first, second = 2 * layer, 2 * layer + 1

        def small_body(m, inner):
            if kept == 1:
                mark_small(m)
            smalls(first + m, layer, m)

            @pl.when(m == 1)
            def _():
                finish(gather_far(first))
                start(gather_core(first))

            softmax(first + m, m, [1, 2, 3])
            return inner

        lax.fori_loop(0, MICRO, small_body, 0)

        def big_body(m, inner):
            if kept == 1:
                mark_big(m)
            finish(gather_core(first + m))
            big(first + m, layer, m)

            @pl.when(m == 0)
            def _():
                finish(gather_far(second))
                start(gather_core(second))

            normalise(first + m, layer, m)
            return inner

        lax.fori_loop(0, MICRO, big_body, 0)
        return carry

    def through_norm(p, layer, m):
        gain, shift = s.vecs[layer, 2], s.vecs[layer, 3]
        upper = upper_lanes()
        for t in range(2):
            lanes = slice(t * 128, (t + 1) * 128)
            normed = s.normed[p, :, lanes]
            shifted = normed * gain + shift
            grad = s.grad_act[m, :, lanes] * jnp.where(
                shifted > 0, 1.0, jnp.exp(jnp.minimum(shifted, 0.0))
            )
            s.grad_vecs[layer, 2] = s.grad_vecs[layer, 2] + grad * normed
            s.grad_vecs[layer, 3] = s.grad_vecs[layer, 3] + grad
            grad = grad * gain
            first = jnp.sum(grad, axis=0, keepdims=True) * (1.0 / WIDTH)
            second = jnp.sum(grad * normed, axis=0, keepdims=True) * (1.0 / WIDTH)
            grad = s.inverse[p, 0:1, lanes] * (grad - first - normed * second)
            s.grad_vecs[layer, 1] = s.grad_vecs[layer, 1] + grad
            s.grad_out_t[p, :, lanes] = grad.astype(BF16)
            other = pltpu.roll(grad, 64, 1)
            s.grad_out[m, 2 * t] = jnp.where(upper, other, grad).astype(BF16)
            s.grad_out[m, 2 * t + 1] = jnp.where(upper, grad, other).astype(BF16)

    def share_grads(p, m, block, step):
        for h in range(HEADS):
            rows = slice(h * HEAD_WIDTH, (h + 1) * HEAD_WIDTH)
            grad = s.grad_out[m, block, rows, :]
            for half in range(2):
                lanes = pl.ds(pl.multiple_of(step * LANES + half * 128, 128), 128)
                product = rows_of[block][p, rows, lanes] * grad
                s.scores[block, step, h : h + 1, half * 128 : (half + 1) * 128] = jnp.sum(
                    product.astype(F32), axis=0, keepdims=True
                )

    def logit_grads(p, blocks):
        for block in blocks:
            shares = [s.shares[p, block, i] for i in range(STEPS)]
            total = halves_sum(
                functools.reduce(
                    jnp.add, [shares[i] * s.scores[block, i] for i in range(STEPS)]
                )
            )
            for i in range(STEPS):
                s.scores[block, i] = 0.8 * shares[i] * (s.scores[block, i] - total)

    def make_terms(p, layer, m, block, step):
        for h in range(HEADS):
            rows = slice(h * HEAD_WIDTH, (h + 1) * HEAD_WIDTH)
            wanted = s.doubled_low[block, rows, :]
            attn = s.attn_low[layer, rows, :]
            grad = s.grad_out[m, block, rows, :]
            slopes, lifted = [], []
            for half in range(2):
                lanes = pl.ds(pl.multiple_of(step * LANES + half * 128, 128), 128)
                part = slice(half * 128, (half + 1) * 128)
                z = rows_of[block][p, rows, lanes] + wanted
                t = jnp.tanh(z)
                w = t + jnp.asarray(1.5, BF16)
                logit_grad = s.scores[block, step, h : h + 1, part].astype(BF16)
                share = s.shares[p, block, step, h : h + 1, part].astype(BF16)
                lifted.append(z * w * logit_grad)
                slope = (w + z * (jnp.asarray(1.0, BF16) - t * t)) * logit_grad
                slopes.append(slope)
                terms[block % 2][rows, lanes] = share * grad + attn * slope
            s.message[m, block, rows, :] = s.message[m, block, rows, :] + (
                slopes[0] + slopes[1]
            ).astype(F32)
            s.grad_vecs[layer, 0, rows, :] = s.grad_vecs[layer, 0, rows, :] + (
                lifted[0] + lifted[1]
            ).astype(F32)

    def over_steps(work):
        def body(step, carry):
            work(step)
            return carry

        lax.fori_loop(0, STEPS, body, 0)

    def big_back(p, layer, m, progress):
        spread(p, 0, True)
        over_steps(lambda step: share_grads(p, m, 0, step))
        logit_grads(p, [0])
        s.message[m] = jnp.zeros((BLOCKS, WIDTH, 128), F32)
        progress()
        over_steps(lambda step: make_terms(p, layer, m, 0, step))
        s.table[p] = nt(s.hot_big[m if kept > 1 else 0], terms[0][...]).astype(BF16)
        start(reduce_core(p))

    def scatter_small(m, b):
        here = pl.ds(b * BIG, 256)
        hot = s.hot_small[m if kept > 1 else 0, b]
        s.grad_ext[here] = s.grad_ext[here] + nt(hot, terms[(b + 1) % 2][...])

    def smalls_back(p, layer, m, progress):
        for b in range(SMALLS):
            spread(p, b + 1, True)
        for b in range(SMALLS):
            over_steps(lambda step: share_grads(p, m, b + 1, step))
        logit_grads(p, [1, 2, 3])
        s.grad_ext[...] = jnp.zeros_like(s.grad_ext)
        progress()
        over_steps(lambda step: make_terms(p, layer, m, 1, step))
        for b in range(1, SMALLS):
            scatter_small(m, b - 1)
            for step in range(STEPS):
                make_terms(p, layer, m, b + 1, step)
        scatter_small(m, SMALLS - 1)
        s.send_rim[p, 0] = s.grad_ext[pl.ds(0, RIM)].astype(BF16)
        s.send_rim[p, 1] = s.grad_ext[pl.ds(RIM + SMALL, RIM)].astype(BF16)
        start(reduce_rims(p))
        s.grad_small[m] = s.grad_ext[pl.ds(RIM, SMALL)]
        attn = s.vecs[layer, 0]
        for t in range(2):
            lanes = slice(t * 128, (t + 1) * 128)
            total = join_halves(s.message[m, 2 * t], s.message[m, 2 * t + 1])
            s.grad_targets_t[p, :, lanes] = (attn * total).astype(BF16)

    def finalise(p, layer, m):
        unit = reduced_unit(p)
        finish(reduce_rims(p))
        low = s.grad_small[m, pl.ds(0, RIM)] + s.land_rim[p, 0].astype(F32)
        high = s.grad_small[m, pl.ds(RIM, RIM)] + s.land_rim[p, 1].astype(F32)
        rows = jnp.concatenate([unit, low, high], axis=0)
        s.grad_sources_t[p] = jnp.transpose(rows.astype(BF16))
        s.grad_act[m] = (
            nn(s.weights[layer, pl.ds(0, WIDTH)], s.grad_sources_t[p])
            + nn(s.weights[layer, pl.ds(WIDTH, WIDTH)], s.grad_targets_t[p])
            + nn(s.weights[layer, pl.ds(2 * WIDTH, WIDTH)], s.grad_out_t[p])
        )

    def weight_grads(layer):
        for k, grads in enumerate((s.grad_sources_t, s.grad_targets_t, s.grad_out_t)):
            total = nt(s.hidden_t[2 * layer], grads[2 * layer]) + nt(
                s.hidden_t[2 * layer + 1], grads[2 * layer + 1]
            )
            if shared_weights:
                s.grad_weights[pl.ds(k * WIDTH, WIDTH)] = total
            else:
                s.weight_sums[layer, pl.ds(k * WIDTH, WIDTH)] = total
        vector_rows = jnp.zeros((8, WIDTH), F32)
        for k in range(4):
            chosen = jnp.where(
                lax.broadcasted_iota(jnp.int32, (8, 128), 0) == k, 2.0 if k == 0 else 1.0, 0.0
            ).astype(F32)
            vector_rows = vector_rows + nt(
                chosen, s.grad_vecs[layer, k], precision=lax.Precision.HIGHEST
            )
        if not shared_weights:
            s.vector_sums[layer] = vector_rows
            return
        for chunk, at in chunks():
            s.table[4 + layer, pl.ds(at, PIECE)] = jnp.concatenate(
                [s.grad_weights[pl.ds(chunk * CHUNK, CHUNK)], vector_rows], axis=0
            ).astype(BF16)
        start(reduce_core(4 + layer))

    def weights_on(layer):
        add_core(4 + layer)
        start(reduce_pieces(layer))

    def weights_done(layer):
        finish(reduce_pieces(layer))
        total = s.table[4 + layer, piece_rows(own_row, own_f)].astype(F32)
        for k in range(2 * len(far) + 1):
            total = total + s.land_piece[layer, k].astype(F32)
        s.weight_sums[layer : layer + 1, :] = jnp.concatenate(
            [total[i : i + 1] for i in range(CHUNK)], axis=1
        )
        own = jnp.where(own_row_of_eight(), total[CHUNK:], 0.0)
        own = jnp.sum(own, axis=0, keepdims=True)
        own = nt(
            jnp.broadcast_to(own, (8, WIDTH)), vector_place(), precision=lax.Precision.HIGHEST
        )
        s.vector_sums[layer : layer + 1, :] = own[:1]

    def backward(i, carry):
        layer = 1 - i
        first, second = 2 * layer, 2 * layer + 1

        def big_body(m, inner):
            if kept == 1:
                mark_big(m)

            @pl.when(i == 1)
            def _():
                finalise(2 + m, 1, m)

            @pl.when(jnp.logical_and(i == 1, m == 1))
            def _():
                weight_grads(1)

            def progress():
                @pl.when(m == 1)
                def _():
                    reduce_on(first)

            through_norm(first + m, layer, m)
            big_back(first + m, layer, m, progress)
            return inner

        lax.fori_loop(0, MICRO, big_body, 0)

        def small_body(m, inner):
            if kept == 1:
                mark_small(m)

            def progress():
                @pl.when(m == 0)
                def _():
                    reduce_on(second)

                if shared_weights:

                    @pl.when(jnp.logical_and(i == 1, m == 1))
                    def _():
                        weights_on(1)

            smalls_back(first + m, layer, m, progress)
            return inner

        lax.fori_loop(0, MICRO, small_body, 0)
        return carry

    barrier = pltpu.get_barrier_semaphore()
    partners = [dict(blk=peer) for peer, _ in far]
    if shared_weights:
        partners = [dict(blk=peer, fsdp=f) for peer, f, _ in all_far()]
    partners += [dict(blk=d) for d in (sibling, before, after)]
    for partner in partners:
        pl.semaphore_signal(barrier, inc=1, device_id=partner, device_id_type=MESH)
    if shared_weights:
        for layer in range(LAYERS):
            own_piece(layer)
    pl.semaphore_wait(barrier, len(partners))

    if shared_weights:
        start(gather_pieces(0))
    prepare(0)
    prepare(1)
    s.scores[...] = jnp.zeros_like(s.scores)
    s.grad_vecs[...] = jnp.zeros_like(s.grad_vecs)
    if kept > 1:
        mark_small(0)
        mark_small(1)
        mark_big(0)
        mark_big(1)
    if shared_weights:
        finish(gather_pieces(0))
        start(gather_core(4))
        start(gather_pieces(1))
        finish(gather_core(4))
    load_layer(0)
    project(0, 0, 0, s.features[0])
    project(1, 0, 1, s.features[1])
    if shared_weights:
        finish(gather_pieces(1))
        start(gather_core(5))
        finish(gather_core(5))
    load_layer(1)
    lax.fori_loop(0, LAYERS, forward, 0)
    lax.fori_loop(0, LAYERS, backward, 0)
    finalise(0, 0, 0)
    s.input_gradient[0] = jnp.transpose(s.grad_act[0])
    finalise(1, 0, 1)
    weight_grads(0)
    s.input_gradient[1] = jnp.transpose(s.grad_act[1])
    if shared_weights:
        weights_on(0)
        weights_done(1)
        weights_done(0)


def per_device(
    depth, fsdp_count, features, neighbours, slot_mask, projections, vectors, out_cotangent
):
    layers, weight_chunk = projections.shape
    shared_weights = fsdp_count == 2 and weight_chunk == CHUNK * WIDTH and depth == 4
    inputs = dict(
        features=features[:, 0],
        neighbours=jnp.swapaxes(neighbours[:, 0], 1, 2),
        slot_mask=jnp.swapaxes(slot_mask[:, 0], 1, 2),
        out_cotangent=out_cotangent[:, 0],
    )
    if shared_weights:
        inputs["projections"] = projections
        inputs["vectors"] = vectors
        weight_shape, vector_shape = projections.shape, vectors.shape
    else:
        axes = ("blk", "fsdp")
        gathered = lax.all_gather(projections, axes, axis=1, tiled=True)
        inputs["weights"] = gathered.reshape(layers, 3 * WIDTH, WIDTH)
        gathered = lax.all_gather(vectors, axes, axis=1, tiled=True)
        inputs["all_vectors"] = jnp.pad(
            gathered.reshape(layers, 4, WIDTH), ((0, 0), (0, 4), (0, 0))
        )
        weight_shape, vector_shape = (layers, 3 * WIDTH, WIDTH), (layers, 8, WIDTH)
    outputs = dict(
        layer_output=jax.ShapeDtypeStruct((MICRO, NODES, WIDTH), BF16),
        input_gradient=jax.ShapeDtypeStruct((MICRO, NODES, WIDTH), F32),
        weight_sums=jax.ShapeDtypeStruct(weight_shape, F32),
        vector_sums=jax.ShapeDtypeStruct(vector_shape, F32),
    )
    scratch = scratch_plan(depth, shared_weights)
    in_vmem = pl.BlockSpec(memory_space=pltpu.VMEM)
    layer_output, input_gradient, weight_sums, vector_sums = pl.pallas_call(
        functools.partial(
            step_kernel, depth, shared_weights, [*inputs, *outputs, *scratch]
        ),
        out_shape=list(outputs.values()),
        in_specs=[in_vmem] * len(inputs),
        out_specs=[in_vmem] * len(outputs),
        scratch_shapes=list(scratch.values()),
        compiler_params=pltpu.CompilerParams(
            collective_id=0, has_side_effects=True, vmem_limit_bytes=63 * 1024 * 1024
        ),
    )(*inputs.values())
    if not shared_weights:
        axes = ("blk", "fsdp")
        weight_sums = lax.psum_scatter(
            weight_sums.reshape(layers, -1), axes, scatter_dimension=1, tiled=True
        )
        vector_sums = lax.psum_scatter(
            vector_sums[:, :4].reshape(layers, -1), axes, scatter_dimension=1, tiled=True
        )
    return layer_output[:, None], input_gradient[:, None], weight_sums, vector_sums


def solution(mesh):
    return jax.shard_map(
        functools.partial(per_device, mesh.shape["blk"] // 4, mesh.shape["fsdp"]),
        mesh=mesh,
        in_specs=(
            P(None, "fsdp", "blk", None),
            P(None, "fsdp", "blk", None),
            P(None, "fsdp", "blk", None),
            P(None, ("blk", "fsdp")),
            P(None, ("blk", "fsdp")),
            P(None, "fsdp", "blk", None),
        ),
        out_specs=(
            P(None, "fsdp", "blk", None),
            P(None, "fsdp", "blk", None),
            P(None, ("blk", "fsdp")),
            P(None, ("blk", "fsdp")),
        ),
        check_vma=False,
    )
```

```python
import functools
import types

import jax
import jax.numpy as jnp
from jax import lax
from jax.experimental import pallas as pl
from jax.experimental.pallas import tpu as pltpu
from jax.sharding import PartitionSpec as P

HEADS = 4
MICRO = 2
LAYERS = 2
SLOTS = 32
WIDTH = 256
HEAD_WIDTH = WIDTH // HEADS
NODES = 256
BIG = 64
SMALL = NODES - BIG
RIM = 96
EXT = SMALL + 2 * RIM
BLOCKS = NODES // BIG
SMALLS = BLOCKS - 1
PAIRS = BIG * SLOTS
STEPS = 8
LANES = PAIRS // STEPS
UNIT = BIG
CHUNK = 24
PIECE = UNIT // 2
EPSILON = 1e-05
F32 = jnp.float32
BF16 = jnp.bfloat16
MESH = pl.DeviceIdType.MESH


def nn(left, right):
    return lax.dot_general(
        left, right, (((1,), (0,)), ((), ())), preferred_element_type=F32
    )


def nt(left, right, precision=None):
    return lax.dot_general(
        left, right, (((1,), (1,)), ((), ())), preferred_element_type=F32, precision=precision
    )


def tn(left, right):
    return lax.dot_general(
        left, right, (((0,), (0,)), ((), ())), preferred_element_type=F32
    )


def upper_lanes():
    return lax.broadcasted_iota(jnp.int32, (WIDTH, 128), 1) >= 64


def join_halves(even, odd):
    upper = upper_lanes()
    return jnp.where(upper, odd, even) + pltpu.roll(jnp.where(upper, even, odd), 64, 1)


def scratch_plan(depth, shared_weights):
    big_total = 4 * depth * UNIT
    tables = 4 + (LAYERS if shared_weights else 0)
    copies = MICRO if depth <= 4 else 1
    peers = 2 * depth - 1
    vm = pltpu.VMEM
    plan = dict(
        hot_big=vm((copies, big_total, PAIRS), BF16),
        hot_small=vm((copies, SMALLS, 256, PAIRS), BF16),
        place=vm((MICRO, BLOCKS, STEPS, LANES), jnp.int32),
        used=vm((MICRO, BLOCKS, STEPS, LANES), F32),
        rows_0=vm((4, WIDTH, PAIRS), BF16),
        rows_1=vm((4, WIDTH, PAIRS), BF16),
        rows_2=vm((4, WIDTH, PAIRS), BF16),
        rows_3=vm((4, WIDTH, PAIRS), BF16),
        shares=vm((4, BLOCKS, STEPS, 8, LANES), F32),
        table=vm((tables, big_total, WIDTH), BF16),
        ext=vm((4, EXT, WIDTH), BF16),
        turned_big=vm((WIDTH, big_total), BF16),
        turned_small=vm((SMALLS, WIDTH, 256), BF16),
        hidden_t=vm((4, WIDTH, NODES), BF16),
        weights_t=vm((LAYERS, 3 * WIDTH, WIDTH), BF16),
        vecs=vm((LAYERS, 4, WIDTH, 128), F32),
        targets=vm((4, WIDTH, NODES), F32),
        residue=vm((MICRO, WIDTH, NODES), F32),
        doubled=vm((BLOCKS, WIDTH, 128), F32),
        scores=vm((BLOCKS, STEPS, 8, LANES), F32),
        share_grad=vm((MICRO, BLOCKS, STEPS, 8, LANES), F32),
        message=vm((MICRO, BLOCKS, WIDTH, 128), F32),
        normed=vm((4, WIDTH, NODES), F32),
        inverse=vm((4, 8, NODES), F32),
        act=vm((WIDTH, NODES), BF16),
        grad_act=vm((MICRO, WIDTH, NODES), F32),
        grad_out=vm((MICRO, BLOCKS, WIDTH, 128), F32),
        grad_out_t=vm((4, WIDTH, NODES), BF16),
        grad_targets_t=vm((4, WIDTH, NODES), BF16),
        grad_sources_t=vm((4, WIDTH, NODES), BF16),
        terms_0=vm((WIDTH, 2 * LANES), BF16),
        terms_1=vm((WIDTH, 2 * LANES), BF16),
        part_sum=vm((big_total, WIDTH), F32),
        grad_ext=vm((EXT, WIDTH), F32),
        head_weights=vm((WIDTH, WIDTH), F32),
        grad_small=vm((MICRO, SMALL, WIDTH), F32),
        grad_vecs=vm((LAYERS, 4, WIDTH, 128), F32),
        land_core=vm((tables, big_total // 2, WIDTH), BF16),
        land=vm((4, peers, UNIT, WIDTH), BF16),
        land_rim=vm((4, 2, RIM, WIDTH), BF16),
        send_rim=vm((4, 2, RIM, WIDTH), BF16),
        gather_send=pltpu.SemaphoreType.DMA((tables, 18)),
        gather_recv=pltpu.SemaphoreType.DMA((tables, 18)),
        reduce_send=pltpu.SemaphoreType.DMA((tables, 18)),
        reduce_recv=pltpu.SemaphoreType.DMA((tables, 18)),
    )
    if shared_weights:
        plan.update(
            weights=vm((LAYERS, 3 * WIDTH, WIDTH), BF16),
            grad_weights=vm((3 * WIDTH, WIDTH), F32),
            land_piece=vm((LAYERS, 2 * peers + 1, PIECE, WIDTH), BF16),
        )
    return plan


def step_kernel(depth, shared_weights, names, *refs):
    s = types.SimpleNamespace(**dict(zip(names, refs, strict=True)))
    big_total = 4 * depth * UNIT
    kept = s.hot_big.shape[0]
    me = lax.axis_index("blk")
    core = lax.rem(me, 2)
    along_x = lax.rem(lax.div(me, 2), 2)
    along_z = lax.div(me, 4)
    own_f = lax.axis_index("fsdp")
    block_count = 4 * depth
    before = lax.rem(me + block_count - 1, block_count)
    after = lax.rem(me + 1, block_count)
    sibling = along_z * 4 + along_x * 2 + (1 - core)

    def unit_row(z, x, c):
        return pl.multiple_of(((c * 2 + x) * depth + z) * UNIT, UNIT)

    own_row = unit_row(along_z, along_x, core)
    rows_of = (s.rows_0, s.rows_1, s.rows_2, s.rows_3)
    terms = (s.terms_0, s.terms_1)
    far = []
    for dz in sorted(range(depth), reverse=True):
        for dx in (1, 0):
            if dz or dx:
                z, x = lax.rem(along_z + dz, depth), lax.rem(along_x + dx, 2)
                far.append((z * 4 + x * 2 + core, unit_row(z, x, core)))

    def remote(src, dst, sems, slot, **where):
        send, recv = sems
        return pltpu.make_async_remote_copy(
            src_ref=src,
            dst_ref=dst,
            send_sem=send.at[slot],
            recv_sem=recv.at[slot],
            device_id=where,
            device_id_type=MESH,
        )

    gather_sems = (s.gather_send, s.gather_recv)
    reduce_sems = (s.reduce_send, s.reduce_recv)
    core_slot, low_slot, high_slot = 15, 16, 17

    def half_rows(c):
        return pl.ds(unit_row(0, 0, c), 2 * depth * UNIT)

    def piece_row(z, x, c, f):
        return pl.multiple_of((((c * 2 + x) * 2 + f) * depth + z) * PIECE, PIECE)

    own_piece_row = piece_row(along_z, along_x, core, own_f)

    def gather_far(p):
        unit = s.table.at[p, pl.ds(own_row, UNIT)]
        return [
            remote(unit, unit, gather_sems, (p, k), blk=peer)
            for k, (peer, _) in enumerate(far)
        ]

    def all_far():
        found = []
        for dz in sorted(range(depth), reverse=True):
            for dx in (1, 0):
                for f in (1 - own_f, own_f):
                    if dz or dx or f is not own_f:
                        z, x = lax.rem(along_z + dz, depth), lax.rem(along_x + dx, 2)
                        found.append((z * 4 + x * 2 + core, f, piece_row(z, x, core, f)))
        return found

    def gather_pieces_z(layer):
        piece = s.table.at[4 + layer, pl.ds(own_piece_row, PIECE)]
        peers = [
            lax.rem(along_z + dz, depth) * 4 + along_x * 2 + core for dz in range(1, depth)
        ]
        return [
            remote(piece, piece, gather_sems, (4 + layer, k), blk=peer)
            for k, peer in enumerate(reversed(peers))
        ]

    def gather_pieces_xy(layer):
        column = piece_row(0, along_x, core, own_f)
        piece = s.table.at[4 + layer, pl.ds(column, depth * PIECE)]
        other = along_z * 4 + (1 - along_x) * 2 + core
        peers = [(other, 1 - own_f), (other, own_f), (me, 1 - own_f)]
        return [
            remote(piece, piece, gather_sems, (4 + layer, 8 + k), blk=peer, fsdp=f)
            for k, (peer, f) in enumerate(peers)
        ]

    def gather_core(q):
        half = s.table.at[q, half_rows(core)]
        return [remote(half, half, gather_sems, (q, core_slot), blk=sibling)]

    def gather_rims(p):
        low = remote(
            s.ext.at[p, pl.ds(RIM, RIM)],
            s.ext.at[p, pl.ds(RIM + SMALL, RIM)],
            gather_sems,
            (p, low_slot),
            blk=before,
        )
        high = remote(
            s.ext.at[p, pl.ds(SMALL, RIM)],
            s.ext.at[p, pl.ds(0, RIM)],
            gather_sems,
            (p, high_slot),
            blk=after,
        )
        return [low, high]

    def part_of(q):
        return q if isinstance(q, int) and q >= 4 else 2 + lax.rem(q, 2)

    def reduce_core(q):
        return [
            remote(
                s.table.at[part_of(q), half_rows(1 - core)],
                s.land_core.at[q],
                reduce_sems,
                (q, core_slot),
                blk=sibling,
            )
        ]

    def reduce_far(p):
        return [
            remote(
                s.table.at[part_of(p), pl.ds(row, UNIT)],
                s.land.at[p, k],
                reduce_sems,
                (p, k),
                blk=peer,
            )
            for k, (peer, row) in enumerate(far)
        ]

    def reduce_pieces(layer):
        return [
            remote(
                s.table.at[4 + layer, pl.ds(row, PIECE)],
                s.land_piece.at[layer, k],
                reduce_sems,
                (4 + layer, k),
                blk=peer,
                fsdp=f,
            )
            for k, (peer, f, row) in enumerate(all_far())
        ]

    def reduce_rims(p):
        low = remote(
            s.send_rim.at[p, 0], s.land_rim.at[p, 1], reduce_sems, (p, low_slot), blk=before
        )
        high = remote(
            s.send_rim.at[p, 1], s.land_rim.at[p, 0], reduce_sems, (p, high_slot), blk=after
        )
        return [low, high]

    def start(copies):
        for copy in copies:
            copy.start()

    def finish(copies):
        for copy in copies:
            copy.wait()

    def add_core(q):
        finish(reduce_core(q))
        first = unit_row(0, 0, core)
        at = part_of(q)

        def body(i, carry):
            here = pl.ds(pl.multiple_of(first + i * UNIT, UNIT), UNIT)
            there = pl.ds(pl.multiple_of(i * UNIT, UNIT), UNIT)
            s.table[at, here] = (
                s.table[at, here].astype(F32) + s.land_core[q, there].astype(F32)
            ).astype(BF16)
            return carry

        lax.fori_loop(0, 2 * depth, body, 0)

    def reduce_on(p):
        add_core(p)
        start(reduce_far(p))

    def reduced_unit(p):
        finish(reduce_far(p))
        total = s.table[part_of(p), pl.ds(own_row, UNIT)].astype(F32)
        for k in range(len(far)):
            total = total + s.land[p, k].astype(F32)
        return total

    def prepare(m):
        def compact(rows, block):
            part = rows[:, block * BIG : (block + 1) * BIG]
            tile = jnp.concatenate([part[:16], part[16:]], axis=1)
            return jnp.concatenate([tile[:8], tile[8:]], axis=1)

        picked = s.neighbours[m]
        usable = s.slot_mask[m]
        device = lax.shift_right_logical(picked, 8)
        offset = jnp.bitwise_and(picked, 255)
        z = lax.shift_right_logical(device, 2)
        x = jnp.bitwise_and(lax.shift_right_logical(device, 1), 1)
        c = jnp.bitwise_and(device, 1)
        big_place = ((c * 2 + x) * depth + z) * UNIT + offset
        small_place = (device - me) * SMALL + (offset - BIG)
        for block in range(BLOCKS):
            if block == 0:
                s.place[m, 0] = compact(big_place, 0)
            else:
                s.place[m, block] = compact(small_place + (RIM - (block - 1) * BIG), block)
            s.used[m, block] = compact(usable, block).astype(F32)
        s.hidden_t[m] = jnp.transpose(s.features[m])
        s.grad_act[m] = jnp.transpose(s.out_cotangent[m].astype(F32))

    def mark(row, least):
        tile = lax.broadcasted_iota(jnp.int32, (256, LANES), 0)
        return jnp.where(tile == row - least, 1.0, 0.0).astype(BF16)

    def lanes_of(step):
        return pl.ds(pl.multiple_of(step * LANES, LANES), LANES)

    def mark_big(m):
        slot = m if kept > 1 else 0

        def tile(w, carry):
            here = pl.ds(pl.multiple_of(w * 256, 256), 256)
            for step in range(STEPS):
                lanes = pl.ds(step * LANES, LANES)
                row = s.place[m, 0, pl.ds(step, 1), :]
                s.hot_big[slot, here, lanes] = mark(row, w * 256)
            return carry

        lax.fori_loop(0, big_total // 256, tile, 0)

    def mark_small(m):
        slot = m if kept > 1 else 0

        def block_body(b, carry):
            for step in range(STEPS):
                lanes = pl.ds(step * LANES, LANES)
                row = s.place[m, b + 1, pl.ds(step, 1), :]
                s.hot_small[slot, b, :, lanes] = mark(row, 0)
            return carry

        lax.fori_loop(0, SMALLS, block_body, 0)

    place = me * 2 + own_f
    vector_row, vector_lane = lax.div(place, 8), lax.rem(place, 8) * 32

    def vector_place():
        lane = lax.broadcasted_iota(jnp.int32, (32, WIDTH), 1)
        element = lax.broadcasted_iota(jnp.int32, (32, WIDTH), 0)
        return jnp.where(lane == element + vector_lane, 1.0, 0.0)

    def own_row_of_eight():
        return lax.broadcasted_iota(jnp.int32, (8, WIDTH), 0) == vector_row

    def own_piece(layer):
        flat = s.projections[...].astype(F32)[layer : layer + 1]
        rows = [flat[:, i * WIDTH : (i + 1) * WIDTH] for i in range(CHUNK)]
        own = s.vectors[...][layer : layer + 1].astype(F32)
        own = nn(jnp.broadcast_to(own, (8, 32)).astype(BF16), vector_place().astype(BF16))
        rows.append(jnp.where(own_row_of_eight(), own, 0.0))
        s.table[4 + layer, pl.ds(own_piece_row, PIECE)] = jnp.concatenate(
            rows, axis=0
        ).astype(BF16)

    def chunks():
        for c in range(2):
            for x in range(2):
                for z in range(depth):
                    for y in range(2):
                        yield (
                            ((z * 2 + x) * 2 + c) * 2 + y,
                            (((c * 2 + x) * 2 + y) * depth + z) * PIECE,
                        )

    def load_layer(layer):
        if shared_weights:
            pieces = {
                chunk: s.table[4 + layer, pl.ds(at, PIECE)].astype(F32)
                for chunk, at in chunks()
            }
            s.weights[layer] = jnp.concatenate(
                [pieces[i][:CHUNK] for i in range(len(pieces))], axis=0
            ).astype(BF16)
            rows = pieces[0][CHUNK:]
            for i in range(1, len(pieces)):
                rows = rows + pieces[i][CHUNK:]
        else:
            rows = s.all_vectors[layer].astype(F32)
        for k in range(3):
            rows_k = pl.ds(k * WIDTH, WIDTH)
            s.weights_t[layer, rows_k] = jnp.transpose(s.weights[layer, rows_k])
        which = lax.broadcasted_iota(jnp.int32, (8, 512), 0)
        lane = lax.shift_right_logical(lax.broadcasted_iota(jnp.int32, (8, 512), 1), 7)
        chosen = jnp.where(which == lane, 1.0, 0.0).astype(BF16)
        wide = tn(rows.astype(BF16), chosen)
        for k in range(4):
            s.vecs[layer, k] = wide[:, k * 128 : (k + 1) * 128]

    def share(p, hidden):
        s.table[p, pl.ds(own_row, UNIT)] = hidden[:BIG]
        s.ext[p, pl.ds(RIM, SMALL)] = hidden[BIG:]

    def aim(p, layer, m, hidden):
        s.targets[p] = 0.5 * nt(s.weights_t[layer, pl.ds(WIDTH, WIDTH)], hidden)
        bias = s.vecs[layer, 1]
        s.residue[m] = nt(s.weights_t[layer, pl.ds(2 * WIDTH, WIDTH)], hidden) + jnp.concatenate(
            [bias, bias], axis=1
        )

    def spread(p, block):
        wide = s.targets[p, :, pl.ds((block // 2) * 128, 128)]
        odd = block % 2 == 1
        tile = jnp.where(upper_lanes() == odd, wide, pltpu.roll(wide, 64, 1))
        s.doubled[block] = tile

    def score(p, layer, block, pair, turned, hot):
        lanes = pl.ds(pair * 2 * LANES, 2 * LANES)
        got = nn(turned[...], hot[:, lanes])
        rows_of[block][p, :, lanes] = got.astype(BF16)
        for h in range(HEADS):
            rows = slice(h * HEAD_WIDTH, (h + 1) * HEAD_WIDTH)
            wanted = s.doubled[block, rows, :]
            attn = s.vecs[layer, 0, rows, :]
            for part in range(4):
                z = got[rows, part * 128 : (part + 1) * 128] + wanted
                lifted = z * (jnp.tanh(z) + 1.5)
                half = (part % 2) * 128
                s.scores[block, 2 * pair + part // 2, h : h + 1, half : half + 128] = jnp.sum(
                    lifted * attn, axis=0, keepdims=True
                )

    def halves_max(wide):
        tile = jnp.maximum(wide[:, :128], wide[:, 128:])
        tile = jnp.maximum(tile, pltpu.roll(tile, 64, 1))
        return jnp.concatenate([tile, tile], axis=1)

    def halves_sum(wide):
        tile = wide[:, :128] + wide[:, 128:]
        tile = tile + pltpu.roll(tile, 64, 1)
        return jnp.concatenate([tile, tile], axis=1)

    def softmax(p, m, block):
        used = [s.used[m, block, pl.ds(i, 1), :] for i in range(STEPS)]
        logits = [
            jnp.where(used[i] > 0, 0.8 * s.scores[block, i], -1e30) for i in range(STEPS)
        ]
        largest = halves_max(functools.reduce(jnp.maximum, logits))
        raised = [jnp.exp(logits[i] - largest) * used[i] for i in range(STEPS)]
        scale = 1.0 / halves_sum(functools.reduce(jnp.add, raised))
        for i in range(STEPS):
            s.shares[p, block, i] = raised[i] * scale

    def pass_messages(p, m, block):
        for h in range(HEADS):
            rows = slice(h * HEAD_WIDTH, (h + 1) * HEAD_WIDTH)
            total = jnp.zeros((HEAD_WIDTH, 128), F32)
            for step in range(STEPS):
                for half in range(2):
                    lanes = pl.ds(step * LANES + half * 128, 128)
                    share = s.shares[p, block, step, h : h + 1, half * 128 : (half + 1) * 128]
                    share = share.astype(BF16).astype(F32)
                    total = total + share * rows_of[block][p, rows, lanes].astype(F32)
            s.message[m, block, rows, :] = total

    def sources(layer, rows):
        return (0.5 * nt(s.weights_t[layer, pl.ds(0, WIDTH)], rows)).astype(BF16)

    def smalls(p, layer, m, progress):
        finish(gather_rims(p))
        for b in range(SMALLS):
            s.turned_small[b] = sources(layer, s.ext[p, pl.ds(b * BIG, 256)])
            spread(p, b + 1)
        for b in range(SMALLS):
            if b == 1:
                progress()
            hot = s.hot_small.at[m if kept > 1 else 0, b]
            for pair in range(STEPS // 2):
                score(p, layer, b + 1, pair, s.turned_small.at[b], hot)
            softmax(p, m, b + 1)

    def big(p, layer, m):
        s.turned_big[...] = sources(layer, s.table[p])
        spread(p, 0)
        hot = s.hot_big.at[m if kept > 1 else 0]
        for pair in range(STEPS // 2):
            score(p, layer, 0, pair, s.turned_big, hot)
            if pair + 1 < BLOCKS:
                pass_messages(p, m, pair + 1)
        softmax(p, m, 0)
        pass_messages(p, m, 0)

    def normalise(p, layer, m):
        gain, shift = s.vecs[layer, 2], s.vecs[layer, 3]
        for t in range(2):
            lanes = slice(t * 128, (t + 1) * 128)
            total = join_halves(s.message[m, 2 * t], s.message[m, 2 * t + 1])
            y = 2.0 * total + s.residue[m, :, lanes]
            centred = y - jnp.sum(y, axis=0, keepdims=True) * (1.0 / WIDTH)
            spread_of = jnp.sum(centred * centred, axis=0, keepdims=True) * (1.0 / WIDTH)
            inverse = lax.rsqrt(spread_of + EPSILON)
            normed = centred * inverse
            shifted = normed * gain + shift
            s.normed[p, :, lanes] = normed
            s.inverse[p, 0:1, lanes] = inverse
            act = jnp.where(shifted > 0, shifted, jnp.exp(jnp.minimum(shifted, 0.0)) - 1.0)
            s.act[:, lanes] = act.astype(BF16)

        @pl.when(layer == 0)
        def _():
            s.hidden_t[m + 2] = s.act[...]
            hidden = jnp.transpose(s.act[...])
            share(m + 2, hidden)
            start(gather_rims(m + 2))
            start(gather_far(m + 2))
            aim(m + 2, 1, m, hidden)

        @pl.when(layer == 1)
        def _():
            s.layer_output[m] = jnp.transpose(s.act[...])

    def forward(layer, carry):
        first, second = 2 * layer, 2 * layer + 1

        def small_body(m, inner):
            if kept == 1:
                mark_small(m)

            def progress():
                @pl.when(m == 1)
                def _():
                    finish(gather_far(first))
                    start(gather_core(first))

            smalls(first + m, layer, m, progress)
            return inner

        lax.fori_loop(0, MICRO, small_body, 0)

        def big_body(m, inner):
            if kept == 1:
                mark_big(m)
            finish(gather_core(first + m))
            if shared_weights:

                @pl.when(jnp.logical_and(layer == 0, m == 0))
                def _():
                    finish(gather_pieces_xy(1))
                    start(gather_core(5))

            big(first + m, layer, m)

            @pl.when(m == 0)
            def _():
                finish(gather_far(second))
                start(gather_core(second))

            @pl.when(jnp.logical_and(layer == 0, m == 0))
            def _():
                if shared_weights:
                    finish(gather_core(5))
                load_layer(1)

            normalise(first + m, layer, m)
            return inner

        lax.fori_loop(0, MICRO, big_body, 0)
        return carry

    def through_norm(p, layer, m):
        gain, shift = s.vecs[layer, 2], s.vecs[layer, 3]
        upper = upper_lanes()
        for t in range(2):
            lanes = slice(t * 128, (t + 1) * 128)
            normed = s.normed[p, :, lanes]
            shifted = normed * gain + shift
            grad = s.grad_act[m, :, lanes] * jnp.where(
                shifted > 0, 1.0, jnp.exp(jnp.minimum(shifted, 0.0))
            )
            s.grad_vecs[layer, 2] = s.grad_vecs[layer, 2] + grad * normed
            s.grad_vecs[layer, 3] = s.grad_vecs[layer, 3] + grad
            grad = grad * gain
            first = jnp.sum(grad, axis=0, keepdims=True) * (1.0 / WIDTH)
            second = jnp.sum(grad * normed, axis=0, keepdims=True) * (1.0 / WIDTH)
            grad = s.inverse[p, 0:1, lanes] * (grad - first - normed * second)
            s.grad_vecs[layer, 1] = s.grad_vecs[layer, 1] + grad
            s.grad_out_t[p, :, lanes] = grad.astype(BF16)
            grad = grad.astype(BF16).astype(F32)
            other = pltpu.roll(grad, 64, 1)
            s.grad_out[m, 2 * t] = jnp.where(upper, other, grad)
            s.grad_out[m, 2 * t + 1] = jnp.where(upper, grad, other)

    def share_grads(p, m, block, step):
        for h in range(HEADS):
            rows = slice(h * HEAD_WIDTH, (h + 1) * HEAD_WIDTH)
            grad = s.grad_out[m, block, rows, :]
            for half in range(2):
                lanes = pl.ds(pl.multiple_of(step * LANES + half * 128, 128), 128)
                product = rows_of[block][p, rows, lanes].astype(F32) * grad
                s.share_grad[m, block, step, h : h + 1, half * 128 : (half + 1) * 128] = (
                    jnp.sum(product, axis=0, keepdims=True)
                )

    def logit_grads(p, m, block):
        shares = [s.shares[p, block, i] for i in range(STEPS)]
        grads = [s.share_grad[m, block, i] for i in range(STEPS)]
        total = halves_sum(functools.reduce(jnp.add, [a * b for a, b in zip(shares, grads)]))
        for i in range(STEPS):
            s.share_grad[m, block, i] = 0.8 * shares[i] * (grads[i] - total)

    def make_terms(p, layer, m, block, pair):
        for h in range(HEADS):
            rows = slice(h * HEAD_WIDTH, (h + 1) * HEAD_WIDTH)
            wanted = s.doubled[block, rows, :]
            attn = s.vecs[layer, 0, rows, :]
            grad = s.grad_out[m, block, rows, :]
            target_sum = s.message[m, block, rows, :]
            attn_sum = s.grad_vecs[layer, 0, rows, :]
            for part in range(4):
                step, half = 2 * pair + part // 2, (part % 2) * 128
                lanes = pl.ds(step * LANES + half, 128)
                z = rows_of[block][p, rows, lanes].astype(F32) + wanted
                t = jnp.tanh(z)
                w = t + 1.5
                logit_grad = s.share_grad[m, block, step, h : h + 1, half : half + 128]
                attn_sum = attn_sum + logit_grad * (z * w)
                slope = logit_grad * (w + z * (1.0 - t * t))
                target_sum = target_sum + slope
                share = s.shares[p, block, step, h : h + 1, half : half + 128]
                share = share.astype(BF16).astype(F32)
                terms[pair % 2][rows, part * 128 : (part + 1) * 128] = (
                    share * grad + attn * slope
                ).astype(BF16)
            s.message[m, block, rows, :] = target_sum
            s.grad_vecs[layer, 0, rows, :] = attn_sum

    def all_share_grads(p, m, block):
        for step in range(STEPS):
            share_grads(p, m, block, step)
        logit_grads(p, m, block)

    def big_back(p, layer, m):
        spread(p, 0)
        s.message[m] = jnp.zeros((BLOCKS, WIDTH, 128), F32)
        all_share_grads(p, m, 0)
        for pair in range(STEPS // 2):
            make_terms(p, layer, m, 0, pair)
            lanes = pl.ds(pair * 2 * LANES, 2 * LANES)
            added = nt(s.hot_big[m if kept > 1 else 0, :, lanes], terms[pair % 2][...])
            if pair == 0:
                s.part_sum[...] = added
            elif pair + 1 < STEPS // 2:
                s.part_sum[...] = s.part_sum[...] + added
            else:
                s.table[2 + m] = (s.part_sum[...] + added).astype(BF16)

    def smalls_back(p, layer, m, progress):
        for b in range(SMALLS):
            spread(p, b + 1)
        s.grad_ext[...] = jnp.zeros_like(s.grad_ext)
        all_share_grads(p, m, 1)
        for b in range(SMALLS):
            if b == 1:
                progress()
            if b + 1 < SMALLS:
                all_share_grads(p, m, b + 2)
            here = pl.ds(b * BIG, 256)
            for pair in range(STEPS // 2):
                make_terms(p, layer, m, b + 1, pair)
                lanes = pl.ds(pair * 2 * LANES, 2 * LANES)
                hot = s.hot_small[m if kept > 1 else 0, b, :, lanes]
                s.grad_ext[here] = s.grad_ext[here] + nt(hot, terms[pair % 2][...])
        s.send_rim[p, 0] = s.grad_ext[pl.ds(0, RIM)].astype(BF16)
        s.send_rim[p, 1] = s.grad_ext[pl.ds(RIM + SMALL, RIM)].astype(BF16)
        start(reduce_rims(p))
        s.grad_small[m] = s.grad_ext[pl.ds(RIM, SMALL)]
        attn = s.vecs[layer, 0]
        for t in range(2):
            lanes = slice(t * 128, (t + 1) * 128)
            total = join_halves(s.message[m, 2 * t], s.message[m, 2 * t + 1])
            s.grad_targets_t[p, :, lanes] = (attn * total).astype(BF16)

    def finalise(p, layer, m):
        unit = reduced_unit(p)
        finish(reduce_rims(p))
        low = s.grad_small[m, pl.ds(0, RIM)] + s.land_rim[p, 0].astype(F32)
        high = s.grad_small[m, pl.ds(RIM, RIM)] + s.land_rim[p, 1].astype(F32)
        rows = jnp.concatenate([unit, low, high], axis=0)
        s.grad_sources_t[p] = jnp.transpose(rows.astype(BF16))
        s.grad_act[m] = (
            nn(s.weights[layer, pl.ds(0, WIDTH)], s.grad_sources_t[p])
            + nn(s.weights[layer, pl.ds(WIDTH, WIDTH)], s.grad_targets_t[p])
            + nn(s.weights[layer, pl.ds(2 * WIDTH, WIDTH)], s.grad_out_t[p])
        )

    def weight_grads(layer):
        for k, grads in enumerate((s.grad_sources_t, s.grad_targets_t, s.grad_out_t)):
            total = nt(s.hidden_t[2 * layer], grads[2 * layer])
            if layer == 0 and k == 0:
                total = total + s.head_weights[...] + tn(s.ext[1], s.grad_ext[...].astype(BF16))
            else:
                total = total + nt(s.hidden_t[2 * layer + 1], grads[2 * layer + 1])
            if shared_weights:
                s.grad_weights[pl.ds(k * WIDTH, WIDTH)] = total
            else:
                s.weight_sums[layer, pl.ds(k * WIDTH, WIDTH)] = total
        vector_rows = jnp.zeros((8, WIDTH), F32)
        for k in range(4):
            chosen = jnp.where(
                lax.broadcasted_iota(jnp.int32, (8, 128), 0) == k, 2.0 if k == 0 else 1.0, 0.0
            ).astype(F32)
            vector_rows = vector_rows + nt(
                chosen, s.grad_vecs[layer, k], precision=lax.Precision.HIGHEST
            )
        if not shared_weights:
            s.vector_sums[layer] = vector_rows
            return
        for chunk, at in chunks():
            s.table[4 + layer, pl.ds(at, PIECE)] = jnp.concatenate(
                [s.grad_weights[pl.ds(chunk * CHUNK, CHUNK)], vector_rows], axis=0
            ).astype(BF16)
        start(reduce_core(4 + layer))

    def weights_on(layer):
        add_core(4 + layer)
        start(reduce_pieces(layer))

    def weights_done(layer):
        finish(reduce_pieces(layer))
        total = s.table[4 + layer, pl.ds(own_piece_row, PIECE)].astype(F32)
        for k in range(2 * len(far) + 1):
            total = total + s.land_piece[layer, k].astype(F32)
        s.weight_sums[layer : layer + 1, :] = jnp.concatenate(
            [total[i : i + 1] for i in range(CHUNK)], axis=1
        )
        own = jnp.where(own_row_of_eight(), total[CHUNK:], 0.0)
        own = jnp.sum(own, axis=0, keepdims=True)
        own = nt(
            jnp.broadcast_to(own, (8, WIDTH)), vector_place(), precision=lax.Precision.HIGHEST
        )
        s.vector_sums[layer : layer + 1, :] = own[:1]

    def backward(i, carry):
        layer = 1 - i
        first, second = 2 * layer, 2 * layer + 1

        def body(m, inner):
            if kept == 1:
                mark_big(m)
                mark_small(m)

            @pl.when(jnp.logical_and(i == 1, m == 0))
            def _():
                finalise(2, 1, 0)

            through_norm(first + m, layer, m)
            big_back(first + m, layer, m)

            @pl.when(jnp.logical_and(i == 1, m == 1))
            def _():
                s.head_weights[...] = tn(s.table[1], s.table[3])

            start(reduce_core(first + m))

            @pl.when(jnp.logical_and(i == 1, m == 0))
            def _():
                finalise(3, 1, 1)
                weight_grads(1)

            def progress():
                reduce_on(first + m)
                if shared_weights:

                    @pl.when(jnp.logical_and(i == 1, m == 0))
                    def _():
                        weights_on(1)

            smalls_back(first + m, layer, m, progress)
            return inner

        lax.fori_loop(0, MICRO, body, 0)
        return carry

    barrier = pltpu.get_barrier_semaphore()
    partners = [dict(blk=peer) for peer, _ in far]
    if shared_weights:
        partners = [dict(blk=peer, fsdp=f) for peer, f, _ in all_far()]
    partners += [dict(blk=d) for d in (sibling, before, after)]
    for partner in partners:
        pl.semaphore_signal(barrier, inc=1, device_id=partner, device_id_type=MESH)
    if shared_weights:
        for layer in range(LAYERS):
            own_piece(layer)
    pl.semaphore_wait(barrier, len(partners))

    if shared_weights:
        for layer in range(LAYERS):
            start(gather_pieces_z(layer))
    for m in range(MICRO):
        share(m, s.features[m])
        start(gather_rims(m))
    for m in range(MICRO):
        prepare(m)
    if not shared_weights:
        start(gather_far(0))
        start(gather_far(1))
    s.scores[...] = jnp.zeros_like(s.scores)
    s.share_grad[...] = jnp.zeros_like(s.share_grad)
    s.grad_vecs[...] = jnp.zeros_like(s.grad_vecs)
    if kept > 1:
        mark_small(0)
        mark_small(1)
    if shared_weights:
        finish(gather_pieces_z(0))
        start(gather_pieces_xy(0))
        finish(gather_pieces_z(1))
        start(gather_far(0))
    if kept > 1:
        mark_big(0)
        mark_big(1)
    if shared_weights:
        finish(gather_pieces_xy(0))
        start(gather_core(4))
        start(gather_pieces_xy(1))
        start(gather_far(1))
        finish(gather_core(4))
    load_layer(0)
    for m in range(MICRO):
        aim(m, 0, m, s.features[m])
    lax.fori_loop(0, LAYERS, forward, 0)
    lax.fori_loop(0, LAYERS, backward, 0)
    finalise(0, 0, 0)
    weight_grads(0)
    s.input_gradient[0] = jnp.transpose(s.grad_act[0])
    if shared_weights:
        weights_on(0)
    finalise(1, 0, 1)
    s.input_gradient[1] = jnp.transpose(s.grad_act[1])
    if shared_weights:
        weights_done(1)
        weights_done(0)


def hand_over(*refs):
    *arrays, sems = refs
    count = len(arrays) // 2
    copies = [
        pltpu.make_async_copy(arrays[k], arrays[count + k], sems.at[k]) for k in range(count)
    ]
    for copy in copies:
        copy.start()
    for copy in copies:
        copy.wait()


def per_device(
    depth, fsdp_count, features, neighbours, slot_mask, projections, vectors, out_cotangent
):
    layers, weight_chunk = projections.shape
    shared_weights = fsdp_count == 2 and weight_chunk == CHUNK * WIDTH and depth == 4
    inputs = dict(
        features=features[:, 0],
        neighbours=jnp.swapaxes(neighbours[:, 0], 1, 2),
        slot_mask=jnp.swapaxes(slot_mask[:, 0], 1, 2),
        out_cotangent=out_cotangent[:, 0],
    )
    if shared_weights:
        inputs["projections"] = projections
        inputs["vectors"] = vectors
        weight_shape, vector_shape = projections.shape, vectors.shape
    else:
        axes = ("blk", "fsdp")
        gathered = lax.all_gather(projections, axes, axis=1, tiled=True)
        inputs["weights"] = gathered.reshape(layers, 3 * WIDTH, WIDTH)
        gathered = lax.all_gather(vectors, axes, axis=1, tiled=True)
        inputs["all_vectors"] = jnp.pad(
            gathered.reshape(layers, 4, WIDTH), ((0, 0), (0, 4), (0, 0))
        )
        weight_shape, vector_shape = (layers, 3 * WIDTH, WIDTH), (layers, 8, WIDTH)
    outputs = dict(
        layer_output=jax.ShapeDtypeStruct((MICRO, NODES, WIDTH), BF16),
        input_gradient=jax.ShapeDtypeStruct((MICRO, NODES, WIDTH), F32),
        weight_sums=jax.ShapeDtypeStruct(weight_shape, F32),
        vector_sums=jax.ShapeDtypeStruct(vector_shape, F32),
    )
    scratch = scratch_plan(depth, shared_weights)
    in_vmem = pl.BlockSpec(memory_space=pltpu.VMEM)
    results = pl.pallas_call(
        functools.partial(
            step_kernel, depth, shared_weights, [*inputs, *outputs, *scratch]
        ),
        out_shape=list(outputs.values()),
        in_specs=[in_vmem] * len(inputs),
        out_specs=[in_vmem] * len(outputs),
        scratch_shapes=list(scratch.values()),
        compiler_params=pltpu.CompilerParams(
            collective_id=0, has_side_effects=True, vmem_limit_bytes=63 * 1024 * 1024
        ),
    )(*inputs.values())
    if shared_weights:
        results = pl.pallas_call(
            hand_over,
            out_shape=list(outputs.values()),
            in_specs=[pl.BlockSpec(memory_space=pl.ANY)] * len(outputs),
            out_specs=[in_vmem] * len(outputs),
            scratch_shapes=[pltpu.SemaphoreType.DMA((len(outputs),))],
        )(*results)
    layer_output, input_gradient, weight_sums, vector_sums = results
    if not shared_weights:
        axes = ("blk", "fsdp")
        weight_sums = lax.psum_scatter(
            weight_sums.reshape(layers, -1), axes, scatter_dimension=1, tiled=True
        )
        vector_sums = lax.psum_scatter(
            vector_sums[:, :4].reshape(layers, -1), axes, scatter_dimension=1, tiled=True
        )
    return layer_output[:, None], input_gradient[:, None], weight_sums, vector_sums


def solution(mesh):
    return jax.shard_map(
        functools.partial(per_device, mesh.shape["blk"] // 4, mesh.shape["fsdp"]),
        mesh=mesh,
        in_specs=(
            P(None, "fsdp", "blk", None),
            P(None, "fsdp", "blk", None),
            P(None, "fsdp", "blk", None),
            P(None, ("blk", "fsdp")),
            P(None, ("blk", "fsdp")),
            P(None, "fsdp", "blk", None),
        ),
        out_specs=(
            P(None, "fsdp", "blk", None),
            P(None, "fsdp", "blk", None),
            P(None, ("blk", "fsdp")),
            P(None, ("blk", "fsdp")),
        ),
        check_vma=False,
    )
```

```python
import functools
import types

import jax
import jax.numpy as jnp
from jax import lax
from jax.experimental import pallas as pl
from jax.experimental.pallas import tpu as pltpu
from jax.sharding import PartitionSpec as P

HEADS = 4
MICRO = 2
LAYERS = 2
SLOTS = 32
WIDTH = 256
HEAD_WIDTH = WIDTH // HEADS
NODES = 256
BIG = 64
SMALL = NODES - BIG
RIM = 96
EXT = SMALL + 2 * RIM
BLOCKS = NODES // BIG
SMALLS = BLOCKS - 1
PAIRS = BIG * SLOTS
STEPS = 8
LANES = PAIRS // STEPS
UNIT = BIG
CHUNK = 24
PIECE = UNIT // 2
EPSILON = 1e-05
F32 = jnp.float32
BF16 = jnp.bfloat16
MESH = pl.DeviceIdType.MESH


def nn(left, right):
    return lax.dot_general(
        left, right, (((1,), (0,)), ((), ())), preferred_element_type=F32
    )


def nt(left, right, precision=None):
    return lax.dot_general(
        left, right, (((1,), (1,)), ((), ())), preferred_element_type=F32, precision=precision
    )


def tn(left, right):
    return lax.dot_general(
        left, right, (((0,), (0,)), ((), ())), preferred_element_type=F32
    )


def upper_lanes():
    return lax.broadcasted_iota(jnp.int32, (WIDTH, 128), 1) >= 64


def join_halves(even, odd):
    upper = upper_lanes()
    return jnp.where(upper, odd, even) + pltpu.roll(jnp.where(upper, even, odd), 64, 1)


def scratch_plan(depth, shared_weights):
    big_total = 4 * depth * UNIT
    tables = 4 + (LAYERS if shared_weights else 0)
    copies = MICRO if depth <= 4 else 1
    peers = 2 * depth - 1
    vm = pltpu.VMEM
    plan = dict(
        features=vm((MICRO, NODES, WIDTH), BF16),
        neighbours=vm((MICRO, SLOTS, NODES), jnp.int32),
        slot_mask=vm((MICRO, SLOTS, NODES), jnp.int32),
        out_cotangent=vm((MICRO, NODES, WIDTH), BF16),
        layer_output=vm((MICRO, NODES, WIDTH), BF16),
        input_gradient=vm((MICRO, NODES, WIDTH), F32),
        own_sems=pltpu.SemaphoreType.DMA((7,)),
        hot_big=vm((copies, STEPS // 2, big_total, 2 * LANES), BF16),
        hot_small=vm((copies, SMALLS, STEPS // 2, 256, 2 * LANES), BF16),
        place=vm((MICRO, BLOCKS, STEPS, LANES), jnp.int32),
        used=vm((MICRO, BLOCKS, STEPS, LANES), F32),
        rows_0=vm((4, 2 * STEPS, WIDTH, 128), BF16),
        rows_1=vm((4, 2 * STEPS, WIDTH, 128), BF16),
        rows_2=vm((4, 2 * STEPS, WIDTH, 128), BF16),
        rows_3=vm((4, 2 * STEPS, WIDTH, 128), BF16),
        shares=vm((4, BLOCKS, STEPS, 8, LANES), F32),
        table=vm((tables, big_total, WIDTH), BF16),
        ext=vm((4, EXT, WIDTH), BF16),
        turned_big=vm((WIDTH, big_total), BF16),
        turned_small=vm((SMALLS, WIDTH, 256), BF16),
        hidden_t=vm((4, WIDTH, NODES), BF16),
        weights_t=vm((LAYERS, 3 * WIDTH, WIDTH), BF16),
        vecs=vm((LAYERS, 4, WIDTH, 128), F32),
        targets=vm((4, WIDTH, NODES), F32),
        residue=vm((MICRO, WIDTH, NODES), F32),
        doubled=vm((BLOCKS, WIDTH, 128), F32),
        scores=vm((BLOCKS, STEPS, 8, LANES), F32),
        share_grad=vm((MICRO, BLOCKS, STEPS, 8, LANES), F32),
        message=vm((MICRO, BLOCKS, WIDTH, 128), F32),
        normed=vm((4, WIDTH, NODES), F32),
        inverse=vm((4, 8, NODES), F32),
        act=vm((WIDTH, NODES), BF16),
        grad_act=vm((MICRO, WIDTH, NODES), F32),
        grad_out=vm((MICRO, BLOCKS, WIDTH, 128), F32),
        grad_out_t=vm((4, WIDTH, NODES), BF16),
        grad_targets_t=vm((4, WIDTH, NODES), BF16),
        grad_sources_t=vm((4, WIDTH, NODES), BF16),
        terms_0=vm((WIDTH, 2 * LANES), BF16),
        terms_1=vm((WIDTH, 2 * LANES), BF16),
        part_sum=vm((big_total, WIDTH), F32),
        grad_ext=vm((EXT, WIDTH), F32),
        head_weights=vm((WIDTH, WIDTH), F32),
        grad_small=vm((MICRO, SMALL, WIDTH), F32),
        grad_vecs=vm((LAYERS, 4, WIDTH, 128), F32),
        land_core=vm((tables, big_total // 2, WIDTH), BF16),
        land=vm((4, peers, UNIT, WIDTH), BF16),
        land_rim=vm((4, 2, RIM, WIDTH), BF16),
        send_rim=vm((4, 2, RIM, WIDTH), BF16),
        gather_send=pltpu.SemaphoreType.DMA((tables, 18)),
        gather_recv=pltpu.SemaphoreType.DMA((tables, 18)),
        reduce_send=pltpu.SemaphoreType.DMA((tables, 18)),
        reduce_recv=pltpu.SemaphoreType.DMA((tables, 18)),
    )
    if shared_weights:
        plan.update(
            weights=vm((LAYERS, 3 * WIDTH, WIDTH), BF16),
            grad_weights=vm((3 * WIDTH, WIDTH), F32),
            land_piece=vm((LAYERS, 2 * peers + 1, PIECE, WIDTH), BF16),
        )
    return plan


def step_kernel(depth, shared_weights, names, *refs):
    s = types.SimpleNamespace(**dict(zip(names, refs, strict=True)))
    big_total = 4 * depth * UNIT
    kept = s.hot_big.shape[0]
    me = lax.axis_index("blk")
    core = lax.rem(me, 2)
    along_x = lax.rem(lax.div(me, 2), 2)
    along_z = lax.div(me, 4)
    own_f = lax.axis_index("fsdp")
    block_count = 4 * depth
    before = lax.rem(me + block_count - 1, block_count)
    after = lax.rem(me + 1, block_count)
    sibling = along_z * 4 + along_x * 2 + (1 - core)

    def unit_row(z, x, c):
        return pl.multiple_of(((c * 2 + x) * depth + z) * UNIT, UNIT)

    own_row = unit_row(along_z, along_x, core)
    rows_of = (s.rows_0, s.rows_1, s.rows_2, s.rows_3)
    terms = (s.terms_0, s.terms_1)
    far = []
    for dz in sorted(range(depth), reverse=True):
        for dx in (1, 0):
            if dz or dx:
                z, x = lax.rem(along_z + dz, depth), lax.rem(along_x + dx, 2)
                far.append((z * 4 + x * 2 + core, unit_row(z, x, core)))

    def remote(src, dst, sems, slot, **where):
        send, recv = sems
        return pltpu.make_async_remote_copy(
            src_ref=src,
            dst_ref=dst,
            send_sem=send.at[slot],
            recv_sem=recv.at[slot],
            device_id=where,
            device_id_type=MESH,
        )

    gather_sems = (s.gather_send, s.gather_recv)
    reduce_sems = (s.reduce_send, s.reduce_recv)
    core_slot, low_slot, high_slot = 15, 16, 17

    def half_rows(c):
        return pl.ds(unit_row(0, 0, c), 2 * depth * UNIT)

    def piece_row(z, x, c, f):
        return pl.multiple_of((((c * 2 + x) * 2 + f) * depth + z) * PIECE, PIECE)

    own_piece_row = piece_row(along_z, along_x, core, own_f)

    def gather_far(p):
        unit = s.table.at[p, pl.ds(own_row, UNIT)]
        return [
            remote(unit, unit, gather_sems, (p, k), blk=peer)
            for k, (peer, _) in enumerate(far)
        ]

    def all_far():
        found = []
        for dz in sorted(range(depth), reverse=True):
            for dx in (1, 0):
                for f in (1 - own_f, own_f):
                    if dz or dx or f is not own_f:
                        z, x = lax.rem(along_z + dz, depth), lax.rem(along_x + dx, 2)
                        found.append((z * 4 + x * 2 + core, f, piece_row(z, x, core, f)))
        return found

    def gather_pieces_z(layer):
        piece = s.table.at[4 + layer, pl.ds(own_piece_row, PIECE)]
        peers = [
            lax.rem(along_z + dz, depth) * 4 + along_x * 2 + core for dz in range(1, depth)
        ]
        return [
            remote(piece, piece, gather_sems, (4 + layer, k), blk=peer)
            for k, peer in enumerate(reversed(peers))
        ]

    def gather_pieces_xy(layer):
        column = piece_row(0, along_x, core, own_f)
        piece = s.table.at[4 + layer, pl.ds(column, depth * PIECE)]
        other = along_z * 4 + (1 - along_x) * 2 + core
        peers = [(other, 1 - own_f), (other, own_f), (me, 1 - own_f)]
        return [
            remote(piece, piece, gather_sems, (4 + layer, 8 + k), blk=peer, fsdp=f)
            for k, (peer, f) in enumerate(peers)
        ]

    def gather_core(q):
        half = s.table.at[q, half_rows(core)]
        return [remote(half, half, gather_sems, (q, core_slot), blk=sibling)]

    def gather_rims(p):
        low = remote(
            s.ext.at[p, pl.ds(RIM, RIM)],
            s.ext.at[p, pl.ds(RIM + SMALL, RIM)],
            gather_sems,
            (p, low_slot),
            blk=before,
        )
        high = remote(
            s.ext.at[p, pl.ds(SMALL, RIM)],
            s.ext.at[p, pl.ds(0, RIM)],
            gather_sems,
            (p, high_slot),
            blk=after,
        )
        return [low, high]

    def part_of(q):
        return q if isinstance(q, int) and q >= 4 else 2 + lax.rem(q, 2)

    def reduce_core(q):
        return [
            remote(
                s.table.at[part_of(q), half_rows(1 - core)],
                s.land_core.at[q],
                reduce_sems,
                (q, core_slot),
                blk=sibling,
            )
        ]

    def reduce_far(p):
        return [
            remote(
                s.table.at[part_of(p), pl.ds(row, UNIT)],
                s.land.at[p, k],
                reduce_sems,
                (p, k),
                blk=peer,
            )
            for k, (peer, row) in enumerate(far)
        ]

    def reduce_pieces(layer):
        return [
            remote(
                s.table.at[4 + layer, pl.ds(row, PIECE)],
                s.land_piece.at[layer, k],
                reduce_sems,
                (4 + layer, k),
                blk=peer,
                fsdp=f,
            )
            for k, (peer, f, row) in enumerate(all_far())
        ]

    def reduce_rims(p):
        low = remote(
            s.send_rim.at[p, 0], s.land_rim.at[p, 1], reduce_sems, (p, low_slot), blk=before
        )
        high = remote(
            s.send_rim.at[p, 1], s.land_rim.at[p, 0], reduce_sems, (p, high_slot), blk=after
        )
        return [low, high]

    def bring(k, name):
        return [
            pltpu.make_async_copy(getattr(s, name + "_hbm"), getattr(s, name), s.own_sems.at[k])
        ]

    def hand_out(k, name, m=None):
        kept_ref, out_ref = getattr(s, name), getattr(s, name + "_hbm")
        if m is not None:
            kept_ref, out_ref = kept_ref.at[m], out_ref.at[m]
        return [pltpu.make_async_copy(kept_ref, out_ref, s.own_sems.at[k])]

    def start(copies):
        for copy in copies:
            copy.start()

    def finish(copies):
        for copy in copies:
            copy.wait()

    def add_core(q):
        finish(reduce_core(q))
        first = unit_row(0, 0, core)
        at = part_of(q)

        def body(i, carry):
            here = pl.ds(pl.multiple_of(first + i * UNIT, UNIT), UNIT)
            there = pl.ds(pl.multiple_of(i * UNIT, UNIT), UNIT)
            s.table[at, here] = (
                s.table[at, here].astype(F32) + s.land_core[q, there].astype(F32)
            ).astype(BF16)
            return carry

        lax.fori_loop(0, 2 * depth, body, 0)

    def reduce_on(p):
        add_core(p)
        start(reduce_far(p))

    def reduced_unit(p):
        finish(reduce_far(p))
        total = s.table[part_of(p), pl.ds(own_row, UNIT)].astype(F32)
        for k in range(len(far)):
            total = total + s.land[p, k].astype(F32)
        return total

    def prepare(m):
        def compact(rows, block):
            part = rows[:, block * BIG : (block + 1) * BIG]
            tile = jnp.concatenate([part[:16], part[16:]], axis=1)
            return jnp.concatenate([tile[:8], tile[8:]], axis=1)

        picked = s.neighbours[m]
        usable = s.slot_mask[m]
        device = lax.shift_right_logical(picked, 8)
        offset = jnp.bitwise_and(picked, 255)
        z = lax.shift_right_logical(device, 2)
        x = jnp.bitwise_and(lax.shift_right_logical(device, 1), 1)
        c = jnp.bitwise_and(device, 1)
        big_place = ((c * 2 + x) * depth + z) * UNIT + offset
        small_place = (device - me) * SMALL + (offset - BIG)
        for block in range(BLOCKS):
            if block == 0:
                s.place[m, 0] = compact(big_place, 0)
            else:
                s.place[m, block] = compact(small_place + (RIM - (block - 1) * BIG), block)
            s.used[m, block] = compact(usable, block).astype(F32)
        s.hidden_t[m] = jnp.transpose(s.features[m])
        s.grad_act[m] = jnp.transpose(s.out_cotangent[m].astype(F32))

    def mark(row, least):
        tile = lax.broadcasted_iota(jnp.int32, (256, LANES), 0)
        return jnp.where(tile == row - least, 1.0, 0.0).astype(BF16)

    def lanes_of(step):
        return pl.ds(pl.multiple_of(step * LANES, LANES), LANES)

    def mark_big(m):
        slot = m if kept > 1 else 0

        def tile(w, carry):
            here = pl.ds(pl.multiple_of(w * 256, 256), 256)
            for step in range(STEPS):
                lanes = pl.ds(step % 2 * LANES, LANES)
                row = s.place[m, 0, pl.ds(step, 1), :]
                s.hot_big[slot, step // 2, here, lanes] = mark(row, w * 256)
            return carry

        lax.fori_loop(0, big_total // 256, tile, 0)

    def mark_small(m):
        slot = m if kept > 1 else 0

        def block_body(b, carry):
            for step in range(STEPS):
                lanes = pl.ds(step % 2 * LANES, LANES)
                row = s.place[m, b + 1, pl.ds(step, 1), :]
                s.hot_small[slot, b, step // 2, :, lanes] = mark(row, 0)
            return carry

        lax.fori_loop(0, SMALLS, block_body, 0)

    place = me * 2 + own_f
    vector_row, vector_lane = lax.div(place, 8), lax.rem(place, 8) * 32

    def vector_place():
        lane = lax.broadcasted_iota(jnp.int32, (32, WIDTH), 1)
        element = lax.broadcasted_iota(jnp.int32, (32, WIDTH), 0)
        return jnp.where(lane == element + vector_lane, 1.0, 0.0)

    def own_row_of_eight():
        return lax.broadcasted_iota(jnp.int32, (8, WIDTH), 0) == vector_row

    def own_piece(layer):
        flat = s.projections[...].astype(F32)[layer : layer + 1]
        rows = [flat[:, i * WIDTH : (i + 1) * WIDTH] for i in range(CHUNK)]
        own = s.vectors[...][layer : layer + 1].astype(F32)
        own = nn(jnp.broadcast_to(own, (8, 32)).astype(BF16), vector_place().astype(BF16))
        rows.append(jnp.where(own_row_of_eight(), own, 0.0))
        s.table[4 + layer, pl.ds(own_piece_row, PIECE)] = jnp.concatenate(
            rows, axis=0
        ).astype(BF16)

    def chunks():
        for c in range(2):
            for x in range(2):
                for z in range(depth):
                    for y in range(2):
                        yield (
                            ((z * 2 + x) * 2 + c) * 2 + y,
                            (((c * 2 + x) * 2 + y) * depth + z) * PIECE,
                        )

    def load_layer(layer):
        if shared_weights:
            pieces = {
                chunk: s.table[4 + layer, pl.ds(at, PIECE)].astype(F32)
                for chunk, at in chunks()
            }
            s.weights[layer] = jnp.concatenate(
                [pieces[i][:CHUNK] for i in range(len(pieces))], axis=0
            ).astype(BF16)
            rows = pieces[0][CHUNK:]
            for i in range(1, len(pieces)):
                rows = rows + pieces[i][CHUNK:]
        else:
            rows = s.all_vectors[layer].astype(F32)
        for k in range(3):
            rows_k = pl.ds(k * WIDTH, WIDTH)
            s.weights_t[layer, rows_k] = jnp.transpose(s.weights[layer, rows_k])
        which = lax.broadcasted_iota(jnp.int32, (8, 512), 0)
        lane = lax.shift_right_logical(lax.broadcasted_iota(jnp.int32, (8, 512), 1), 7)
        chosen = jnp.where(which == lane, 1.0, 0.0).astype(BF16)
        wide = tn(rows.astype(BF16), chosen)
        for k in range(4):
            s.vecs[layer, k] = wide[:, k * 128 : (k + 1) * 128]

    def share(p, hidden):
        s.table[p, pl.ds(own_row, UNIT)] = hidden[:BIG]
        s.ext[p, pl.ds(RIM, SMALL)] = hidden[BIG:]

    def aim(p, layer, m, hidden):
        s.targets[p] = 0.5 * nt(s.weights_t[layer, pl.ds(WIDTH, WIDTH)], hidden)
        bias = s.vecs[layer, 1]
        s.residue[m] = nt(s.weights_t[layer, pl.ds(2 * WIDTH, WIDTH)], hidden) + jnp.concatenate(
            [bias, bias], axis=1
        )

    def spread(p, block):
        wide = s.targets[p, :, pl.ds((block // 2) * 128, 128)]
        odd = block % 2 == 1
        tile = jnp.where(upper_lanes() == odd, wide, pltpu.roll(wide, 64, 1))
        s.doubled[block] = tile

    def score(p, layer, block, pair, turned, hot):
        got = nn(turned[...], hot[pair])
        low = got.astype(BF16)
        for part in range(4):
            rows_of[block][p, 4 * pair + part] = low[:, part * 128 : (part + 1) * 128]
        for h in range(HEADS):
            rows = slice(h * HEAD_WIDTH, (h + 1) * HEAD_WIDTH)
            wanted = s.doubled[block, rows, :]
            attn = s.vecs[layer, 0, rows, :]
            for part in range(4):
                z = got[rows, part * 128 : (part + 1) * 128] + wanted
                lifted = z * (jnp.tanh(z) + 1.5)
                half = (part % 2) * 128
                s.scores[block, 2 * pair + part // 2, h : h + 1, half : half + 128] = jnp.sum(
                    lifted * attn, axis=0, keepdims=True
                )

    def halves_max(wide):
        tile = jnp.maximum(wide[:, :128], wide[:, 128:])
        tile = jnp.maximum(tile, pltpu.roll(tile, 64, 1))
        return jnp.concatenate([tile, tile], axis=1)

    def halves_sum(wide):
        tile = wide[:, :128] + wide[:, 128:]
        tile = tile + pltpu.roll(tile, 64, 1)
        return jnp.concatenate([tile, tile], axis=1)

    def softmax(p, m, block):
        used = [s.used[m, block, pl.ds(i, 1), :] for i in range(STEPS)]
        logits = [
            jnp.where(used[i] > 0, 0.8 * s.scores[block, i], -1e30) for i in range(STEPS)
        ]
        largest = halves_max(functools.reduce(jnp.maximum, logits))
        raised = [jnp.exp(logits[i] - largest) * used[i] for i in range(STEPS)]
        scale = 1.0 / halves_sum(functools.reduce(jnp.add, raised))
        for i in range(STEPS):
            s.shares[p, block, i] = raised[i] * scale

    def pass_messages(p, m, block):
        for h in range(HEADS):
            rows = slice(h * HEAD_WIDTH, (h + 1) * HEAD_WIDTH)
            total = jnp.zeros((HEAD_WIDTH, 128), F32)
            for step in range(STEPS):
                for half in range(2):
                    share = s.shares[p, block, step, h : h + 1, half * 128 : (half + 1) * 128]
                    share = share.astype(BF16).astype(F32)
                    total = total + share * rows_of[block][p, 2 * step + half, rows].astype(F32)
            s.message[m, block, rows, :] = total

    def sources(layer, rows):
        return (0.5 * nt(s.weights_t[layer, pl.ds(0, WIDTH)], rows)).astype(BF16)

    def smalls(p, layer, m, progress):
        finish(gather_rims(p))
        for b in range(SMALLS):
            s.turned_small[b] = sources(layer, s.ext[p, pl.ds(b * BIG, 256)])
            spread(p, b + 1)
        for b in range(SMALLS):
            if b == 2:
                progress()
            hot = s.hot_small.at[m if kept > 1 else 0, b]
            for pair in range(STEPS // 2):
                score(p, layer, b + 1, pair, s.turned_small.at[b], hot)
            softmax(p, m, b + 1)

    def big(p, layer, m):
        s.turned_big[...] = sources(layer, s.table[p])
        spread(p, 0)
        hot = s.hot_big.at[m if kept > 1 else 0]
        for pair in range(STEPS // 2):
            score(p, layer, 0, pair, s.turned_big, hot)
            if pair + 1 < BLOCKS:
                pass_messages(p, m, pair + 1)
        softmax(p, m, 0)
        pass_messages(p, m, 0)

    def normalise(p, layer, m):
        gain, shift = s.vecs[layer, 2], s.vecs[layer, 3]
        for t in range(2):
            lanes = slice(t * 128, (t + 1) * 128)
            total = join_halves(s.message[m, 2 * t], s.message[m, 2 * t + 1])
            y = 2.0 * total + s.residue[m, :, lanes]
            centred = y - jnp.sum(y, axis=0, keepdims=True) * (1.0 / WIDTH)
            spread_of = jnp.sum(centred * centred, axis=0, keepdims=True) * (1.0 / WIDTH)
            inverse = lax.rsqrt(spread_of + EPSILON)
            normed = centred * inverse
            shifted = normed * gain + shift
            s.normed[p, :, lanes] = normed
            s.inverse[p, 0:1, lanes] = inverse
            act = jnp.where(shifted > 0, shifted, jnp.exp(jnp.minimum(shifted, 0.0)) - 1.0)
            s.act[:, lanes] = act.astype(BF16)

        @pl.when(layer == 0)
        def _():
            s.hidden_t[m + 2] = s.act[...]
            hidden = jnp.transpose(s.act[...])
            share(m + 2, hidden)
            start(gather_rims(m + 2))
            start(gather_far(m + 2))
            aim(m + 2, 1, m, hidden)

        @pl.when(layer == 1)
        def _():
            s.layer_output[m] = jnp.transpose(s.act[...])

    def forward(layer, carry):
        def body(m, inner):
            p = 2 * layer + m
            if kept == 1:
                mark_small(m)
                mark_big(m)

            def progress():
                finish(gather_far(p))
                start(gather_core(p))

            smalls(p, layer, m, progress)
            if shared_weights:

                @pl.when(jnp.logical_and(layer == 0, m == 0))
                def _():
                    finish(gather_pieces_xy(1))
                    start(gather_core(5))

            finish(gather_core(p))
            big(p, layer, m)

            @pl.when(jnp.logical_and(layer == 0, m == 0))
            def _():
                if shared_weights:
                    finish(gather_core(5))
                load_layer(1)

            normalise(p, layer, m)
            return inner

        lax.fori_loop(0, MICRO, body, 0)
        return carry

    def through_norm(p, layer, m):
        gain, shift = s.vecs[layer, 2], s.vecs[layer, 3]
        upper = upper_lanes()
        for t in range(2):
            lanes = slice(t * 128, (t + 1) * 128)
            normed = s.normed[p, :, lanes]
            shifted = normed * gain + shift
            grad = s.grad_act[m, :, lanes] * jnp.where(
                shifted > 0, 1.0, jnp.exp(jnp.minimum(shifted, 0.0))
            )
            s.grad_vecs[layer, 2] = s.grad_vecs[layer, 2] + grad * normed
            s.grad_vecs[layer, 3] = s.grad_vecs[layer, 3] + grad
            grad = grad * gain
            first = jnp.sum(grad, axis=0, keepdims=True) * (1.0 / WIDTH)
            second = jnp.sum(grad * normed, axis=0, keepdims=True) * (1.0 / WIDTH)
            grad = s.inverse[p, 0:1, lanes] * (grad - first - normed * second)
            s.grad_vecs[layer, 1] = s.grad_vecs[layer, 1] + grad
            s.grad_out_t[p, :, lanes] = grad.astype(BF16)
            grad = grad.astype(BF16).astype(F32)
            other = pltpu.roll(grad, 64, 1)
            s.grad_out[m, 2 * t] = jnp.where(upper, other, grad)
            s.grad_out[m, 2 * t + 1] = jnp.where(upper, grad, other)

    def share_grads(p, m, block, step):
        for h in range(HEADS):
            rows = slice(h * HEAD_WIDTH, (h + 1) * HEAD_WIDTH)
            grad = s.grad_out[m, block, rows, :]
            for half in range(2):
                product = rows_of[block][p, 2 * step + half, rows].astype(F32) * grad
                s.share_grad[m, block, step, h : h + 1, half * 128 : (half + 1) * 128] = (
                    jnp.sum(product, axis=0, keepdims=True)
                )

    def logit_grads(p, m, block):
        shares = [s.shares[p, block, i] for i in range(STEPS)]
        grads = [s.share_grad[m, block, i] for i in range(STEPS)]
        total = halves_sum(functools.reduce(jnp.add, [a * b for a, b in zip(shares, grads)]))
        for i in range(STEPS):
            s.share_grad[m, block, i] = 0.8 * shares[i] * (grads[i] - total)

    def make_terms(p, layer, m, block, pair):
        for h in range(HEADS):
            rows = slice(h * HEAD_WIDTH, (h + 1) * HEAD_WIDTH)
            wanted = s.doubled[block, rows, :]
            attn = s.vecs[layer, 0, rows, :]
            grad = s.grad_out[m, block, rows, :]
            target_sum = s.message[m, block, rows, :]
            attn_sum = s.grad_vecs[layer, 0, rows, :]
            for part in range(4):
                step, half = 2 * pair + part // 2, (part % 2) * 128
                z = rows_of[block][p, 4 * pair + part, rows].astype(F32) + wanted
                t = jnp.tanh(z)
                w = t + 1.5
                logit_grad = s.share_grad[m, block, step, h : h + 1, half : half + 128]
                attn_sum = attn_sum + logit_grad * (z * w)
                slope = logit_grad * (w + z * (1.0 - t * t))
                target_sum = target_sum + slope
                share = s.shares[p, block, step, h : h + 1, half : half + 128]
                share = share.astype(BF16).astype(F32)
                terms[pair % 2][rows, part * 128 : (part + 1) * 128] = (
                    share * grad + attn * slope
                ).astype(BF16)
            s.message[m, block, rows, :] = target_sum
            s.grad_vecs[layer, 0, rows, :] = attn_sum

    def all_share_grads(p, m, block):
        for step in range(STEPS):
            share_grads(p, m, block, step)
        logit_grads(p, m, block)

    def big_back(p, layer, m):
        spread(p, 0)
        s.message[m] = jnp.zeros((BLOCKS, WIDTH, 128), F32)
        all_share_grads(p, m, 0)
        for pair in range(STEPS // 2):
            make_terms(p, layer, m, 0, pair)
            added = nt(s.hot_big[m if kept > 1 else 0, pair], terms[pair % 2][...])
            if pair == 0:
                s.part_sum[...] = added
            elif pair + 1 < STEPS // 2:
                s.part_sum[...] = s.part_sum[...] + added
            else:
                s.table[2 + m] = (s.part_sum[...] + added).astype(BF16)

    def smalls_back(p, layer, m, progress):
        for b in range(SMALLS):
            spread(p, b + 1)
        s.grad_ext[...] = jnp.zeros_like(s.grad_ext)
        all_share_grads(p, m, 1)
        for b in range(SMALLS):
            if b == 1:
                progress()
            if b + 1 < SMALLS:
                all_share_grads(p, m, b + 2)
            here = pl.ds(b * BIG, 256)
            for pair in range(STEPS // 2):
                make_terms(p, layer, m, b + 1, pair)
                hot = s.hot_small[m if kept > 1 else 0, b, pair]
                s.grad_ext[here] = s.grad_ext[here] + nt(hot, terms[pair % 2][...])
        s.send_rim[p, 0] = s.grad_ext[pl.ds(0, RIM)].astype(BF16)
        s.send_rim[p, 1] = s.grad_ext[pl.ds(RIM + SMALL, RIM)].astype(BF16)
        start(reduce_rims(p))
        s.grad_small[m] = s.grad_ext[pl.ds(RIM, SMALL)]
        attn = s.vecs[layer, 0]
        for t in range(2):
            lanes = slice(t * 128, (t + 1) * 128)
            total = join_halves(s.message[m, 2 * t], s.message[m, 2 * t + 1])
            s.grad_targets_t[p, :, lanes] = (attn * total).astype(BF16)

    def finalise_sources(p, m):
        unit = reduced_unit(p)
        finish(reduce_rims(p))
        low = s.grad_small[m, pl.ds(0, RIM)] + s.land_rim[p, 0].astype(F32)
        high = s.grad_small[m, pl.ds(RIM, RIM)] + s.land_rim[p, 1].astype(F32)
        rows = jnp.concatenate([unit, low, high], axis=0)
        s.grad_sources_t[p] = jnp.transpose(rows.astype(BF16))

    def finalise_hidden(p, layer, m):
        s.grad_act[m] = (
            nn(s.weights[layer, pl.ds(0, WIDTH)], s.grad_sources_t[p])
            + nn(s.weights[layer, pl.ds(WIDTH, WIDTH)], s.grad_targets_t[p])
            + nn(s.weights[layer, pl.ds(2 * WIDTH, WIDTH)], s.grad_out_t[p])
        )

    def finalise(p, layer, m):
        finalise_sources(p, m)
        finalise_hidden(p, layer, m)

    def weight_grads(layer):
        for k, grads in enumerate((s.grad_sources_t, s.grad_targets_t, s.grad_out_t)):
            total = nt(s.hidden_t[2 * layer], grads[2 * layer])
            if layer == 0 and k == 0:
                total = total + s.head_weights[...] + tn(s.ext[1], s.grad_ext[...].astype(BF16))
            else:
                total = total + nt(s.hidden_t[2 * layer + 1], grads[2 * layer + 1])
            if shared_weights:
                s.grad_weights[pl.ds(k * WIDTH, WIDTH)] = total
            else:
                s.weight_sums[layer, pl.ds(k * WIDTH, WIDTH)] = total
        vector_rows = jnp.zeros((8, WIDTH), F32)
        for k in range(4):
            chosen = jnp.where(
                lax.broadcasted_iota(jnp.int32, (8, 128), 0) == k, 2.0 if k == 0 else 1.0, 0.0
            ).astype(F32)
            vector_rows = vector_rows + nt(
                chosen, s.grad_vecs[layer, k], precision=lax.Precision.HIGHEST
            )
        if not shared_weights:
            s.vector_sums[layer] = vector_rows
            return
        for chunk, at in chunks():
            s.table[4 + layer, pl.ds(at, PIECE)] = jnp.concatenate(
                [s.grad_weights[pl.ds(chunk * CHUNK, CHUNK)], vector_rows], axis=0
            ).astype(BF16)
        start(reduce_core(4 + layer))

    def weights_on(layer):
        add_core(4 + layer)
        start(reduce_pieces(layer))

    def weights_done(layer):
        finish(reduce_pieces(layer))
        total = s.table[4 + layer, pl.ds(own_piece_row, PIECE)].astype(F32)
        for k in range(2 * len(far) + 1):
            total = total + s.land_piece[layer, k].astype(F32)
        s.weight_sums[layer : layer + 1, :] = jnp.concatenate(
            [total[i : i + 1] for i in range(CHUNK)], axis=1
        )
        own = jnp.where(own_row_of_eight(), total[CHUNK:], 0.0)
        own = jnp.sum(own, axis=0, keepdims=True)
        own = nt(
            jnp.broadcast_to(own, (8, WIDTH)), vector_place(), precision=lax.Precision.HIGHEST
        )
        s.vector_sums[layer : layer + 1, :] = own[:1]

    def backward(i, carry):
        layer = 1 - i
        first, second = 2 * layer, 2 * layer + 1

        def body(m, inner):
            if kept == 1:
                mark_big(m)
                mark_small(m)

            @pl.when(jnp.logical_and(i == 1, m == 0))
            def _():
                finalise(2, 1, 0)

            through_norm(first + m, layer, m)
            big_back(first + m, layer, m)

            @pl.when(jnp.logical_and(i == 1, m == 1))
            def _():
                s.head_weights[...] = tn(s.table[1], s.table[3])

            start(reduce_core(first + m))

            @pl.when(jnp.logical_and(i == 1, m == 0))
            def _():
                finalise(3, 1, 1)
                weight_grads(1)

            def progress():
                reduce_on(first + m)
                if shared_weights:

                    @pl.when(jnp.logical_and(i == 1, m == 0))
                    def _():
                        weights_on(1)

            smalls_back(first + m, layer, m, progress)
            return inner

        lax.fori_loop(0, MICRO, body, 0)
        return carry

    barrier = pltpu.get_barrier_semaphore()
    partners = [dict(blk=peer) for peer, _ in far]
    if shared_weights:
        partners = [dict(blk=peer, fsdp=f) for peer, f, _ in all_far()]
    partners += [dict(blk=d) for d in (sibling, before, after)]
    for partner in partners:
        pl.semaphore_signal(barrier, inc=1, device_id=partner, device_id_type=MESH)
    brought = ("features", "neighbours", "slot_mask", "out_cotangent")
    for k, name in enumerate(brought):
        start(bring(k, name))
    if shared_weights:
        for layer in range(LAYERS):
            own_piece(layer)
    pl.semaphore_wait(barrier, len(partners))

    if shared_weights:
        for layer in range(LAYERS):
            start(gather_pieces_z(layer))
    finish(bring(0, "features"))
    for m in range(MICRO):
        share(m, s.features[m])
        start(gather_rims(m))
    for k in (1, 2, 3):
        finish(bring(k, brought[k]))
    for m in range(MICRO):
        prepare(m)
    if not shared_weights:
        start(gather_far(0))
        start(gather_far(1))
    s.scores[...] = jnp.zeros_like(s.scores)
    s.share_grad[...] = jnp.zeros_like(s.share_grad)
    s.grad_vecs[...] = jnp.zeros_like(s.grad_vecs)
    if kept > 1:
        mark_small(0)
        mark_small(1)
    if shared_weights:
        finish(gather_pieces_z(0))
        start(gather_pieces_xy(0))
        finish(gather_pieces_z(1))
        start(gather_far(0))
    if kept > 1:
        mark_big(0)
        mark_big(1)
    if shared_weights:
        finish(gather_pieces_xy(0))
        start(gather_core(4))
        start(gather_pieces_xy(1))
        start(gather_far(1))
        finish(gather_core(4))
    load_layer(0)
    for m in range(MICRO):
        aim(m, 0, m, s.features[m])
    lax.fori_loop(0, LAYERS, forward, 0)
    start(hand_out(4, "layer_output"))
    lax.fori_loop(0, LAYERS, backward, 0)
    finalise_sources(0, 0)
    weight_grads(0)
    finalise_hidden(0, 0, 0)
    if shared_weights:
        weights_on(0)
    s.input_gradient[0] = jnp.transpose(s.grad_act[0])
    start(hand_out(5, "input_gradient", 0))
    finalise(1, 0, 1)
    s.input_gradient[1] = jnp.transpose(s.grad_act[1])
    start(hand_out(6, "input_gradient", 1))
    if shared_weights:
        weights_done(1)
        weights_done(0)
    finish(hand_out(4, "layer_output"))
    for m in range(MICRO):
        finish(hand_out(5 + m, "input_gradient", m))


def hand_over(*refs):
    *arrays, sems = refs
    count = len(arrays) // 2
    copies = [
        pltpu.make_async_copy(arrays[k], arrays[count + k], sems.at[k]) for k in range(count)
    ]
    for copy in copies:
        copy.start()
    for copy in copies:
        copy.wait()


def per_device(
    depth, fsdp_count, features, neighbours, slot_mask, projections, vectors, out_cotangent
):
    layers, weight_chunk = projections.shape
    shared_weights = fsdp_count == 2 and weight_chunk == CHUNK * WIDTH and depth == 4
    inputs = dict(
        features_hbm=features[:, 0],
        neighbours_hbm=jnp.swapaxes(neighbours[:, 0], 1, 2),
        slot_mask_hbm=jnp.swapaxes(slot_mask[:, 0], 1, 2),
        out_cotangent_hbm=out_cotangent[:, 0],
    )
    if shared_weights:
        inputs["projections"] = projections
        inputs["vectors"] = vectors
        weight_shape, vector_shape = projections.shape, vectors.shape
    else:
        axes = ("blk", "fsdp")
        gathered = lax.all_gather(projections, axes, axis=1, tiled=True)
        inputs["weights"] = gathered.reshape(layers, 3 * WIDTH, WIDTH)
        gathered = lax.all_gather(vectors, axes, axis=1, tiled=True)
        inputs["all_vectors"] = jnp.pad(
            gathered.reshape(layers, 4, WIDTH), ((0, 0), (0, 4), (0, 0))
        )
        weight_shape, vector_shape = (layers, 3 * WIDTH, WIDTH), (layers, 8, WIDTH)
    outputs = dict(
        layer_output_hbm=jax.ShapeDtypeStruct((MICRO, NODES, WIDTH), BF16),
        input_gradient_hbm=jax.ShapeDtypeStruct((MICRO, NODES, WIDTH), F32),
        weight_sums=jax.ShapeDtypeStruct(weight_shape, F32),
        vector_sums=jax.ShapeDtypeStruct(vector_shape, F32),
    )
    scratch = scratch_plan(depth, shared_weights)
    in_vmem = pl.BlockSpec(memory_space=pltpu.VMEM)
    in_hbm = pl.BlockSpec(memory_space=pl.ANY)
    results = pl.pallas_call(
        functools.partial(
            step_kernel, depth, shared_weights, [*inputs, *outputs, *scratch]
        ),
        out_shape=list(outputs.values()),
        in_specs=[in_hbm if name.endswith("_hbm") else in_vmem for name in inputs],
        out_specs=[in_hbm if name.endswith("_hbm") else in_vmem for name in outputs],
        scratch_shapes=list(scratch.values()),
        compiler_params=pltpu.CompilerParams(
            collective_id=0, has_side_effects=True, vmem_limit_bytes=63 * 1024 * 1024
        ),
    )(*inputs.values())
    if shared_weights:
        results = pl.pallas_call(
            hand_over,
            out_shape=list(outputs.values()),
            in_specs=[in_hbm] * len(outputs),
            out_specs=[in_vmem] * len(outputs),
            scratch_shapes=[pltpu.SemaphoreType.DMA((len(outputs),))],
        )(*results)
    layer_output, input_gradient, weight_sums, vector_sums = results
    if not shared_weights:
        axes = ("blk", "fsdp")
        weight_sums = lax.psum_scatter(
            weight_sums.reshape(layers, -1), axes, scatter_dimension=1, tiled=True
        )
        vector_sums = lax.psum_scatter(
            vector_sums[:, :4].reshape(layers, -1), axes, scatter_dimension=1, tiled=True
        )
    return layer_output[:, None], input_gradient[:, None], weight_sums, vector_sums


def solution(mesh):
    return jax.shard_map(
        functools.partial(per_device, mesh.shape["blk"] // 4, mesh.shape["fsdp"]),
        mesh=mesh,
        in_specs=(
            P(None, "fsdp", "blk", None),
            P(None, "fsdp", "blk", None),
            P(None, "fsdp", "blk", None),
            P(None, ("blk", "fsdp")),
            P(None, ("blk", "fsdp")),
            P(None, "fsdp", "blk", None),
        ),
        out_specs=(
            P(None, "fsdp", "blk", None),
            P(None, "fsdp", "blk", None),
            P(None, ("blk", "fsdp")),
            P(None, ("blk", "fsdp")),
        ),
        check_vma=False,
    )
```

```python
import functools
import types

import jax
import jax.numpy as jnp
from jax import lax
from jax.experimental import pallas as pl
from jax.experimental.pallas import tpu as pltpu
from jax.sharding import PartitionSpec as P

HEADS = 4
MICRO = 2
LAYERS = 2
SLOTS = 32
WIDTH = 256
HEAD_WIDTH = WIDTH // HEADS
NODES = 256
BIG = 64
SMALL = NODES - BIG
RIM = 96
EXT = SMALL + 2 * RIM
BLOCKS = NODES // BIG
SMALLS = BLOCKS - 1
PAIRS = BIG * SLOTS
STEPS = 8
LANES = PAIRS // STEPS
UNIT = BIG
CHUNK = 24
PIECE = UNIT // 2
EPSILON = 1e-05
F32 = jnp.float32
BF16 = jnp.bfloat16
MESH = pl.DeviceIdType.MESH


def nn(left, right):
    return lax.dot_general(
        left, right, (((1,), (0,)), ((), ())), preferred_element_type=F32
    )


def nt(left, right, precision=None):
    return lax.dot_general(
        left, right, (((1,), (1,)), ((), ())), preferred_element_type=F32, precision=precision
    )


def tn(left, right):
    return lax.dot_general(
        left, right, (((0,), (0,)), ((), ())), preferred_element_type=F32
    )


def upper_lanes():
    return lax.broadcasted_iota(jnp.int32, (WIDTH, 128), 1) >= 64


def join_halves(even, odd):
    upper = upper_lanes()
    return jnp.where(upper, odd, even) + pltpu.roll(jnp.where(upper, even, odd), 64, 1)


def scratch_plan(depth, shared_weights):
    big_total = 4 * depth * UNIT
    tables = 4 + (LAYERS if shared_weights else 0)
    copies = MICRO if depth <= 4 else 1
    peers = 2 * depth - 1
    vm = pltpu.VMEM
    plan = dict(
        features=vm((MICRO, NODES, WIDTH), BF16),
        neighbours=vm((MICRO, SLOTS, NODES), jnp.int32),
        slot_mask=vm((MICRO, SLOTS, NODES), jnp.int32),
        out_cotangent=vm((MICRO, NODES, WIDTH), BF16),
        layer_output=vm((MICRO, NODES, WIDTH), BF16),
        input_gradient=vm((MICRO, NODES, WIDTH), F32),
        own_sems=pltpu.SemaphoreType.DMA((7,)),
        hot_big=vm((copies, STEPS // 2, big_total, 2 * LANES), BF16),
        hot_small=vm((copies, SMALLS, STEPS // 2, 256, 2 * LANES), BF16),
        place=vm((MICRO, BLOCKS, STEPS, LANES), jnp.int32),
        used=vm((MICRO, BLOCKS, STEPS, LANES), F32),
        rows_0=vm((4, 2 * STEPS, WIDTH, 128), BF16),
        rows_1=vm((4, 2 * STEPS, WIDTH, 128), BF16),
        rows_2=vm((4, 2 * STEPS, WIDTH, 128), BF16),
        rows_3=vm((4, 2 * STEPS, WIDTH, 128), BF16),
        shares=vm((4, BLOCKS, STEPS, 8, LANES), F32),
        table=vm((tables, big_total, WIDTH), BF16),
        ext=vm((4, EXT, WIDTH), BF16),
        turned_big=vm((WIDTH, big_total), BF16),
        turned_small=vm((SMALLS, WIDTH, 256), BF16),
        hidden_t=vm((4, WIDTH, NODES), BF16),
        weights_t=vm((LAYERS, 3 * WIDTH, WIDTH), BF16),
        vecs=vm((LAYERS, 4, WIDTH, 128), F32),
        targets=vm((4, WIDTH, NODES), F32),
        residue=vm((MICRO, WIDTH, NODES), F32),
        doubled=vm((BLOCKS, WIDTH, 128), F32),
        scores=vm((BLOCKS, STEPS, 8, LANES), F32),
        low_shares=vm((BLOCKS, STEPS, 8, LANES), F32),
        share_grad=vm((BLOCKS, STEPS, 8, LANES), F32),
        message=vm((MICRO, BLOCKS, WIDTH, 128), F32),
        normed=vm((4, WIDTH, NODES), F32),
        inverse=vm((4, 8, NODES), F32),
        act=vm((WIDTH, NODES), BF16),
        grad_act=vm((MICRO, WIDTH, NODES), F32),
        grad_out=vm((MICRO, BLOCKS, WIDTH, 128), F32),
        grad_out_t=vm((4, WIDTH, NODES), BF16),
        grad_targets_t=vm((4, WIDTH, NODES), BF16),
        grad_sources_t=vm((4, WIDTH, NODES), BF16),
        terms_0=vm((WIDTH, 2 * LANES), BF16),
        terms_1=vm((WIDTH, 2 * LANES), BF16),
        part_sum=vm((big_total, WIDTH), F32),
        grad_ext=vm((EXT, WIDTH), F32),
        head_weights=vm((WIDTH, WIDTH), F32),
        grad_small=vm((MICRO, SMALL, WIDTH), F32),
        grad_vecs=vm((LAYERS, 4, WIDTH, 128), F32),
        land_core=vm((tables, big_total // 2, WIDTH), BF16),
        land=vm((4, peers, UNIT, WIDTH), BF16),
        land_rim=vm((4, 2, RIM, WIDTH), BF16),
        send_rim=vm((4, 2, RIM, WIDTH), BF16),
        gather_send=pltpu.SemaphoreType.DMA((tables, 18)),
        gather_recv=pltpu.SemaphoreType.DMA((tables, 18)),
        reduce_send=pltpu.SemaphoreType.DMA((tables, 18)),
        reduce_recv=pltpu.SemaphoreType.DMA((tables, 18)),
    )
    if shared_weights:
        plan.update(
            weights=vm((LAYERS, 3 * WIDTH, WIDTH), BF16),
            grad_weights=vm((3 * WIDTH, WIDTH), F32),
            land_piece=vm((LAYERS, 2 * peers + 1, PIECE, WIDTH), BF16),
        )
    return plan


def step_kernel(depth, shared_weights, names, *refs):
    s = types.SimpleNamespace(**dict(zip(names, refs, strict=True)))
    big_total = 4 * depth * UNIT
    kept = s.hot_big.shape[0]
    me = lax.axis_index("blk")
    core = lax.rem(me, 2)
    along_x = lax.rem(lax.div(me, 2), 2)
    along_z = lax.div(me, 4)
    own_f = lax.axis_index("fsdp")
    block_count = 4 * depth
    before = lax.rem(me + block_count - 1, block_count)
    after = lax.rem(me + 1, block_count)
    sibling = along_z * 4 + along_x * 2 + (1 - core)

    def unit_row(z, x, c):
        return pl.multiple_of(((c * 2 + x) * depth + z) * UNIT, UNIT)

    own_row = unit_row(along_z, along_x, core)
    rows_of = (s.rows_0, s.rows_1, s.rows_2, s.rows_3)
    terms = (s.terms_0, s.terms_1)
    far = []
    for dz in sorted(range(depth), reverse=True):
        for dx in (1, 0):
            if dz or dx:
                z, x = lax.rem(along_z + dz, depth), lax.rem(along_x + dx, 2)
                far.append((z * 4 + x * 2 + core, unit_row(z, x, core)))

    def remote(src, dst, sems, slot, **where):
        send, recv = sems
        return pltpu.make_async_remote_copy(
            src_ref=src,
            dst_ref=dst,
            send_sem=send.at[slot],
            recv_sem=recv.at[slot],
            device_id=where,
            device_id_type=MESH,
        )

    gather_sems = (s.gather_send, s.gather_recv)
    reduce_sems = (s.reduce_send, s.reduce_recv)
    core_slot, low_slot, high_slot = 15, 16, 17

    def half_rows(c):
        return pl.ds(unit_row(0, 0, c), 2 * depth * UNIT)

    def piece_row(z, x, c, f):
        return pl.multiple_of((((c * 2 + x) * 2 + f) * depth + z) * PIECE, PIECE)

    own_piece_row = piece_row(along_z, along_x, core, own_f)

    def gather_far(p):
        unit = s.table.at[p, pl.ds(own_row, UNIT)]
        return [
            remote(unit, unit, gather_sems, (p, k), blk=peer)
            for k, (peer, _) in enumerate(far)
        ]

    def all_far():
        found = []
        for dz in sorted(range(depth), reverse=True):
            for dx in (1, 0):
                for f in (1 - own_f, own_f):
                    if dz or dx or f is not own_f:
                        z, x = lax.rem(along_z + dz, depth), lax.rem(along_x + dx, 2)
                        found.append((z * 4 + x * 2 + core, f, piece_row(z, x, core, f)))
        return found

    def gather_pieces_z(layer):
        piece = s.table.at[4 + layer, pl.ds(own_piece_row, PIECE)]
        peers = [
            lax.rem(along_z + dz, depth) * 4 + along_x * 2 + core for dz in range(1, depth)
        ]
        return [
            remote(piece, piece, gather_sems, (4 + layer, k), blk=peer)
            for k, peer in enumerate(reversed(peers))
        ]

    def gather_pieces_xy(layer):
        column = piece_row(0, along_x, core, own_f)
        piece = s.table.at[4 + layer, pl.ds(column, depth * PIECE)]
        other = along_z * 4 + (1 - along_x) * 2 + core
        peers = [(other, 1 - own_f), (other, own_f), (me, 1 - own_f)]
        return [
            remote(piece, piece, gather_sems, (4 + layer, 8 + k), blk=peer, fsdp=f)
            for k, (peer, f) in enumerate(peers)
        ]

    def gather_core(q):
        half = s.table.at[q, half_rows(core)]
        return [remote(half, half, gather_sems, (q, core_slot), blk=sibling)]

    def gather_rims(p):
        low = remote(
            s.ext.at[p, pl.ds(RIM, RIM)],
            s.ext.at[p, pl.ds(RIM + SMALL, RIM)],
            gather_sems,
            (p, low_slot),
            blk=before,
        )
        high = remote(
            s.ext.at[p, pl.ds(SMALL, RIM)],
            s.ext.at[p, pl.ds(0, RIM)],
            gather_sems,
            (p, high_slot),
            blk=after,
        )
        return [low, high]

    def part_of(q):
        return q if isinstance(q, int) and q >= 4 else 2 + lax.rem(q, 2)

    def reduce_core(q):
        return [
            remote(
                s.table.at[part_of(q), half_rows(1 - core)],
                s.land_core.at[q],
                reduce_sems,
                (q, core_slot),
                blk=sibling,
            )
        ]

    def reduce_far(p):
        return [
            remote(
                s.table.at[part_of(p), pl.ds(row, UNIT)],
                s.land.at[p, k],
                reduce_sems,
                (p, k),
                blk=peer,
            )
            for k, (peer, row) in enumerate(far)
        ]

    def reduce_pieces(layer):
        return [
            remote(
                s.table.at[4 + layer, pl.ds(row, PIECE)],
                s.land_piece.at[layer, k],
                reduce_sems,
                (4 + layer, k),
                blk=peer,
                fsdp=f,
            )
            for k, (peer, f, row) in enumerate(all_far())
        ]

    def reduce_rims(p):
        low = remote(
            s.send_rim.at[p, 0], s.land_rim.at[p, 1], reduce_sems, (p, low_slot), blk=before
        )
        high = remote(
            s.send_rim.at[p, 1], s.land_rim.at[p, 0], reduce_sems, (p, high_slot), blk=after
        )
        return [low, high]

    def bring(k, name):
        return [
            pltpu.make_async_copy(getattr(s, name + "_hbm"), getattr(s, name), s.own_sems.at[k])
        ]

    def hand_out(k, name, m=None):
        kept_ref, out_ref = getattr(s, name), getattr(s, name + "_hbm")
        if m is not None:
            kept_ref, out_ref = kept_ref.at[m], out_ref.at[m]
        return [pltpu.make_async_copy(kept_ref, out_ref, s.own_sems.at[k])]

    def start(copies):
        for copy in copies:
            copy.start()

    def finish(copies):
        for copy in copies:
            copy.wait()

    def add_core(q):
        finish(reduce_core(q))
        first = unit_row(0, 0, core)
        at = part_of(q)

        def body(i, carry):
            here = pl.ds(pl.multiple_of(first + i * UNIT, UNIT), UNIT)
            there = pl.ds(pl.multiple_of(i * UNIT, UNIT), UNIT)
            s.table[at, here] = (
                s.table[at, here].astype(F32) + s.land_core[q, there].astype(F32)
            ).astype(BF16)
            return carry

        lax.fori_loop(0, 2 * depth, body, 0)

    def reduce_on(p):
        add_core(p)
        start(reduce_far(p))

    def reduced_unit(p):
        finish(reduce_far(p))
        total = s.table[part_of(p), pl.ds(own_row, UNIT)].astype(F32)
        for k in range(len(far)):
            total = total + s.land[p, k].astype(F32)
        return total

    def prepare(m):
        def compact(rows, block):
            part = rows[:, block * BIG : (block + 1) * BIG]
            tile = jnp.concatenate([part[:16], part[16:]], axis=1)
            return jnp.concatenate([tile[:8], tile[8:]], axis=1)

        picked = s.neighbours[m]
        usable = s.slot_mask[m]
        device = lax.shift_right_logical(picked, 8)
        offset = jnp.bitwise_and(picked, 255)
        z = lax.shift_right_logical(device, 2)
        x = jnp.bitwise_and(lax.shift_right_logical(device, 1), 1)
        c = jnp.bitwise_and(device, 1)
        big_place = ((c * 2 + x) * depth + z) * UNIT + offset
        small_place = (device - me) * SMALL + (offset - BIG)
        for block in range(BLOCKS):
            if block == 0:
                s.place[m, 0] = compact(big_place, 0)
            else:
                s.place[m, block] = compact(small_place + (RIM - (block - 1) * BIG), block)
            s.used[m, block] = compact(usable, block).astype(F32)
        s.hidden_t[m] = jnp.transpose(s.features[m])
        s.grad_act[m] = jnp.transpose(s.out_cotangent[m].astype(F32))

    def mark(row, least):
        tile = lax.broadcasted_iota(jnp.int32, (256, LANES), 0)
        return jnp.where(tile == row - least, 1.0, 0.0).astype(BF16)

    def lanes_of(step):
        return pl.ds(pl.multiple_of(step * LANES, LANES), LANES)

    def mark_big(m):
        slot = m if kept > 1 else 0

        def tile(w, carry):
            here = pl.ds(pl.multiple_of(w * 256, 256), 256)
            for step in range(STEPS):
                lanes = pl.ds(step % 2 * LANES, LANES)
                row = s.place[m, 0, pl.ds(step, 1), :]
                s.hot_big[slot, step // 2, here, lanes] = mark(row, w * 256)
            return carry

        lax.fori_loop(0, big_total // 256, tile, 0)

    def mark_small(m):
        slot = m if kept > 1 else 0

        def block_body(b, carry):
            for step in range(STEPS):
                lanes = pl.ds(step % 2 * LANES, LANES)
                row = s.place[m, b + 1, pl.ds(step, 1), :]
                s.hot_small[slot, b, step // 2, :, lanes] = mark(row, 0)
            return carry

        lax.fori_loop(0, SMALLS, block_body, 0)

    place = me * 2 + own_f
    vector_row, vector_lane = lax.div(place, 8), lax.rem(place, 8) * 32

    def vector_place():
        lane = lax.broadcasted_iota(jnp.int32, (32, WIDTH), 1)
        element = lax.broadcasted_iota(jnp.int32, (32, WIDTH), 0)
        return jnp.where(lane == element + vector_lane, 1.0, 0.0)

    def own_row_of_eight():
        return lax.broadcasted_iota(jnp.int32, (8, WIDTH), 0) == vector_row

    def own_piece(layer):
        flat = s.projections[...].astype(F32)[layer : layer + 1]
        rows = [flat[:, i * WIDTH : (i + 1) * WIDTH] for i in range(CHUNK)]
        own = s.vectors[...][layer : layer + 1].astype(F32)
        own = nn(jnp.broadcast_to(own, (8, 32)).astype(BF16), vector_place().astype(BF16))
        rows.append(jnp.where(own_row_of_eight(), own, 0.0))
        s.table[4 + layer, pl.ds(own_piece_row, PIECE)] = jnp.concatenate(
            rows, axis=0
        ).astype(BF16)

    def chunks():
        for c in range(2):
            for x in range(2):
                for z in range(depth):
                    for y in range(2):
                        yield (
                            ((z * 2 + x) * 2 + c) * 2 + y,
                            (((c * 2 + x) * 2 + y) * depth + z) * PIECE,
                        )

    def load_layer(layer):
        if shared_weights:
            pieces = {
                chunk: s.table[4 + layer, pl.ds(at, PIECE)].astype(F32)
                for chunk, at in chunks()
            }
            s.weights[layer] = jnp.concatenate(
                [pieces[i][:CHUNK] for i in range(len(pieces))], axis=0
            ).astype(BF16)
            rows = pieces[0][CHUNK:]
            for i in range(1, len(pieces)):
                rows = rows + pieces[i][CHUNK:]
        else:
            rows = s.all_vectors[layer].astype(F32)
        for k in range(3):
            rows_k = pl.ds(k * WIDTH, WIDTH)
            s.weights_t[layer, rows_k] = jnp.transpose(s.weights[layer, rows_k])
        which = lax.broadcasted_iota(jnp.int32, (8, 512), 0)
        lane = lax.shift_right_logical(lax.broadcasted_iota(jnp.int32, (8, 512), 1), 7)
        chosen = jnp.where(which == lane, 1.0, 0.0).astype(BF16)
        wide = tn(rows.astype(BF16), chosen)
        for k in range(4):
            s.vecs[layer, k] = wide[:, k * 128 : (k + 1) * 128]

    def share(p, hidden):
        s.table[p, pl.ds(own_row, UNIT)] = hidden[:BIG]
        s.ext[p, pl.ds(RIM, SMALL)] = hidden[BIG:]

    def aim(p, layer, m, hidden):
        s.targets[p] = 0.5 * nt(s.weights_t[layer, pl.ds(WIDTH, WIDTH)], hidden)
        bias = s.vecs[layer, 1]
        s.residue[m] = nt(s.weights_t[layer, pl.ds(2 * WIDTH, WIDTH)], hidden) + jnp.concatenate(
            [bias, bias], axis=1
        )

    def spread(p, block):
        wide = s.targets[p, :, pl.ds((block // 2) * 128, 128)]
        odd = block % 2 == 1
        tile = jnp.where(upper_lanes() == odd, wide, pltpu.roll(wide, 64, 1))
        s.doubled[block] = tile

    def score(p, layer, block, pair, turned, hot):
        got = nn(turned[...], hot[pair])
        low = got.astype(BF16)
        for part in range(4):
            rows_of[block][p, 4 * pair + part] = low[:, part * 128 : (part + 1) * 128]
        for h in range(HEADS):
            rows = slice(h * HEAD_WIDTH, (h + 1) * HEAD_WIDTH)
            wanted = s.doubled[block, rows, :]
            attn = s.vecs[layer, 0, rows, :]
            for part in range(4):
                z = got[rows, part * 128 : (part + 1) * 128] + wanted
                lifted = z * (jnp.tanh(z) + 1.5)
                half = (part % 2) * 128
                s.scores[block, 2 * pair + part // 2, h : h + 1, half : half + 128] = jnp.sum(
                    lifted * attn, axis=0, keepdims=True
                )

    def halves_max(wide):
        tile = jnp.maximum(wide[:, :128], wide[:, 128:])
        tile = jnp.maximum(tile, pltpu.roll(tile, 64, 1))
        return jnp.concatenate([tile, tile], axis=1)

    def halves_sum(wide):
        tile = wide[:, :128] + wide[:, 128:]
        tile = tile + pltpu.roll(tile, 64, 1)
        return jnp.concatenate([tile, tile], axis=1)

    def softmax(p, m, block):
        used = [s.used[m, block, pl.ds(i, 1), :] for i in range(STEPS)]
        logits = [
            jnp.where(used[i] > 0, 0.8 * s.scores[block, i], -1e30) for i in range(STEPS)
        ]
        largest = halves_max(functools.reduce(jnp.maximum, logits))
        raised = [jnp.exp(logits[i] - largest) * used[i] for i in range(STEPS)]
        scale = 1.0 / halves_sum(functools.reduce(jnp.add, raised))
        for i in range(STEPS):
            share = raised[i] * scale
            s.shares[p, block, i] = share
            s.low_shares[block, i] = share.astype(BF16).astype(F32)

    def pass_messages(p, m, block):
        for h in range(HEADS):
            rows = slice(h * HEAD_WIDTH, (h + 1) * HEAD_WIDTH)
            total = jnp.zeros((HEAD_WIDTH, 128), F32)
            for step in range(STEPS):
                for half in range(2):
                    share = s.low_shares[block, step, h : h + 1, half * 128 : (half + 1) * 128]
                    total = total + share * rows_of[block][p, 2 * step + half, rows].astype(F32)
            s.message[m, block, rows, :] = total

    def sources(layer, rows):
        return (0.5 * nt(s.weights_t[layer, pl.ds(0, WIDTH)], rows)).astype(BF16)

    def smalls(p, layer, m, progress):
        finish(gather_rims(p))
        for b in range(SMALLS):
            s.turned_small[b] = sources(layer, s.ext[p, pl.ds(b * BIG, 256)])
            spread(p, b + 1)
        for b in range(SMALLS):
            if b == 2:
                progress()
            hot = s.hot_small.at[m if kept > 1 else 0, b]
            for pair in range(STEPS // 2):
                score(p, layer, b + 1, pair, s.turned_small.at[b], hot)
            softmax(p, m, b + 1)

    def big(p, layer, m):
        s.turned_big[...] = sources(layer, s.table[p])
        spread(p, 0)
        hot = s.hot_big.at[m if kept > 1 else 0]
        for pair in range(STEPS // 2):
            score(p, layer, 0, pair, s.turned_big, hot)
            if pair + 1 < BLOCKS:
                pass_messages(p, m, pair + 1)
        softmax(p, m, 0)
        pass_messages(p, m, 0)

    def normalise(p, layer, m):
        gain, shift = s.vecs[layer, 2], s.vecs[layer, 3]
        for t in range(2):
            lanes = slice(t * 128, (t + 1) * 128)
            total = join_halves(s.message[m, 2 * t], s.message[m, 2 * t + 1])
            y = 2.0 * total + s.residue[m, :, lanes]
            centred = y - jnp.sum(y, axis=0, keepdims=True) * (1.0 / WIDTH)
            spread_of = jnp.sum(centred * centred, axis=0, keepdims=True) * (1.0 / WIDTH)
            inverse = lax.rsqrt(spread_of + EPSILON)
            normed = centred * inverse
            shifted = normed * gain + shift
            s.normed[p, :, lanes] = normed
            s.inverse[p, 0:1, lanes] = inverse
            act = jnp.where(shifted > 0, shifted, jnp.exp(jnp.minimum(shifted, 0.0)) - 1.0)
            s.act[:, lanes] = act.astype(BF16)

        @pl.when(layer == 0)
        def _():
            s.hidden_t[m + 2] = s.act[...]
            hidden = jnp.transpose(s.act[...])
            share(m + 2, hidden)
            start(gather_rims(m + 2))
            start(gather_far(m + 2))
            aim(m + 2, 1, m, hidden)

        @pl.when(layer == 1)
        def _():
            s.layer_output[m] = jnp.transpose(s.act[...])

    def forward(layer, carry):
        def body(m, inner):
            p = 2 * layer + m
            if kept == 1:
                mark_small(m)
                mark_big(m)

            def progress():
                finish(gather_far(p))
                start(gather_core(p))

            smalls(p, layer, m, progress)
            if shared_weights:

                @pl.when(jnp.logical_and(layer == 0, m == 0))
                def _():
                    finish(gather_pieces_xy(1))
                    start(gather_core(5))

            finish(gather_core(p))
            big(p, layer, m)

            @pl.when(jnp.logical_and(layer == 0, m == 0))
            def _():
                if shared_weights:
                    finish(gather_core(5))
                load_layer(1)

            normalise(p, layer, m)
            return inner

        lax.fori_loop(0, MICRO, body, 0)
        return carry

    def through_norm(p, layer, m):
        gain, shift = s.vecs[layer, 2], s.vecs[layer, 3]
        upper = upper_lanes()
        for t in range(2):
            lanes = slice(t * 128, (t + 1) * 128)
            normed = s.normed[p, :, lanes]
            shifted = normed * gain + shift
            grad = s.grad_act[m, :, lanes] * jnp.where(
                shifted > 0, 1.0, jnp.exp(jnp.minimum(shifted, 0.0))
            )
            s.grad_vecs[layer, 2] = s.grad_vecs[layer, 2] + grad * normed
            s.grad_vecs[layer, 3] = s.grad_vecs[layer, 3] + grad
            grad = grad * gain
            first = jnp.sum(grad, axis=0, keepdims=True) * (1.0 / WIDTH)
            second = jnp.sum(grad * normed, axis=0, keepdims=True) * (1.0 / WIDTH)
            grad = s.inverse[p, 0:1, lanes] * (grad - first - normed * second)
            s.grad_vecs[layer, 1] = s.grad_vecs[layer, 1] + grad
            s.grad_out_t[p, :, lanes] = grad.astype(BF16)
            grad = grad.astype(BF16).astype(F32)
            other = pltpu.roll(grad, 64, 1)
            s.grad_out[m, 2 * t] = jnp.where(upper, other, grad)
            s.grad_out[m, 2 * t + 1] = jnp.where(upper, grad, other)

    def share_grads(p, m, block, step):
        for h in range(HEADS):
            rows = slice(h * HEAD_WIDTH, (h + 1) * HEAD_WIDTH)
            grad = s.grad_out[m, block, rows, :]
            for half in range(2):
                product = rows_of[block][p, 2 * step + half, rows].astype(F32) * grad
                s.share_grad[block, step, h : h + 1, half * 128 : (half + 1) * 128] = (
                    jnp.sum(product, axis=0, keepdims=True)
                )

    def logit_grads(p, m, block):
        shares = [s.shares[p, block, i] for i in range(STEPS)]
        grads = [s.share_grad[block, i] for i in range(STEPS)]
        total = halves_sum(functools.reduce(jnp.add, [a * b for a, b in zip(shares, grads)]))
        for i in range(STEPS):
            s.share_grad[block, i] = 0.8 * shares[i] * (grads[i] - total)
            s.low_shares[block, i] = shares[i].astype(BF16).astype(F32)

    def make_terms(p, layer, m, block, pair):
        for h in range(HEADS):
            rows = slice(h * HEAD_WIDTH, (h + 1) * HEAD_WIDTH)
            wanted = s.doubled[block, rows, :]
            attn = s.vecs[layer, 0, rows, :]
            grad = s.grad_out[m, block, rows, :]
            target_sum = s.message[m, block, rows, :]
            attn_sum = s.grad_vecs[layer, 0, rows, :]
            for part in range(4):
                step, half = 2 * pair + part // 2, (part % 2) * 128
                z = rows_of[block][p, 4 * pair + part, rows].astype(F32) + wanted
                t = jnp.tanh(z)
                w = t + 1.5
                logit_grad = s.share_grad[block, step, h : h + 1, half : half + 128]
                attn_sum = attn_sum + logit_grad * (z * w)
                slope = logit_grad * (w + z * (1.0 - t * t))
                target_sum = target_sum + slope
                share = s.low_shares[block, step, h : h + 1, half : half + 128]
                terms[pair % 2][rows, part * 128 : (part + 1) * 128] = (
                    share * grad + attn * slope
                ).astype(BF16)
            s.message[m, block, rows, :] = target_sum
            s.grad_vecs[layer, 0, rows, :] = attn_sum

    def all_share_grads(p, m, block):
        for step in range(STEPS):
            share_grads(p, m, block, step)
        logit_grads(p, m, block)

    def big_back(p, layer, m):
        spread(p, 0)
        s.message[m] = jnp.zeros((BLOCKS, WIDTH, 128), F32)
        all_share_grads(p, m, 0)
        for pair in range(STEPS // 2):
            make_terms(p, layer, m, 0, pair)
            added = nt(s.hot_big[m if kept > 1 else 0, pair], terms[pair % 2][...])
            if pair == 0:
                s.part_sum[...] = added
            elif pair + 1 < STEPS // 2:
                s.part_sum[...] = s.part_sum[...] + added
            else:
                s.table[2 + m] = (s.part_sum[...] + added).astype(BF16)

    def smalls_back(p, layer, m, progress):
        for b in range(SMALLS):
            spread(p, b + 1)
        s.grad_ext[...] = jnp.zeros_like(s.grad_ext)
        all_share_grads(p, m, 1)
        for b in range(SMALLS):
            if b + 1 < SMALLS:
                all_share_grads(p, m, b + 2)
            if b == 0:
                progress()
            here = pl.ds(b * BIG, 256)
            for pair in range(STEPS // 2):
                make_terms(p, layer, m, b + 1, pair)
                hot = s.hot_small[m if kept > 1 else 0, b, pair]
                s.grad_ext[here] = s.grad_ext[here] + nt(hot, terms[pair % 2][...])
        s.send_rim[p, 0] = s.grad_ext[pl.ds(0, RIM)].astype(BF16)
        s.send_rim[p, 1] = s.grad_ext[pl.ds(RIM + SMALL, RIM)].astype(BF16)
        start(reduce_rims(p))
        s.grad_small[m] = s.grad_ext[pl.ds(RIM, SMALL)]
        attn = s.vecs[layer, 0]
        for t in range(2):
            lanes = slice(t * 128, (t + 1) * 128)
            total = join_halves(s.message[m, 2 * t], s.message[m, 2 * t + 1])
            s.grad_targets_t[p, :, lanes] = (attn * total).astype(BF16)

    def finalise_sources(p, m):
        unit = reduced_unit(p)
        finish(reduce_rims(p))
        low = s.grad_small[m, pl.ds(0, RIM)] + s.land_rim[p, 0].astype(F32)
        high = s.grad_small[m, pl.ds(RIM, RIM)] + s.land_rim[p, 1].astype(F32)
        rows = jnp.concatenate([unit, low, high], axis=0)
        s.grad_sources_t[p] = jnp.transpose(rows.astype(BF16))

    def finalise_hidden(p, layer, m):
        s.grad_act[m] = (
            nn(s.weights[layer, pl.ds(0, WIDTH)], s.grad_sources_t[p])
            + nn(s.weights[layer, pl.ds(WIDTH, WIDTH)], s.grad_targets_t[p])
            + nn(s.weights[layer, pl.ds(2 * WIDTH, WIDTH)], s.grad_out_t[p])
        )

    def finalise(p, layer, m):
        finalise_sources(p, m)
        finalise_hidden(p, layer, m)

    def weight_grads(layer):
        for k, grads in enumerate((s.grad_sources_t, s.grad_targets_t, s.grad_out_t)):
            total = nt(s.hidden_t[2 * layer], grads[2 * layer])
            if layer == 0 and k == 0:
                total = total + s.head_weights[...] + tn(s.ext[1], s.grad_ext[...].astype(BF16))
            else:
                total = total + nt(s.hidden_t[2 * layer + 1], grads[2 * layer + 1])
            if shared_weights:
                s.grad_weights[pl.ds(k * WIDTH, WIDTH)] = total
            else:
                s.weight_sums[layer, pl.ds(k * WIDTH, WIDTH)] = total
        vector_rows = jnp.zeros((8, WIDTH), F32)
        for k in range(4):
            chosen = jnp.where(
                lax.broadcasted_iota(jnp.int32, (8, 128), 0) == k, 2.0 if k == 0 else 1.0, 0.0
            ).astype(F32)
            vector_rows = vector_rows + nt(
                chosen, s.grad_vecs[layer, k], precision=lax.Precision.HIGHEST
            )
        if not shared_weights:
            s.vector_sums[layer] = vector_rows
            return
        for chunk, at in chunks():
            s.table[4 + layer, pl.ds(at, PIECE)] = jnp.concatenate(
                [s.grad_weights[pl.ds(chunk * CHUNK, CHUNK)], vector_rows], axis=0
            ).astype(BF16)
        start(reduce_core(4 + layer))

    def weights_on(layer):
        add_core(4 + layer)
        start(reduce_pieces(layer))

    def weights_done(layer):
        finish(reduce_pieces(layer))
        total = s.table[4 + layer, pl.ds(own_piece_row, PIECE)].astype(F32)
        for k in range(2 * len(far) + 1):
            total = total + s.land_piece[layer, k].astype(F32)
        s.weight_sums[layer : layer + 1, :] = jnp.concatenate(
            [total[i : i + 1] for i in range(CHUNK)], axis=1
        )
        own = jnp.where(own_row_of_eight(), total[CHUNK:], 0.0)
        own = jnp.sum(own, axis=0, keepdims=True)
        own = nt(
            jnp.broadcast_to(own, (8, WIDTH)), vector_place(), precision=lax.Precision.HIGHEST
        )
        s.vector_sums[layer : layer + 1, :] = own[:1]

    def backward(i, carry):
        layer = 1 - i
        first, second = 2 * layer, 2 * layer + 1

        def body(m, inner):
            if kept == 1:
                mark_big(m)
                mark_small(m)

            @pl.when(jnp.logical_and(i == 1, m == 0))
            def _():
                finalise(2, 1, 0)

            if shared_weights:

                @pl.when(jnp.logical_and(i == 1, m == 1))
                def _():
                    weights_on(1)

            through_norm(first + m, layer, m)
            big_back(first + m, layer, m)

            @pl.when(jnp.logical_and(i == 1, m == 1))
            def _():
                s.head_weights[...] = tn(s.table[1], s.table[3])

            start(reduce_core(first + m))

            @pl.when(jnp.logical_and(i == 1, m == 0))
            def _():
                finalise(3, 1, 1)
                weight_grads(1)

            def progress():
                reduce_on(first + m)

            smalls_back(first + m, layer, m, progress)
            return inner

        lax.fori_loop(0, MICRO, body, 0)
        return carry

    barrier = pltpu.get_barrier_semaphore()
    partners = [dict(blk=peer) for peer, _ in far]
    if shared_weights:
        partners = [dict(blk=peer, fsdp=f) for peer, f, _ in all_far()]
    partners += [dict(blk=d) for d in (sibling, before, after)]
    for partner in partners:
        pl.semaphore_signal(barrier, inc=1, device_id=partner, device_id_type=MESH)
    brought = ("features", "neighbours", "slot_mask", "out_cotangent")
    for k, name in enumerate(brought):
        start(bring(k, name))
    if shared_weights:
        for layer in range(LAYERS):
            own_piece(layer)
    pl.semaphore_wait(barrier, len(partners))

    if shared_weights:
        for layer in range(LAYERS):
            start(gather_pieces_z(layer))
    finish(bring(0, "features"))
    for m in range(MICRO):
        share(m, s.features[m])
        start(gather_rims(m))
    for k in (1, 2, 3):
        finish(bring(k, brought[k]))
    for m in range(MICRO):
        prepare(m)
    if not shared_weights:
        start(gather_far(0))
        start(gather_far(1))
    s.scores[...] = jnp.zeros_like(s.scores)
    s.share_grad[...] = jnp.zeros_like(s.share_grad)
    s.grad_vecs[...] = jnp.zeros_like(s.grad_vecs)
    if kept > 1:
        mark_small(0)
        mark_small(1)
    if shared_weights:
        finish(gather_pieces_z(0))
        start(gather_pieces_xy(0))
        finish(gather_pieces_z(1))
        start(gather_far(0))
    if kept > 1:
        mark_big(0)
        mark_big(1)
    if shared_weights:
        finish(gather_pieces_xy(0))
        start(gather_core(4))
        start(gather_pieces_xy(1))
        start(gather_far(1))
        finish(gather_core(4))
    load_layer(0)
    for m in range(MICRO):
        aim(m, 0, m, s.features[m])
    lax.fori_loop(0, LAYERS, forward, 0)
    start(hand_out(4, "layer_output"))
    lax.fori_loop(0, LAYERS, backward, 0)
    finalise_sources(0, 0)
    weight_grads(0)
    finalise_hidden(0, 0, 0)
    if shared_weights:
        weights_on(0)
    s.input_gradient[0] = jnp.transpose(s.grad_act[0])
    start(hand_out(5, "input_gradient", 0))
    finalise(1, 0, 1)
    s.input_gradient[1] = jnp.transpose(s.grad_act[1])
    start(hand_out(6, "input_gradient", 1))
    if shared_weights:
        weights_done(1)
        weights_done(0)
    finish(hand_out(4, "layer_output"))
    for m in range(MICRO):
        finish(hand_out(5 + m, "input_gradient", m))


def hand_over(*refs):
    count = (len(refs) - 1) // 3
    sources, places, rooms, sems = refs[:count], refs[count : 2 * count], refs[2 * count : -1], refs[-1]
    moves = []
    for source, place, room in zip(sources, places, rooms):
        parts = [pl.ds(m, 1) for m in range(MICRO)] if len(source.shape) == 3 else [pl.ds(0, 2)]
        for part in parts:
            k = len(moves)
            moves.append(
                (
                    pltpu.make_async_copy(source.at[part], room.at[part], sems.at[0, k]),
                    pltpu.make_async_copy(room.at[part], place.at[part], sems.at[1, k]),
                )
            )
    for inward, _ in moves:
        inward.start()
    for inward, outward in moves:
        inward.wait()
        outward.start()
    for _, outward in moves:
        outward.wait()


def per_device(
    depth, fsdp_count, features, neighbours, slot_mask, projections, vectors, out_cotangent
):
    layers, weight_chunk = projections.shape
    shared_weights = fsdp_count == 2 and weight_chunk == CHUNK * WIDTH and depth == 4
    inputs = dict(
        features_hbm=features[:, 0],
        neighbours_hbm=jnp.swapaxes(neighbours[:, 0], 1, 2),
        slot_mask_hbm=jnp.swapaxes(slot_mask[:, 0], 1, 2),
        out_cotangent_hbm=out_cotangent[:, 0],
    )
    if shared_weights:
        inputs["projections"] = projections
        inputs["vectors"] = vectors
        weight_shape, vector_shape = projections.shape, vectors.shape
    else:
        axes = ("blk", "fsdp")
        gathered = lax.all_gather(projections, axes, axis=1, tiled=True)
        inputs["weights"] = gathered.reshape(layers, 3 * WIDTH, WIDTH)
        gathered = lax.all_gather(vectors, axes, axis=1, tiled=True)
        inputs["all_vectors"] = jnp.pad(
            gathered.reshape(layers, 4, WIDTH), ((0, 0), (0, 4), (0, 0))
        )
        weight_shape, vector_shape = (layers, 3 * WIDTH, WIDTH), (layers, 8, WIDTH)
    outputs = dict(
        layer_output_hbm=jax.ShapeDtypeStruct((MICRO, NODES, WIDTH), BF16),
        input_gradient_hbm=jax.ShapeDtypeStruct((MICRO, NODES, WIDTH), F32),
        weight_sums=jax.ShapeDtypeStruct(weight_shape, F32),
        vector_sums=jax.ShapeDtypeStruct(vector_shape, F32),
    )
    scratch = scratch_plan(depth, shared_weights)
    in_vmem = pl.BlockSpec(memory_space=pltpu.VMEM)
    in_hbm = pl.BlockSpec(memory_space=pl.ANY)
    results = pl.pallas_call(
        functools.partial(
            step_kernel, depth, shared_weights, [*inputs, *outputs, *scratch]
        ),
        out_shape=list(outputs.values()),
        in_specs=[in_hbm if name.endswith("_hbm") else in_vmem for name in inputs],
        out_specs=[in_hbm if name.endswith("_hbm") else in_vmem for name in outputs],
        scratch_shapes=list(scratch.values()),
        compiler_params=pltpu.CompilerParams(
            collective_id=0, has_side_effects=True, vmem_limit_bytes=63 * 1024 * 1024
        ),
    )(*inputs.values())
    if shared_weights:
        results = pl.pallas_call(
            hand_over,
            out_shape=list(outputs.values()),
            in_specs=[in_hbm] * len(outputs),
            out_specs=[in_hbm] * len(outputs),
            scratch_shapes=[pltpu.VMEM(x.shape, x.dtype) for x in outputs.values()]
            + [pltpu.SemaphoreType.DMA((2, 2 * len(outputs)))],
        )(*results)
    layer_output, input_gradient, weight_sums, vector_sums = results
    if not shared_weights:
        axes = ("blk", "fsdp")
        weight_sums = lax.psum_scatter(
            weight_sums.reshape(layers, -1), axes, scatter_dimension=1, tiled=True
        )
        vector_sums = lax.psum_scatter(
            vector_sums[:, :4].reshape(layers, -1), axes, scatter_dimension=1, tiled=True
        )
    return layer_output[:, None], input_gradient[:, None], weight_sums, vector_sums


def solution(mesh):
    return jax.shard_map(
        functools.partial(per_device, mesh.shape["blk"] // 4, mesh.shape["fsdp"]),
        mesh=mesh,
        in_specs=(
            P(None, "fsdp", "blk", None),
            P(None, "fsdp", "blk", None),
            P(None, "fsdp", "blk", None),
            P(None, ("blk", "fsdp")),
            P(None, ("blk", "fsdp")),
            P(None, "fsdp", "blk", None),
        ),
        out_specs=(
            P(None, "fsdp", "blk", None),
            P(None, "fsdp", "blk", None),
            P(None, ("blk", "fsdp")),
            P(None, ("blk", "fsdp")),
        ),
        check_vma=False,
    )
```

```python
import functools
import types

import jax
import jax.numpy as jnp
from jax import lax
from jax.experimental import pallas as pl
from jax.experimental.pallas import tpu as pltpu
from jax.sharding import PartitionSpec as P

HEADS = 4
MICRO = 2
LAYERS = 2
SLOTS = 32
WIDTH = 256
HEAD_WIDTH = WIDTH // HEADS
NODES = 256
BIG = 64
SMALL = NODES - BIG
RIM = 96
EXT = SMALL + 2 * RIM
BLOCKS = NODES // BIG
SMALLS = BLOCKS - 1
PAIRS = BIG * SLOTS
STEPS = 8
LANES = PAIRS // STEPS
UNIT = BIG
CHUNK = 24
PIECE = UNIT // 2
EPSILON = 1e-05
F32 = jnp.float32
BF16 = jnp.bfloat16
MESH = pl.DeviceIdType.MESH


def nn(left, right):
    return lax.dot_general(
        left, right, (((1,), (0,)), ((), ())), preferred_element_type=F32
    )


def nt(left, right, precision=None):
    return lax.dot_general(
        left, right, (((1,), (1,)), ((), ())), preferred_element_type=F32, precision=precision
    )


def tn(left, right):
    return lax.dot_general(
        left, right, (((0,), (0,)), ((), ())), preferred_element_type=F32
    )


def upper_lanes():
    return lax.broadcasted_iota(jnp.int32, (WIDTH, 128), 1) >= 64


def join_halves(even, odd):
    upper = upper_lanes()
    return jnp.where(upper, odd, even) + pltpu.roll(jnp.where(upper, even, odd), 64, 1)


def scratch_plan(depth, shared_weights):
    big_total = 4 * depth * UNIT
    tables = 4 + (LAYERS if shared_weights else 0)
    copies = MICRO if depth <= 4 else 1
    peers = 2 * depth - 1
    vm = pltpu.VMEM
    plan = dict(
        features=vm((MICRO, NODES, WIDTH), BF16),
        neighbours=vm((MICRO, SLOTS, NODES), jnp.int32),
        slot_mask=vm((MICRO, SLOTS, NODES), jnp.int32),
        out_cotangent=vm((MICRO, NODES, WIDTH), BF16),
        layer_output=vm((MICRO, NODES, WIDTH), BF16),
        input_gradient=vm((MICRO, NODES, WIDTH), F32),
        own_sems=pltpu.SemaphoreType.DMA((7,)),
        hot_big=vm((copies, STEPS // 2, big_total, 2 * LANES), BF16),
        hot_small=vm((copies, SMALLS, STEPS // 2, 256, 2 * LANES), BF16),
        place=vm((MICRO, BLOCKS, STEPS, LANES), jnp.int32),
        used=vm((MICRO, BLOCKS, STEPS, LANES), F32),
        rows_0=vm((4, 2 * STEPS, WIDTH, 128), BF16),
        rows_1=vm((4, 2 * STEPS, WIDTH, 128), BF16),
        rows_2=vm((4, 2 * STEPS, WIDTH, 128), BF16),
        rows_3=vm((4, 2 * STEPS, WIDTH, 128), BF16),
        shares=vm((4, BLOCKS, STEPS, 8, LANES), F32),
        table=vm((tables, big_total, WIDTH), BF16),
        ext=vm((4, EXT, WIDTH), BF16),
        turned_big=vm((WIDTH, big_total), BF16),
        turned_small=vm((SMALLS, WIDTH, 256), BF16),
        hidden_t=vm((4, WIDTH, NODES), BF16),
        weights_t=vm((LAYERS, 3 * WIDTH, WIDTH), BF16),
        vecs=vm((LAYERS, 4, WIDTH, 128), F32),
        targets=vm((4, WIDTH, NODES), F32),
        residue=vm((MICRO, WIDTH, NODES), F32),
        doubled=vm((BLOCKS, WIDTH, 128), F32),
        scores=vm((BLOCKS, STEPS, 8, LANES), F32),
        low_shares=vm((BLOCKS, STEPS, 8, LANES), F32),
        share_grad=vm((BLOCKS, STEPS, 8, LANES), F32),
        message=vm((MICRO, BLOCKS, WIDTH, 128), F32),
        normed=vm((4, WIDTH, NODES), F32),
        inverse=vm((4, 8, NODES), F32),
        act=vm((WIDTH, NODES), BF16),
        grad_act=vm((MICRO, WIDTH, NODES), F32),
        grad_out=vm((MICRO, BLOCKS, WIDTH, 128), F32),
        grad_out_t=vm((4, WIDTH, NODES), BF16),
        grad_targets_t=vm((4, WIDTH, NODES), BF16),
        grad_sources_t=vm((4, WIDTH, NODES), BF16),
        terms_0=vm((WIDTH, 2 * LANES), BF16),
        terms_1=vm((WIDTH, 2 * LANES), BF16),
        part_sum=vm((big_total, WIDTH), F32),
        grad_ext=vm((EXT, WIDTH), F32),
        head_weights=vm((WIDTH, WIDTH), F32),
        grad_small=vm((MICRO, SMALL, WIDTH), F32),
        grad_vecs=vm((LAYERS, 4, WIDTH, 128), F32),
        land_core=vm((tables, big_total // 2, WIDTH), BF16),
        land=vm((4, peers, UNIT, WIDTH), BF16),
        land_rim=vm((4, 2, RIM, WIDTH), BF16),
        send_rim=vm((4, 2, RIM, WIDTH), BF16),
        gather_send=pltpu.SemaphoreType.DMA((tables, 18)),
        gather_recv=pltpu.SemaphoreType.DMA((tables, 18)),
        reduce_send=pltpu.SemaphoreType.DMA((tables, 18)),
        reduce_recv=pltpu.SemaphoreType.DMA((tables, 18)),
    )
    if shared_weights:
        plan.update(
            weights=vm((LAYERS, 3 * WIDTH, WIDTH), BF16),
            grad_weights=vm((3 * WIDTH, WIDTH), F32),
            land_piece=vm((LAYERS, 2 * peers + 1, PIECE, WIDTH), BF16),
        )
    return plan


def step_kernel(depth, shared_weights, names, *refs):
    s = types.SimpleNamespace(**dict(zip(names, refs, strict=True)))
    big_total = 4 * depth * UNIT
    kept = s.hot_big.shape[0]
    me = lax.axis_index("blk")
    core = lax.rem(me, 2)
    along_x = lax.rem(lax.div(me, 2), 2)
    along_z = lax.div(me, 4)
    own_f = lax.axis_index("fsdp")
    block_count = 4 * depth
    before = lax.rem(me + block_count - 1, block_count)
    after = lax.rem(me + 1, block_count)
    sibling = along_z * 4 + along_x * 2 + (1 - core)

    def unit_row(z, x, c):
        return pl.multiple_of(((c * 2 + x) * depth + z) * UNIT, UNIT)

    own_row = unit_row(along_z, along_x, core)
    rows_of = (s.rows_0, s.rows_1, s.rows_2, s.rows_3)
    terms = (s.terms_0, s.terms_1)
    far = []
    for dz in sorted(range(depth), reverse=True):
        for dx in (1, 0):
            if dz or dx:
                z, x = lax.rem(along_z + dz, depth), lax.rem(along_x + dx, 2)
                far.append((z * 4 + x * 2 + core, unit_row(z, x, core)))

    def remote(src, dst, sems, slot, **where):
        send, recv = sems
        return pltpu.make_async_remote_copy(
            src_ref=src,
            dst_ref=dst,
            send_sem=send.at[slot],
            recv_sem=recv.at[slot],
            device_id=where,
            device_id_type=MESH,
        )

    gather_sems = (s.gather_send, s.gather_recv)
    reduce_sems = (s.reduce_send, s.reduce_recv)
    core_slot, low_slot, high_slot = 15, 16, 17

    def half_rows(c):
        return pl.ds(unit_row(0, 0, c), 2 * depth * UNIT)

    def piece_row(z, x, c, f):
        return pl.multiple_of((((c * 2 + x) * 2 + f) * depth + z) * PIECE, PIECE)

    own_piece_row = piece_row(along_z, along_x, core, own_f)

    def gather_far(p):
        unit = s.table.at[p, pl.ds(own_row, UNIT)]
        return [
            remote(unit, unit, gather_sems, (p, k), blk=peer)
            for k, (peer, _) in enumerate(far)
        ]

    def all_far():
        found = []
        for dz in sorted(range(depth), reverse=True):
            for dx in (1, 0):
                for f in (1 - own_f, own_f):
                    if dz or dx or f is not own_f:
                        z, x = lax.rem(along_z + dz, depth), lax.rem(along_x + dx, 2)
                        found.append((z * 4 + x * 2 + core, f, piece_row(z, x, core, f)))
        return found

    def gather_pieces_z(layer):
        piece = s.table.at[4 + layer, pl.ds(own_piece_row, PIECE)]
        peers = [
            lax.rem(along_z + dz, depth) * 4 + along_x * 2 + core for dz in range(1, depth)
        ]
        return [
            remote(piece, piece, gather_sems, (4 + layer, k), blk=peer)
            for k, peer in enumerate(reversed(peers))
        ]

    def gather_pieces_xy(layer):
        column = piece_row(0, along_x, core, own_f)
        piece = s.table.at[4 + layer, pl.ds(column, depth * PIECE)]
        other = along_z * 4 + (1 - along_x) * 2 + core
        peers = [(other, 1 - own_f), (other, own_f), (me, 1 - own_f)]
        return [
            remote(piece, piece, gather_sems, (4 + layer, 8 + k), blk=peer, fsdp=f)
            for k, (peer, f) in enumerate(peers)
        ]

    def gather_core(q):
        half = s.table.at[q, half_rows(core)]
        return [remote(half, half, gather_sems, (q, core_slot), blk=sibling)]

    def gather_rims(p):
        low = remote(
            s.ext.at[p, pl.ds(RIM, RIM)],
            s.ext.at[p, pl.ds(RIM + SMALL, RIM)],
            gather_sems,
            (p, low_slot),
            blk=before,
        )
        high = remote(
            s.ext.at[p, pl.ds(SMALL, RIM)],
            s.ext.at[p, pl.ds(0, RIM)],
            gather_sems,
            (p, high_slot),
            blk=after,
        )
        return [low, high]

    def part_of(q):
        return q if isinstance(q, int) and q >= 4 else 2 + lax.rem(q, 2)

    def reduce_core(q):
        return [
            remote(
                s.table.at[part_of(q), half_rows(1 - core)],
                s.land_core.at[q],
                reduce_sems,
                (q, core_slot),
                blk=sibling,
            )
        ]

    def reduce_far(p):
        return [
            remote(
                s.table.at[part_of(p), pl.ds(row, UNIT)],
                s.land.at[p, k],
                reduce_sems,
                (p, k),
                blk=peer,
            )
            for k, (peer, row) in enumerate(far)
        ]

    def reduce_pieces(layer):
        return [
            remote(
                s.table.at[4 + layer, pl.ds(row, PIECE)],
                s.land_piece.at[layer, k],
                reduce_sems,
                (4 + layer, k),
                blk=peer,
                fsdp=f,
            )
            for k, (peer, f, row) in enumerate(all_far())
        ]

    def reduce_rims(p):
        low = remote(
            s.send_rim.at[p, 0], s.land_rim.at[p, 1], reduce_sems, (p, low_slot), blk=before
        )
        high = remote(
            s.send_rim.at[p, 1], s.land_rim.at[p, 0], reduce_sems, (p, high_slot), blk=after
        )
        return [low, high]

    def bring(k, name):
        return [
            pltpu.make_async_copy(getattr(s, name + "_hbm"), getattr(s, name), s.own_sems.at[k])
        ]

    def hand_out(k, name, m=None):
        kept_ref, out_ref = getattr(s, name), getattr(s, name + "_hbm")
        if m is not None:
            kept_ref, out_ref = kept_ref.at[m], out_ref.at[m]
        return [pltpu.make_async_copy(kept_ref, out_ref, s.own_sems.at[k])]

    def start(copies):
        for copy in copies:
            copy.start()

    def finish(copies):
        for copy in copies:
            copy.wait()

    def add_core(q):
        finish(reduce_core(q))
        first = unit_row(0, 0, core)
        at = part_of(q)

        def body(i, carry):
            here = pl.ds(pl.multiple_of(first + i * UNIT, UNIT), UNIT)
            there = pl.ds(pl.multiple_of(i * UNIT, UNIT), UNIT)
            s.table[at, here] = (
                s.table[at, here].astype(F32) + s.land_core[q, there].astype(F32)
            ).astype(BF16)
            return carry

        lax.fori_loop(0, 2 * depth, body, 0)

    def reduce_on(p):
        add_core(p)
        start(reduce_far(p))

    def reduced_unit(p):
        finish(reduce_far(p))
        total = s.table[part_of(p), pl.ds(own_row, UNIT)].astype(F32)
        for k in range(len(far)):
            total = total + s.land[p, k].astype(F32)
        return total

    def prepare(m):
        def compact(rows, block):
            part = rows[:, block * BIG : (block + 1) * BIG]
            tile = jnp.concatenate([part[:16], part[16:]], axis=1)
            return jnp.concatenate([tile[:8], tile[8:]], axis=1)

        picked = s.neighbours[m]
        usable = s.slot_mask[m]
        device = lax.shift_right_logical(picked, 8)
        offset = jnp.bitwise_and(picked, 255)
        z = lax.shift_right_logical(device, 2)
        x = jnp.bitwise_and(lax.shift_right_logical(device, 1), 1)
        c = jnp.bitwise_and(device, 1)
        big_place = ((c * 2 + x) * depth + z) * UNIT + offset
        small_place = (device - me) * SMALL + (offset - BIG)
        for block in range(BLOCKS):
            if block == 0:
                s.place[m, 0] = compact(big_place, 0)
            else:
                s.place[m, block] = compact(small_place + (RIM - (block - 1) * BIG), block)
            s.used[m, block] = compact(usable, block).astype(F32)
        s.hidden_t[m] = jnp.transpose(s.features[m])
        s.grad_act[m] = jnp.transpose(s.out_cotangent[m].astype(F32))

    def mark(row, least):
        tile = lax.broadcasted_iota(jnp.int32, (256, LANES), 0)
        return jnp.where(tile == row - least, 1.0, 0.0).astype(BF16)

    def lanes_of(step):
        return pl.ds(pl.multiple_of(step * LANES, LANES), LANES)

    def mark_big(m):
        slot = m if kept > 1 else 0

        def tile(w, carry):
            here = pl.ds(pl.multiple_of(w * 256, 256), 256)
            for step in range(STEPS):
                lanes = pl.ds(step % 2 * LANES, LANES)
                row = s.place[m, 0, pl.ds(step, 1), :]
                s.hot_big[slot, step // 2, here, lanes] = mark(row, w * 256)
            return carry

        lax.fori_loop(0, big_total // 256, tile, 0)

    def mark_small(m):
        slot = m if kept > 1 else 0

        def block_body(b, carry):
            for step in range(STEPS):
                lanes = pl.ds(step % 2 * LANES, LANES)
                row = s.place[m, b + 1, pl.ds(step, 1), :]
                s.hot_small[slot, b, step // 2, :, lanes] = mark(row, 0)
            return carry

        lax.fori_loop(0, SMALLS, block_body, 0)

    place = me * 2 + own_f
    vector_row, vector_lane = lax.div(place, 8), lax.rem(place, 8) * 32

    def vector_place():
        lane = lax.broadcasted_iota(jnp.int32, (32, WIDTH), 1)
        element = lax.broadcasted_iota(jnp.int32, (32, WIDTH), 0)
        return jnp.where(lane == element + vector_lane, 1.0, 0.0)

    def own_row_of_eight():
        return lax.broadcasted_iota(jnp.int32, (8, WIDTH), 0) == vector_row

    def own_piece(layer):
        flat = s.projections[...].astype(F32)[layer : layer + 1]
        rows = [flat[:, i * WIDTH : (i + 1) * WIDTH] for i in range(CHUNK)]
        own = s.vectors[...][layer : layer + 1].astype(F32)
        own = nn(jnp.broadcast_to(own, (8, 32)).astype(BF16), vector_place().astype(BF16))
        rows.append(jnp.where(own_row_of_eight(), own, 0.0))
        s.table[4 + layer, pl.ds(own_piece_row, PIECE)] = jnp.concatenate(
            rows, axis=0
        ).astype(BF16)

    def chunks():
        for c in range(2):
            for x in range(2):
                for z in range(depth):
                    for y in range(2):
                        yield (
                            ((z * 2 + x) * 2 + c) * 2 + y,
                            (((c * 2 + x) * 2 + y) * depth + z) * PIECE,
                        )

    def load_layer(layer):
        if shared_weights:
            pieces = {
                chunk: s.table[4 + layer, pl.ds(at, PIECE)].astype(F32)
                for chunk, at in chunks()
            }
            s.weights[layer] = jnp.concatenate(
                [pieces[i][:CHUNK] for i in range(len(pieces))], axis=0
            ).astype(BF16)
            rows = pieces[0][CHUNK:]
            for i in range(1, len(pieces)):
                rows = rows + pieces[i][CHUNK:]
        else:
            rows = s.all_vectors[layer].astype(F32)
        for k in range(3):
            rows_k = pl.ds(k * WIDTH, WIDTH)
            s.weights_t[layer, rows_k] = jnp.transpose(s.weights[layer, rows_k])
        which = lax.broadcasted_iota(jnp.int32, (8, 512), 0)
        lane = lax.shift_right_logical(lax.broadcasted_iota(jnp.int32, (8, 512), 1), 7)
        chosen = jnp.where(which == lane, 1.0, 0.0).astype(BF16)
        wide = tn(rows.astype(BF16), chosen)
        for k in range(4):
            s.vecs[layer, k] = wide[:, k * 128 : (k + 1) * 128]

    def share(p, hidden):
        s.table[p, pl.ds(own_row, UNIT)] = hidden[:BIG]
        s.ext[p, pl.ds(RIM, SMALL)] = hidden[BIG:]

    def aim(p, layer, m, hidden):
        s.targets[p] = 0.5 * nt(s.weights_t[layer, pl.ds(WIDTH, WIDTH)], hidden)
        bias = s.vecs[layer, 1]
        s.residue[m] = nt(s.weights_t[layer, pl.ds(2 * WIDTH, WIDTH)], hidden) + jnp.concatenate(
            [bias, bias], axis=1
        )

    def spread(p, block):
        wide = s.targets[p, :, pl.ds((block // 2) * 128, 128)]
        odd = block % 2 == 1
        tile = jnp.where(upper_lanes() == odd, wide, pltpu.roll(wide, 64, 1))
        s.doubled[block] = tile

    def score(p, layer, block, pair, turned, hot):
        got = nn(turned[...], hot[pair])
        low = got.astype(BF16)
        for part in range(4):
            rows_of[block][p, 4 * pair + part] = low[:, part * 128 : (part + 1) * 128]
        for h in range(HEADS):
            rows = slice(h * HEAD_WIDTH, (h + 1) * HEAD_WIDTH)
            wanted = s.doubled[block, rows, :]
            attn = s.vecs[layer, 0, rows, :]
            for part in range(4):
                z = got[rows, part * 128 : (part + 1) * 128] + wanted
                lifted = z * (jnp.tanh(z) + 1.5)
                half = (part % 2) * 128
                s.scores[block, 2 * pair + part // 2, h : h + 1, half : half + 128] = jnp.sum(
                    lifted * attn, axis=0, keepdims=True
                )

    def halves_max(wide):
        tile = jnp.maximum(wide[:, :128], wide[:, 128:])
        tile = jnp.maximum(tile, pltpu.roll(tile, 64, 1))
        return jnp.concatenate([tile, tile], axis=1)

    def halves_sum(wide):
        tile = wide[:, :128] + wide[:, 128:]
        tile = tile + pltpu.roll(tile, 64, 1)
        return jnp.concatenate([tile, tile], axis=1)

    def softmax(p, m, block):
        used = [s.used[m, block, pl.ds(i, 1), :] for i in range(STEPS)]
        logits = [
            jnp.where(used[i] > 0, 0.8 * s.scores[block, i], -1e30) for i in range(STEPS)
        ]
        largest = halves_max(functools.reduce(jnp.maximum, logits))
        raised = [jnp.exp(logits[i] - largest) * used[i] for i in range(STEPS)]
        scale = 1.0 / halves_sum(functools.reduce(jnp.add, raised))
        for i in range(STEPS):
            share = raised[i] * scale
            s.shares[p, block, i] = share
            s.low_shares[block, i] = share.astype(BF16).astype(F32)

    def pass_messages(p, m, block):
        for h in range(HEADS):
            rows = slice(h * HEAD_WIDTH, (h + 1) * HEAD_WIDTH)
            total = jnp.zeros((HEAD_WIDTH, 128), F32)
            for step in range(STEPS):
                for half in range(2):
                    share = s.low_shares[block, step, h : h + 1, half * 128 : (half + 1) * 128]
                    total = total + share * rows_of[block][p, 2 * step + half, rows].astype(F32)
            s.message[m, block, rows, :] = total

    def sources(layer, rows):
        return (0.5 * nt(s.weights_t[layer, pl.ds(0, WIDTH)], rows)).astype(BF16)

    def smalls(p, layer, m, progress):
        finish(gather_rims(p))
        for b in range(SMALLS):
            s.turned_small[b] = sources(layer, s.ext[p, pl.ds(b * BIG, 256)])
            spread(p, b + 1)
        for b in range(SMALLS):
            if b == 2:
                progress()
            hot = s.hot_small.at[m if kept > 1 else 0, b]
            for pair in range(STEPS // 2):
                score(p, layer, b + 1, pair, s.turned_small.at[b], hot)
            softmax(p, m, b + 1)

    def big(p, layer, m):
        s.turned_big[...] = sources(layer, s.table[p])
        spread(p, 0)
        hot = s.hot_big.at[m if kept > 1 else 0]
        for pair in range(STEPS // 2):
            score(p, layer, 0, pair, s.turned_big, hot)
            if pair + 1 < BLOCKS:
                pass_messages(p, m, pair + 1)
        softmax(p, m, 0)
        pass_messages(p, m, 0)

    def normalise(p, layer, m):
        gain, shift = s.vecs[layer, 2], s.vecs[layer, 3]
        for t in range(2):
            lanes = slice(t * 128, (t + 1) * 128)
            total = join_halves(s.message[m, 2 * t], s.message[m, 2 * t + 1])
            y = 2.0 * total + s.residue[m, :, lanes]
            centred = y - jnp.sum(y, axis=0, keepdims=True) * (1.0 / WIDTH)
            spread_of = jnp.sum(centred * centred, axis=0, keepdims=True) * (1.0 / WIDTH)
            inverse = lax.rsqrt(spread_of + EPSILON)
            normed = centred * inverse
            shifted = normed * gain + shift
            s.normed[p, :, lanes] = normed
            s.inverse[p, 0:1, lanes] = inverse
            act = jnp.where(shifted > 0, shifted, jnp.exp(jnp.minimum(shifted, 0.0)) - 1.0)
            s.act[:, lanes] = act.astype(BF16)

        @pl.when(layer == 0)
        def _():
            s.hidden_t[m + 2] = s.act[...]
            hidden = jnp.transpose(s.act[...])
            share(m + 2, hidden)
            start(gather_rims(m + 2))
            start(gather_far(m + 2))
            aim(m + 2, 1, m, hidden)

        @pl.when(layer == 1)
        def _():
            s.layer_output[m] = jnp.transpose(s.act[...])

    def forward(layer, carry):
        def body(m, inner):
            p = 2 * layer + m
            if kept == 1:
                mark_small(m)
                mark_big(m)

            def progress():
                finish(gather_far(p))
                start(gather_core(p))

            smalls(p, layer, m, progress)
            if shared_weights:

                @pl.when(jnp.logical_and(layer == 0, m == 0))
                def _():
                    finish(gather_pieces_xy(1))
                    start(gather_core(5))

            finish(gather_core(p))
            big(p, layer, m)

            @pl.when(jnp.logical_and(layer == 0, m == 0))
            def _():
                if shared_weights:
                    finish(gather_core(5))
                load_layer(1)

            normalise(p, layer, m)
            return inner

        lax.fori_loop(0, MICRO, body, 0)
        return carry

    def through_norm(p, layer, m):
        gain, shift = s.vecs[layer, 2], s.vecs[layer, 3]
        upper = upper_lanes()
        for t in range(2):
            lanes = slice(t * 128, (t + 1) * 128)
            normed = s.normed[p, :, lanes]
            shifted = normed * gain + shift
            grad = s.grad_act[m, :, lanes] * jnp.where(
                shifted > 0, 1.0, jnp.exp(jnp.minimum(shifted, 0.0))
            )
            s.grad_vecs[layer, 2] = s.grad_vecs[layer, 2] + grad * normed
            s.grad_vecs[layer, 3] = s.grad_vecs[layer, 3] + grad
            grad = grad * gain
            first = jnp.sum(grad, axis=0, keepdims=True) * (1.0 / WIDTH)
            second = jnp.sum(grad * normed, axis=0, keepdims=True) * (1.0 / WIDTH)
            grad = s.inverse[p, 0:1, lanes] * (grad - first - normed * second)
            s.grad_vecs[layer, 1] = s.grad_vecs[layer, 1] + grad
            s.grad_out_t[p, :, lanes] = grad.astype(BF16)
            grad = grad.astype(BF16).astype(F32)
            other = pltpu.roll(grad, 64, 1)
            s.grad_out[m, 2 * t] = jnp.where(upper, other, grad)
            s.grad_out[m, 2 * t + 1] = jnp.where(upper, grad, other)

    def share_grads(p, m, block, step):
        for h in range(HEADS):
            rows = slice(h * HEAD_WIDTH, (h + 1) * HEAD_WIDTH)
            grad = s.grad_out[m, block, rows, :]
            for half in range(2):
                product = rows_of[block][p, 2 * step + half, rows].astype(F32) * grad
                s.share_grad[block, step, h : h + 1, half * 128 : (half + 1) * 128] = (
                    jnp.sum(product, axis=0, keepdims=True)
                )

    def logit_grads(p, m, block):
        shares = [s.shares[p, block, i] for i in range(STEPS)]
        grads = [s.share_grad[block, i] for i in range(STEPS)]
        total = halves_sum(functools.reduce(jnp.add, [a * b for a, b in zip(shares, grads)]))
        for i in range(STEPS):
            s.share_grad[block, i] = 0.8 * shares[i] * (grads[i] - total)
            s.low_shares[block, i] = shares[i].astype(BF16).astype(F32)

    def make_terms(p, layer, m, block, pair):
        for h in range(HEADS):
            rows = slice(h * HEAD_WIDTH, (h + 1) * HEAD_WIDTH)
            wanted = s.doubled[block, rows, :]
            attn = s.vecs[layer, 0, rows, :]
            grad = s.grad_out[m, block, rows, :]
            target_sum = s.message[m, block, rows, :]
            attn_sum = s.grad_vecs[layer, 0, rows, :]
            for part in range(4):
                step, half = 2 * pair + part // 2, (part % 2) * 128
                z = rows_of[block][p, 4 * pair + part, rows].astype(F32) + wanted
                t = jnp.tanh(z)
                w = t + 1.5
                logit_grad = s.share_grad[block, step, h : h + 1, half : half + 128]
                attn_sum = attn_sum + logit_grad * (z * w)
                slope = logit_grad * (w + z * (1.0 - t * t))
                target_sum = target_sum + slope
                share = s.low_shares[block, step, h : h + 1, half : half + 128]
                terms[pair % 2][rows, part * 128 : (part + 1) * 128] = (
                    share * grad + attn * slope
                ).astype(BF16)
            s.message[m, block, rows, :] = target_sum
            s.grad_vecs[layer, 0, rows, :] = attn_sum

    def all_share_grads(p, m, block):
        for step in range(STEPS):
            share_grads(p, m, block, step)
        logit_grads(p, m, block)

    def big_back(p, layer, m):
        spread(p, 0)
        s.message[m] = jnp.zeros((BLOCKS, WIDTH, 128), F32)
        all_share_grads(p, m, 0)
        for pair in range(STEPS // 2):
            make_terms(p, layer, m, 0, pair)
            added = nt(s.hot_big[m if kept > 1 else 0, pair], terms[pair % 2][...])
            if pair == 0:
                s.part_sum[...] = added
            elif pair + 1 < STEPS // 2:
                s.part_sum[...] = s.part_sum[...] + added
            else:
                s.table[2 + m] = (s.part_sum[...] + added).astype(BF16)

    def smalls_back(p, layer, m, progress):
        for b in range(SMALLS):
            spread(p, b + 1)
        s.grad_ext[...] = jnp.zeros_like(s.grad_ext)
        all_share_grads(p, m, 1)
        for b in range(SMALLS):
            if b + 1 < SMALLS:
                all_share_grads(p, m, b + 2)
            if b == 0:
                progress()
            here = pl.ds(b * BIG, 256)
            for pair in range(STEPS // 2):
                make_terms(p, layer, m, b + 1, pair)
                hot = s.hot_small[m if kept > 1 else 0, b, pair]
                s.grad_ext[here] = s.grad_ext[here] + nt(hot, terms[pair % 2][...])
        s.send_rim[p, 0] = s.grad_ext[pl.ds(0, RIM)].astype(BF16)
        s.send_rim[p, 1] = s.grad_ext[pl.ds(RIM + SMALL, RIM)].astype(BF16)
        start(reduce_rims(p))
        s.grad_small[m] = s.grad_ext[pl.ds(RIM, SMALL)]
        attn = s.vecs[layer, 0]
        for t in range(2):
            lanes = slice(t * 128, (t + 1) * 128)
            total = join_halves(s.message[m, 2 * t], s.message[m, 2 * t + 1])
            s.grad_targets_t[p, :, lanes] = (attn * total).astype(BF16)

    def finalise_sources(p, m):
        unit = reduced_unit(p)
        finish(reduce_rims(p))
        low = s.grad_small[m, pl.ds(0, RIM)] + s.land_rim[p, 0].astype(F32)
        high = s.grad_small[m, pl.ds(RIM, RIM)] + s.land_rim[p, 1].astype(F32)
        rows = jnp.concatenate([unit, low, high], axis=0)
        s.grad_sources_t[p] = jnp.transpose(rows.astype(BF16))

    def finalise_hidden(p, layer, m):
        s.grad_act[m] = (
            nn(s.weights[layer, pl.ds(0, WIDTH)], s.grad_sources_t[p])
            + nn(s.weights[layer, pl.ds(WIDTH, WIDTH)], s.grad_targets_t[p])
            + nn(s.weights[layer, pl.ds(2 * WIDTH, WIDTH)], s.grad_out_t[p])
        )

    def finalise(p, layer, m):
        finalise_sources(p, m)
        finalise_hidden(p, layer, m)

    def weight_grads(layer):
        for k, grads in enumerate((s.grad_sources_t, s.grad_targets_t, s.grad_out_t)):
            total = nt(s.hidden_t[2 * layer], grads[2 * layer])
            if layer == 0 and k == 0:
                total = total + s.head_weights[...] + tn(s.ext[1], s.grad_ext[...].astype(BF16))
            else:
                total = total + nt(s.hidden_t[2 * layer + 1], grads[2 * layer + 1])
            if shared_weights:
                s.grad_weights[pl.ds(k * WIDTH, WIDTH)] = total
            else:
                s.weight_sums[layer, pl.ds(k * WIDTH, WIDTH)] = total
        vector_rows = jnp.zeros((8, WIDTH), F32)
        for k in range(4):
            chosen = jnp.where(
                lax.broadcasted_iota(jnp.int32, (8, 128), 0) == k, 2.0 if k == 0 else 1.0, 0.0
            ).astype(F32)
            vector_rows = vector_rows + nt(
                chosen, s.grad_vecs[layer, k], precision=lax.Precision.HIGHEST
            )
        if not shared_weights:
            s.vector_sums[layer] = vector_rows
            return
        for chunk, at in chunks():
            s.table[4 + layer, pl.ds(at, PIECE)] = jnp.concatenate(
                [s.grad_weights[pl.ds(chunk * CHUNK, CHUNK)], vector_rows], axis=0
            ).astype(BF16)
        start(reduce_core(4 + layer))

    def weights_on(layer):
        add_core(4 + layer)
        start(reduce_pieces(layer))

    def weights_done(layer):
        finish(reduce_pieces(layer))
        total = s.table[4 + layer, pl.ds(own_piece_row, PIECE)].astype(F32)
        for k in range(2 * len(far) + 1):
            total = total + s.land_piece[layer, k].astype(F32)
        s.weight_sums[layer : layer + 1, :] = jnp.concatenate(
            [total[i : i + 1] for i in range(CHUNK)], axis=1
        )
        own = jnp.where(own_row_of_eight(), total[CHUNK:], 0.0)
        own = jnp.sum(own, axis=0, keepdims=True)
        own = nt(
            jnp.broadcast_to(own, (8, WIDTH)), vector_place(), precision=lax.Precision.HIGHEST
        )
        s.vector_sums[layer : layer + 1, :] = own[:1]

    def backward(i, carry):
        layer = 1 - i
        first, second = 2 * layer, 2 * layer + 1

        def body(m, inner):
            if kept == 1:
                mark_big(m)
                mark_small(m)

            @pl.when(jnp.logical_and(i == 1, m == 0))
            def _():
                finalise(2, 1, 0)

            if shared_weights:

                @pl.when(jnp.logical_and(i == 1, m == 1))
                def _():
                    weights_on(1)

            through_norm(first + m, layer, m)
            big_back(first + m, layer, m)

            start(reduce_core(first + m))

            @pl.when(jnp.logical_and(i == 1, m == 1))
            def _():
                s.head_weights[...] = tn(s.table[1], s.table[3])

            @pl.when(jnp.logical_and(i == 1, m == 0))
            def _():
                finalise(3, 1, 1)
                weight_grads(1)

            def progress():
                reduce_on(first + m)

            smalls_back(first + m, layer, m, progress)
            return inner

        lax.fori_loop(0, MICRO, body, 0)
        return carry

    barrier = pltpu.get_barrier_semaphore()
    partners = [dict(blk=peer) for peer, _ in far]
    if shared_weights:
        partners = [dict(blk=peer, fsdp=f) for peer, f, _ in all_far()]
    partners += [dict(blk=d) for d in (sibling, before, after)]
    for partner in partners:
        pl.semaphore_signal(barrier, inc=1, device_id=partner, device_id_type=MESH)
    brought = ("features", "neighbours", "slot_mask", "out_cotangent")
    for k, name in enumerate(brought):
        start(bring(k, name))
    if shared_weights:
        for layer in range(LAYERS):
            own_piece(layer)
    pl.semaphore_wait(barrier, len(partners))

    if shared_weights:
        start(gather_pieces_z(0))
    finish(bring(0, "features"))
    for m in range(MICRO):
        share(m, s.features[m])
        start(gather_rims(m))
    for k in (1, 2, 3):
        finish(bring(k, brought[k]))
    for m in range(MICRO):
        prepare(m)
    if not shared_weights:
        start(gather_far(0))
        start(gather_far(1))
    s.scores[...] = jnp.zeros_like(s.scores)
    s.share_grad[...] = jnp.zeros_like(s.share_grad)
    s.grad_vecs[...] = jnp.zeros_like(s.grad_vecs)
    if kept > 1:
        mark_small(0)
        mark_small(1)
    if shared_weights:
        finish(gather_pieces_z(0))
        start(gather_pieces_xy(0))
        start(gather_pieces_z(1))
        start(gather_far(0))
    if kept > 1:
        mark_big(0)
        mark_big(1)
    if shared_weights:
        finish(gather_pieces_xy(0))
        finish(gather_pieces_z(1))
        start(gather_core(4))
        start(gather_pieces_xy(1))
        start(gather_far(1))
        finish(gather_core(4))
    load_layer(0)
    for m in range(MICRO):
        aim(m, 0, m, s.features[m])
    lax.fori_loop(0, LAYERS, forward, 0)
    start(hand_out(4, "layer_output"))
    lax.fori_loop(0, LAYERS, backward, 0)
    finalise_sources(0, 0)
    weight_grads(0)
    finalise_hidden(0, 0, 0)
    if shared_weights:
        weights_on(0)
    s.input_gradient[0] = jnp.transpose(s.grad_act[0])
    start(hand_out(5, "input_gradient", 0))
    finalise(1, 0, 1)
    s.input_gradient[1] = jnp.transpose(s.grad_act[1])
    start(hand_out(6, "input_gradient", 1))
    if shared_weights:
        weights_done(1)
        weights_done(0)
    finish(hand_out(4, "layer_output"))
    for m in range(MICRO):
        finish(hand_out(5 + m, "input_gradient", m))


def hand_over(*refs):
    count = (len(refs) - 1) // 3
    sources, places, rooms, sems = refs[:count], refs[count : 2 * count], refs[2 * count : -1], refs[-1]
    moves = []
    for source, place, room in zip(sources, places, rooms):
        parts = [pl.ds(m, 1) for m in range(MICRO)] if len(source.shape) == 3 else [pl.ds(0, 2)]
        for part in parts:
            k = len(moves)
            moves.append(
                (
                    pltpu.make_async_copy(source.at[part], room.at[part], sems.at[0, k]),
                    pltpu.make_async_copy(room.at[part], place.at[part], sems.at[1, k]),
                )
            )
    for inward, _ in moves:
        inward.start()
    for inward, outward in moves:
        inward.wait()
        outward.start()
    for _, outward in moves:
        outward.wait()


def per_device(
    depth, fsdp_count, features, neighbours, slot_mask, projections, vectors, out_cotangent
):
    layers, weight_chunk = projections.shape
    shared_weights = fsdp_count == 2 and weight_chunk == CHUNK * WIDTH and depth == 4
    inputs = dict(
        features_hbm=features[:, 0],
        neighbours_hbm=jnp.swapaxes(neighbours[:, 0], 1, 2),
        slot_mask_hbm=jnp.swapaxes(slot_mask[:, 0], 1, 2),
        out_cotangent_hbm=out_cotangent[:, 0],
    )
    if shared_weights:
        inputs["projections"] = projections
        inputs["vectors"] = vectors
        weight_shape, vector_shape = projections.shape, vectors.shape
    else:
        axes = ("blk", "fsdp")
        gathered = lax.all_gather(projections, axes, axis=1, tiled=True)
        inputs["weights"] = gathered.reshape(layers, 3 * WIDTH, WIDTH)
        gathered = lax.all_gather(vectors, axes, axis=1, tiled=True)
        inputs["all_vectors"] = jnp.pad(
            gathered.reshape(layers, 4, WIDTH), ((0, 0), (0, 4), (0, 0))
        )
        weight_shape, vector_shape = (layers, 3 * WIDTH, WIDTH), (layers, 8, WIDTH)
    outputs = dict(
        layer_output_hbm=jax.ShapeDtypeStruct((MICRO, NODES, WIDTH), BF16),
        input_gradient_hbm=jax.ShapeDtypeStruct((MICRO, NODES, WIDTH), F32),
        weight_sums=jax.ShapeDtypeStruct(weight_shape, F32),
        vector_sums=jax.ShapeDtypeStruct(vector_shape, F32),
    )
    scratch = scratch_plan(depth, shared_weights)
    in_vmem = pl.BlockSpec(memory_space=pltpu.VMEM)
    in_hbm = pl.BlockSpec(memory_space=pl.ANY)
    results = pl.pallas_call(
        functools.partial(
            step_kernel, depth, shared_weights, [*inputs, *outputs, *scratch]
        ),
        out_shape=list(outputs.values()),
        in_specs=[in_hbm if name.endswith("_hbm") else in_vmem for name in inputs],
        out_specs=[in_hbm if name.endswith("_hbm") else in_vmem for name in outputs],
        scratch_shapes=list(scratch.values()),
        compiler_params=pltpu.CompilerParams(
            collective_id=0, has_side_effects=True, vmem_limit_bytes=63 * 1024 * 1024
        ),
    )(*inputs.values())
    if shared_weights:
        results = pl.pallas_call(
            hand_over,
            out_shape=list(outputs.values()),
            in_specs=[in_hbm] * len(outputs),
            out_specs=[in_hbm] * len(outputs),
            scratch_shapes=[pltpu.VMEM(x.shape, x.dtype) for x in outputs.values()]
            + [pltpu.SemaphoreType.DMA((2, 2 * len(outputs)))],
        )(*results)
    layer_output, input_gradient, weight_sums, vector_sums = results
    if not shared_weights:
        axes = ("blk", "fsdp")
        weight_sums = lax.psum_scatter(
            weight_sums.reshape(layers, -1), axes, scatter_dimension=1, tiled=True
        )
        vector_sums = lax.psum_scatter(
            vector_sums[:, :4].reshape(layers, -1), axes, scatter_dimension=1, tiled=True
        )
    return layer_output[:, None], input_gradient[:, None], weight_sums, vector_sums


def solution(mesh):
    return jax.shard_map(
        functools.partial(per_device, mesh.shape["blk"] // 4, mesh.shape["fsdp"]),
        mesh=mesh,
        in_specs=(
            P(None, "fsdp", "blk", None),
            P(None, "fsdp", "blk", None),
            P(None, "fsdp", "blk", None),
            P(None, ("blk", "fsdp")),
            P(None, ("blk", "fsdp")),
            P(None, "fsdp", "blk", None),
        ),
        out_specs=(
            P(None, "fsdp", "blk", None),
            P(None, "fsdp", "blk", None),
            P(None, ("blk", "fsdp")),
            P(None, ("blk", "fsdp")),
        ),
        check_vma=False,
    )
```
